32 devices in a mesh: design: 2 (over x), slab: 16 (over z, y, core).
Axes of the slice: x: 2, y: 2, z: 4, core: 2. Of those that a mesh axis runs over, the one named last changes fastest.
Arguments:
- e_start: float32 [3, 512, 64, 128], P(None, ('design', 'slab')), parts along dimension 1, may hold values from -6 to 6
- h_start: float32 [3, 512, 64, 128], P(None, ('design', 'slab')), parts along dimension 1, may hold values from -6 to 6
- material: int32 [512, 64, 128], P(('design', 'slab')), parts along dimension 0, may hold values from 0 to 3
- mat_permit: float32 [4], replicated, may hold values from 1 to 4
- mat_loss: float32 [4], replicated, may hold values from 0 to 0.2
- monitor_z: int32 [4], replicated, may hold values from 0 to 255, as said below
- monitor_span: int32 [4, 2], replicated, may hold values from 0 to 64, as said below
- freq_bins: int32 [128], P('slab'), may hold values from 1 to 255
Outputs:
- e_final: float32 [3, 512, 64, 128], P(None, ('design', 'slab')), parts along dimension 1
- h_final: float32 [3, 512, 64, 128], P(None, ('design', 'slab')), parts along dimension 1
- spectrum: float32 [256, 2, 4, 2, 64, 128], P(('design', 'slab')), parts along dimension 0
The draws below stay inside these ranges and needn't reach their ends.
There are 2 independent parts, one for each index of `design`. The reference program is written for one: setup_inputs(seed, part) draws one part's arguments, and reference() takes and returns one part's arrays. A program takes and returns all parts, laid end to end along the dimension named above; an argument that names none is the same for every part. Nothing has to cross between parts.
Inputs may be any that keep to these rules, and one draw needn't show every extreme that they name: `monitor_z`: the 4 monitor planes have distinct z indices. `monitor_span`: each monitor's first row is at most a quarter of 64, and it records between half and three quarters of the rows.
All inputs are finite; a program needn't handle non-finite values.
Results may differ from the reference program's by a relative error of at most 0.000075.
Values sent between devices are 32-bit elements; how exact they have to be, the bound alone decides.
No kernel may reach another device: no remote copies, remote signals or barrier semaphores. Data moves between devices by JAX's collectives and lax.ppermute only.
A program may use at most 128 MiB of HBM per device.

```python
import math
import jax
import jax.numpy as jnp
from jax import lax

NX = 128
NY = 64
STEPS = 8
MON = 4
NMAT = 4
PERIOD = 512
FREQ = 128
NZ = 256


def draw_monitor_z(key, part):
    key = jax.random.fold_in(key, 11)
    inner_key, order_key = jax.random.split(key)
    inner = jax.random.permutation(inner_key, NZ - 2)[:MON - 2].astype(jnp.int32) + 1
    ends = jnp.array([0, NZ - 1], jnp.int32)
    levels = jnp.concatenate([ends, inner])
    return levels[jax.random.permutation(order_key, MON)].astype(jnp.int32)


def draw_monitor_span(key, part):
    key = jax.random.fold_in(key, 12)
    first_key, second_key, order_key = jax.random.split(key, 3)
    lowest = jax.random.randint(first_key, (MON,), 0, NY // 4 + 1)
    extent = jax.random.randint(second_key, (MON,), NY // 2, 3 * NY // 4 + 1)
    lowest = lowest.at[0].set(NY // 4).at[1].set(0)
    extent = extent.at[0].set(NY - NY // 4)
    spans = jnp.stack([lowest, lowest + extent], 1).astype(jnp.int32)
    return spans[jax.random.permutation(order_key, MON)].astype(jnp.int32)


def set_ends(values, own_key, least, largest):
    spot = [jax.random.randint(jax.random.fold_in(own_key, axis), (), 0, length) for axis, length in enumerate(values.shape)]
    widest = values.shape.index(max(values.shape))
    beside = spot[:widest] + [(spot[widest] + 1) % values.shape[widest]] + spot[widest + 1:]
    return values.at[tuple(spot)].set(least).at[tuple(beside)].set(largest)


def block_levels(key, dims, cuts, low, top_value):
    def one(dim, parts):
        steps = jax.random.uniform(jax.random.fold_in(jax.random.fold_in(key, 6), dim), (parts,), jnp.float32, low / len(cuts), top_value / len(cuts))
        return jnp.repeat(jnp.exp(steps), dims[dim] // parts).reshape((-1,) + (1,) * (len(dims) - dim - 1))

    loudness = one(*cuts[0])
    for cut in cuts[1:]:
        loudness = loudness * one(*cut)
    return loudness


def scatter_about(key, dims, deviation, most, pieces=(), kind=jnp.bfloat16):
    gain = block_levels(key, dims, pieces, -0.22, 0.18) if pieces else 1.0
    values = jax.random.normal(key, dims, jnp.float32) * deviation * gain
    return jnp.minimum(jnp.maximum(values, -most), most).astype(kind)


def setup_inputs(seed: int = 0, part: int = 0) -> dict:
    keys = jax.random.split(jax.random.key(seed), 9)
    part_keys = jax.random.split(jax.random.fold_in(keys[8], part), 9)
    return {
        "e_start": scatter_about(part_keys[0], (3, NZ, NY, NX), 1.0, 6.0, ((1, 16),), jnp.float32),
        "h_start": scatter_about(part_keys[1], (3, NZ, NY, NX), 1.0, 6.0, ((1, 16),), jnp.float32),
        "material": set_ends(jax.random.randint(part_keys[2], (NZ, NY, NX), 0, NMAT), jax.random.fold_in(part_keys[2], 1), 0, NMAT - 1).astype(jnp.int32),
        "mat_permit": jnp.clip(jax.random.uniform(keys[3], (NMAT,), jnp.float32, 1.0, 4.0), 1.0, 4.0),
        "mat_loss": jnp.clip(jax.random.uniform(keys[4], (NMAT,), jnp.float32, 0.0, 0.2), 0.0, 0.2),
        "monitor_z": draw_monitor_z(jax.random.fold_in(keys[8], 71), part),
        "monitor_span": draw_monitor_span(jax.random.fold_in(keys[8], 71), part),
        "freq_bins": set_ends(jax.random.randint(keys[7], (FREQ,), 1, PERIOD // 2), jax.random.fold_in(keys[7], 1), 1, (PERIOD // 2) - 1).astype(jnp.int32),
    }


courant = 0.5


def forward_diff(values, along):
    upper = lax.slice_in_dim(values, 1, values.shape[along], axis=along)
    zero_plane = jnp.zeros_like(lax.slice_in_dim(values, 0, 1, axis=along))
    return jnp.concatenate([upper, zero_plane], along) - values


def backward_diff(values, along):
    lower = lax.slice_in_dim(values, 0, values.shape[along] - 1, axis=along)
    zero_plane = jnp.zeros_like(lax.slice_in_dim(values, 0, 1, axis=along))
    return values - jnp.concatenate([zero_plane, lower], along)


def curl_with(fields, differ):
    return jnp.stack([differ(fields[2], 1) - differ(fields[1], 0), differ(fields[0], 0) - differ(fields[2], 2), differ(fields[1], 2) - differ(fields[0], 1)])


def look_up(table, material):
    total = jnp.zeros(material.shape, jnp.float32)
    for which in range(NMAT):
        total = total + jnp.where(material == which, table[which], jnp.float32(0.0))
    return total


def reference(e_start, h_start, material, mat_permit, mat_loss, monitor_z, monitor_span, freq_bins):
    permit = look_up(mat_permit, material)
    loss = look_up(mat_loss, material)
    keep_coef = (1.0 - loss) / (1.0 + loss)
    drive_coef = courant / (permit * (1.0 + loss))
    rows_index = jnp.arange(NY, dtype=jnp.int32)
    row_mask = ((rows_index[None, :] >= monitor_span[:, 0:1]) & (rows_index[None, :] < monitor_span[:, 1:2])).astype(jnp.float32)
    e_field = e_start
    h_field = h_start
    samples = []
    for moment in range(STEPS):
        h_field = h_field - courant * curl_with(e_field, forward_diff)
        e_field = keep_coef * e_field + drive_coef * curl_with(h_field, backward_diff)
        planes = jnp.take(e_field[0:2], monitor_z, axis=1).transpose(1, 0, 2, 3)
        samples.append(planes * row_mask[:, None, :, None])
    stacked = jnp.stack(samples).reshape(STEPS, -1)
    moments = jnp.arange(1, STEPS + 1, dtype=jnp.int32)
    phase_turns = (freq_bins[:, None] * moments[None, :]) % PERIOD
    angles = phase_turns.astype(jnp.float32) * jnp.float32(2.0 * math.pi / PERIOD)
    phase_table = jnp.stack([jnp.cos(angles), -jnp.sin(angles)], 1)
    spectrum = jnp.einsum("fks,sq->fkq", phase_table, stacked, precision=lax.Precision.HIGHEST)
    spectrum = spectrum.reshape(FREQ, 2, MON, 2, NY, NX)
    return e_field, h_field, spectrum
```

```python
import functools
import math

import jax
import jax.numpy as jnp
from jax import lax
from jax.experimental import pallas as pl
from jax.experimental.pallas import tpu as pltpu
from jax.sharding import PartitionSpec as P

STEPS = 8
PERIOD = 512
ROUNDS = (4, 3, 1)
GHOST = max(ROUNDS)
COURANT = 0.5
VMEM = pl.BlockSpec(memory_space=pltpu.VMEM)
SMEM = pl.BlockSpec(memory_space=pltpu.SMEM)
ANY = pl.BlockSpec(memory_space=pl.ANY)
LIMIT = 48 * 1024 * 1024


def params():
    return pltpu.CompilerParams(vmem_limit_bytes=LIMIT)


def down_pieces(d, mats):
    pieces = [("e", 0, 2, 0, d)]
    if d > 1:
        pieces += [("e", 2, 1, 0, d - 1), ("h", 0, 3, 0, d - 1)]
    if mats:
        pieces += [("m", 0, 1, 0, mats)]
    return pieces


def up_pieces(d, mats, depth, first):
    pieces = [("e", 0, 3, depth - d, d)]
    if first:
        pieces += [("h", 0, 2, depth - d, d)]
        if d > 1:
            pieces += [("h", 2, 1, depth - d + 1, d - 1)]
    else:
        if d > 1:
            pieces += [("h", 0, 2, depth - d, d - 1)]
        if d > 2:
            pieces += [("h", 2, 1, depth - d + 1, d - 2)]
    if mats:
        pieces += [("m", 0, 1, depth - mats, mats)]
    return pieces


def size_of(pieces):
    return sum(p[2] * p[4] for p in pieces)


def message_size(d, mats, depth, first):
    return max(size_of(down_pieces(d, mats)), size_of(up_pieces(d, mats, depth, first)))


def spots(pieces):
    at = 0
    for name, comp, comps, plane, planes in pieces:
        for c in range(comp, comp + comps):
            yield name, c, plane, planes, at
            at += planes


def first_pack_kernel(d, mats, depth, info, e_ref, h_ref, m_ref, far_ref, near_ref, m_buf, sem):
    even = info[0] == 0

    def pack(down_ref, up_ref):
        copies = []
        for k, (pieces, out) in enumerate(
            ((down_pieces(d, mats), down_ref), (up_pieces(d, mats, depth, True), up_ref))
        ):
            for name, c, plane, planes, at in spots(pieces):
                target = out.at[pl.ds(at, planes)]
                if name == "m":
                    source, target = m_ref.at[pl.ds(plane, planes)], m_buf.at[k]
                else:
                    source = (e_ref if name == "e" else h_ref).at[c, pl.ds(plane, planes)]
                copy = pltpu.make_async_copy(source, target, sem.at[len(copies)])
                copy.start()
                copies.append(copy)
        for copy in copies:
            copy.wait()
        if mats:
            for k, (pieces, out) in enumerate(
                ((down_pieces(d, mats), down_ref), (up_pieces(d, mats, depth, True), up_ref))
            ):
                at = size_of(pieces) - mats
                out[pl.ds(at, mats)] = m_buf[k].astype(jnp.float32)

    @pl.when(even)
    def _():
        pack(far_ref, near_ref)

    @pl.when(jnp.logical_not(even))
    def _():
        pack(near_ref, far_ref)


def round_kernel(
    d, nxt, first, depth, monitors, rows, info, tables, *refs
):
    if first:
        e_in, h_in, m_in, far_in, near_in = refs[:5]
        refs = refs[5:]
    else:
        e_in, h_in, keep_in, drive_in, hb_in, far_in, near_in = refs[:7]
        refs = refs[7:]
    e_out, h_out = refs[:2]
    refs = refs[2:]
    mine_out, other_out = refs[:2]
    refs = refs[2:]
    if nxt:
        hb_out, far_out, near_out = refs[:3]
        refs = refs[3:]
    if first:
        keep_ref, drive_ref = refs[:2]
        refs = refs[2:]
    else:
        keep_ref, drive_ref = keep_in, drive_in
    e, h = refs
    height, width = e.shape[2], e.shape[3]
    mats = GHOST - 1
    even = info[0] == 0
    below, above = info[1], info[2]
    g = GHOST

    for c in range(3):
        e[c, pl.ds(g, depth)] = e_in[c]
        h[c, pl.ds(g, depth)] = h_in[c]

    def unpack(below_ref, above_ref):
        for shift, pieces, source in (
            (-depth, up_pieces(d, mats if first else 0, depth, first), below_ref),
            (depth, down_pieces(d, mats if first else 0), above_ref),
        ):
            for name, c, plane, planes, at in spots(pieces):
                value = source[pl.ds(at, planes)]
                where = g + plane + shift
                if name == "e":
                    e[c, pl.ds(where, planes)] = value
                elif name == "h":
                    h[c, pl.ds(where, planes)] = value
                else:
                    keep_ref[pl.ds(where - 1, planes)] = value

    @pl.when(even)
    def _():
        unpack(far_in, near_in)

    @pl.when(jnp.logical_not(even))
    def _():
        unpack(near_in, far_in)

    if first:
        loss = [jnp.full((1, width), tables[1, k], jnp.float32) for k in range(tables.shape[1])]
        permit = [jnp.full((1, width), tables[0, k], jnp.float32) for k in range(tables.shape[1])]
        keeps = [(1.0 - x) / (1.0 + x) for x in loss]
        drives = [COURANT / (p * (1.0 + x)) for p, x in zip(permit, loss)]

        def look_up(values, which):
            total = jnp.broadcast_to(values[0], which.shape)
            for k in range(1, len(values)):
                total = jnp.where(which == k, values[k], total)
            return total

        def own(z, _):
            which = m_in[z]
            keep_ref[z + mats] = look_up(keeps, which)
            drive_ref[z + mats] = look_up(drives, which)
            return 0

        lax.fori_loop(0, depth, own, 0)

        def ghosts(at, alive):
            which = keep_ref[at].astype(jnp.int32)
            keep_ref[at] = look_up(keeps, which) * alive
            drive_ref[at] = look_up(drives, which) * alive

        for k in range(mats):
            ghosts(k, below.astype(jnp.float32))
            ghosts(mats + depth + k, above.astype(jnp.float32))
    else:
        h[:, g - 1] = hb_in[...]

    row = lax.broadcasted_iota(jnp.int32, (height, width), 0)
    lane = lax.broadcasted_iota(jnp.int32, (height, width), 1)
    row_last, row_first = row == height - 1, row == 0
    lane_last, lane_first = lane == width - 1, lane == 0

    def fore_y(v):
        return jnp.where(row_last, 0.0, pltpu.roll(v, height - 1, 0)) - v

    def fore_x(v):
        return jnp.where(lane_last, 0.0, pltpu.roll(v, width - 1, 1)) - v

    def back_y(v):
        return v - jnp.where(row_first, 0.0, pltpu.roll(v, 1, 0))

    def back_x(v):
        return v - jnp.where(lane_first, 0.0, pltpu.roll(v, 1, 1))

    ghost_factor = COURANT * below.astype(jnp.float32)

    def step_h(at):
        factor = jnp.where(at < g, ghost_factor, COURANT)
        ex, ey, ez = e[0, at], e[1, at], e[2, at]
        hx = h[0, at] - factor * (fore_y(ez) - (e[1, at + 1] - ey))
        hy = h[1, at] - factor * ((e[0, at + 1] - ex) - fore_x(ez))
        hz = h[2, at] - factor * (fore_x(ey) - fore_y(ex))
        h[0, at] = hx
        h[1, at] = hy
        h[2, at] = hz
        return hx, hy, hz

    def step_both(at, _):
        hx, hy, hz = step_h(at)
        keep, drive = keep_ref[at - 1], drive_ref[at - 1]
        e[0, at] = keep * e[0, at] + drive * (back_y(hz) - (hy - h[1, at - 1]))
        e[1, at] = keep * e[1, at] + drive * ((hx - h[0, at - 1]) - back_x(hz))
        e[2, at] = keep * e[2, at] + drive * (back_x(hy) - back_y(hx))
        return 0

    mine, other = info[0], 1 - info[0]
    kept_row = lax.broadcasted_iota(jnp.int32, (rows, width), 0)
    for s in range(1, d + 1):
        low = g - (d - s)
        high = g + depth + (d - s)
        step_h(low - 1)
        lax.fori_loop(low, high, step_both, 0)
        for m in range(monitors):
            offset, start, extent = info[3 + m], info[3 + monitors + m], info[3 + 2 * monitors + m]
            held = jnp.logical_and(offset >= 0, offset < depth)
            spot = g + jnp.clip(offset, 0, depth - 1)
            taken = jnp.where(held, extent, 0)
            for out, c in ((mine_out, mine), (other_out, other)):
                plane = pltpu.roll(e[c, spot], height - start, 0)[:rows]
                out[s - 1, m] = jnp.where(kept_row < taken, plane, 0.0)

    for c in range(3):
        e_out[c] = e[c, pl.ds(g, depth)]
        h_out[c] = h[c, pl.ds(g, depth)]
    if nxt:
        hb_out[...] = h[:, g - 1]

        def pack(down_ref, up_ref):
            for pieces, out in (
                (down_pieces(nxt, 0), down_ref),
                (up_pieces(nxt, 0, depth, False), up_ref),
            ):
                for name, c, plane, planes, at in spots(pieces):
                    source = e if name == "e" else h
                    out[pl.ds(at, planes)] = source[c, pl.ds(g + plane, planes)]

        @pl.when(even)
        def _():
            pack(far_out, near_out)

        @pl.when(jnp.logical_not(even))
        def _():
            pack(near_out, far_out)


def spectrum_kernel(
    chunks, freqs, monitors, height, info, table, *refs
):
    samples = refs[: 2 * len(chunks)]
    out = refs[-1]
    rows, width = samples[0].shape[2:]
    f = pl.program_id(0)
    steps = sum(chunks)
    pad = jnp.zeros((height - rows, width), jnp.float32)
    for m in range(monitors):
        start = info[3 + monitors + m]
        for side in range(2):
            c = info[0] if side == 0 else 1 - info[0]
            planes = [
                samples[2 * k + side][t, m] for k in range(len(chunks)) for t in range(chunks[k])
            ]
            for part in range(2):
                total = planes[0] * table[f, part * steps]
                for t in range(1, steps):
                    total = total + planes[t] * table[f, part * steps + t]
                placed = pltpu.roll(jnp.concatenate([total, pad], 0), start, 0)
                out[0, part, m, c] = placed


def per_device(
    slabs, e_start, h_start, material, mat_permit, mat_loss, monitor_z, monitor_span, freq_bins
):
    depth, height, width = e_start.shape[1:]
    monitors = monitor_z.shape[0]
    freqs = freq_bins.shape[0]
    rows = 3 * height // 4
    mats = GHOST - 1
    me = lax.axis_index("slab")
    info = jnp.concatenate(
        [
            jnp.stack([me % 2, (me > 0).astype(jnp.int32), (me < slabs - 1).astype(jnp.int32)]),
            monitor_z - me * depth,
            monitor_span[:, 0],
            monitor_span[:, 1] - monitor_span[:, 0],
        ]
    ).astype(jnp.int32)
    tables = jnp.stack([mat_permit, mat_loss])
    moments = jnp.arange(1, STEPS + 1, dtype=jnp.int32)
    phase_turns = freq_bins[:, None] * moments[None, :] % PERIOD
    angles = phase_turns.astype(jnp.float32) * jnp.float32(2.0 * math.pi / PERIOD)
    phase_table = jnp.concatenate([jnp.cos(angles), -jnp.sin(angles)], 1)

    far_pairs = []
    for i in range(1, slabs - 1, 2):
        far_pairs += [(i, i + 1), (i + 1, i)]
    near_pairs = [(i, i ^ 1) for i in range(slabs)]

    def exchange(far, near):
        return lax.ppermute(far, "slab", far_pairs), lax.ppermute(near, "slab", near_pairs)

    def f32(*shape):
        return jax.ShapeDtypeStruct(shape, jnp.float32)

    d = ROUNDS[0]
    size = message_size(d, mats, depth, True)
    copies = sum(1 for _ in spots(down_pieces(d, mats))) + sum(
        1 for _ in spots(up_pieces(d, mats, depth, True))
    )
    with jax.named_scope("first_pack"):
        far, near = pl.pallas_call(
            functools.partial(first_pack_kernel, d, mats, depth),
            out_shape=[f32(size, height, width)] * 2,
            in_specs=[SMEM, ANY, ANY, ANY],
            out_specs=[VMEM] * 2,
            scratch_shapes=[
                pltpu.VMEM((2, mats, height, width), jnp.int32),
                pltpu.SemaphoreType.DMA((copies,)),
            ],
            compiler_params=params(),
        )(info, e_start, h_start, material)

    e, h = e_start, h_start
    keep = drive = hb = None
    chunks = []
    for k, d in enumerate(ROUNDS):
        first = k == 0
        nxt = ROUNDS[k + 1] if k + 1 < len(ROUNDS) else 0
        far, near = exchange(far, near)
        if first:
            operands = (e, h, material, far, near)
        else:
            operands = (e, h, keep, drive, hb, far, near)
        outs = [f32(*e.shape), f32(*h.shape)] + [f32(d, monitors, rows, width)] * 2
        if nxt:
            size = message_size(nxt, 0, depth, False)
            outs += [f32(3, height, width)] + [f32(size, height, width)] * 2
        if first:
            outs += [f32(depth + 2 * mats, height, width)] * 2
        extended = (3, depth + 2 * GHOST, height, width)
        with jax.named_scope(f"round{k}"):
            results = pl.pallas_call(
                functools.partial(round_kernel, d, nxt, first, depth, monitors, rows),
                out_shape=outs,
                in_specs=[SMEM, SMEM] + [VMEM] * len(operands),
                out_specs=[VMEM] * len(outs),
                scratch_shapes=[pltpu.VMEM(extended, jnp.float32)] * 2,
                compiler_params=params(),
            )(info, tables, *operands)
        e, h, mine, other = results[:4]
        results = results[4:]
        if nxt:
            hb, far, near = results[:3]
            results = results[3:]
        if first:
            keep, drive = results
        total = mine + lax.ppermute(other, "slab", near_pairs)
        stride = 2
        while stride < slabs:
            total = total + lax.ppermute(
                total, "slab", [(i, i ^ stride) for i in range(slabs)]
            )
            stride *= 2
        partner = lax.ppermute(total, "slab", near_pairs)
        chunks += [total, partner]

    with jax.named_scope("spectrum"):
        block = (1, 2, monitors, 2, height, width)
        spectrum = pl.pallas_call(
            functools.partial(spectrum_kernel, ROUNDS, freqs, monitors, height),
            out_shape=f32(freqs, *block[1:]),
            grid=(freqs,),
            in_specs=[SMEM, SMEM] + [VMEM] * len(chunks),
            out_specs=pl.BlockSpec(block, lambda f: (f, 0, 0, 0, 0, 0)),
            compiler_params=params(),
        )(info, phase_table, *chunks)
    return e, h, spectrum


def solution(mesh):
    slabs = mesh.shape["slab"]
    in_specs = (
        P(None, ("design", "slab"), None, None),
        P(None, ("design", "slab"), None, None),
        P(("design", "slab"), None, None),
        P(),
        P(),
        P(),
        P(),
        P("slab"),
    )
    out_specs = (
        P(None, ("design", "slab"), None, None),
        P(None, ("design", "slab"), None, None),
        P(("design", "slab"), None, None, None, None, None),
    )
    return jax.shard_map(
        functools.partial(per_device, slabs),
        mesh=mesh,
        in_specs=in_specs,
        out_specs=out_specs,
        check_vma=False,
    )
```

```python
import functools
import math

import jax
import jax.numpy as jnp
from jax import lax
from jax.experimental import pallas as pl
from jax.experimental.pallas import tpu as pltpu
from jax.sharding import PartitionSpec as P

STEPS = 8
PERIOD = 512
ROUNDS = (4, 4)
SCATTER = (True, True)
GHOST = max(ROUNDS)
COURANT = 0.5
VMEM = pl.BlockSpec(memory_space=pltpu.VMEM)
SMEM = pl.BlockSpec(memory_space=pltpu.SMEM)
ANY = pl.BlockSpec(memory_space=pl.ANY)
HBM = pl.BlockSpec(memory_space=pltpu.HBM)
LIMIT = 24 * 1024 * 1024
PAD = 8


def params():
    return pltpu.CompilerParams(vmem_limit_bytes=LIMIT)


def cost(microseconds):
    return pl.CostEstimate(
        flops=0, bytes_accessed=int(microseconds * 3.0e6), transcendentals=0
    )


def down_pieces(d, mats):
    pieces = [("e", 0, 2, 0, d)]
    if d > 1:
        pieces += [("e", 2, 1, 0, d - 1), ("h", 0, 3, 0, d - 1)]
    if mats:
        pieces += [("m", 0, 1, 0, mats)]
    return pieces


def up_pieces(d, mats, depth, first):
    pieces = [("e", 0, 3, depth - d, d)]
    if first:
        pieces += [("h", 0, 2, depth - d, d)]
        if d > 1:
            pieces += [("h", 2, 1, depth - d + 1, d - 1)]
    else:
        if d > 1:
            pieces += [("h", 0, 2, depth - d, d - 1)]
        if d > 2:
            pieces += [("h", 2, 1, depth - d + 1, d - 2)]
    if mats:
        pieces += [("m", 0, 1, depth - mats, mats)]
    return pieces


def size_of(pieces):
    return sum(p[2] * p[4] for p in pieces)


def message_size(d, mats, depth, first):
    return max(size_of(down_pieces(d, mats)), size_of(up_pieces(d, mats, depth, first)))


def spots(pieces):
    at = 0
    for name, comp, comps, plane, planes in pieces:
        for c in range(comp, comp + comps):
            yield name, c, plane, planes, at
            at += planes


def start_all(pairs, sem):
    copies = [pltpu.make_async_copy(a, b, sem.at[k]) for k, (a, b) in enumerate(pairs)]
    for copy in copies:
        copy.start()
    return copies


def first_pack_kernel(d, mats, depth, e_ref, h_ref, m_ref, far_ref, near_ref, m_buf, sem):
    even = lax.rem(lax.axis_index("slab"), 2) == 0

    def pack(down_ref, up_ref):
        sides = (
            (down_pieces(d, mats), down_ref),
            (up_pieces(d, mats, depth, True), up_ref),
        )
        moves = []
        for k, (pieces, out) in enumerate(sides):
            for name, c, plane, planes, at in spots(pieces):
                if name == "m":
                    moves.append((m_ref.at[pl.ds(plane, planes)], m_buf.at[k]))
                else:
                    source = e_ref if name == "e" else h_ref
                    moves.append((source.at[c, pl.ds(plane, planes)], out.at[pl.ds(at, planes)]))
        for copy in start_all(moves, sem):
            copy.wait()
        if mats:
            for k, (pieces, out) in enumerate(sides):
                out[pl.ds(size_of(pieces) - mats, mats)] = m_buf[k].astype(jnp.float32)

    @pl.when(even)
    def _():
        pack(far_ref, near_ref)

    @pl.when(jnp.logical_not(even))
    def _():
        pack(near_ref, far_ref)


class Yee:
    def __init__(self, e, h, coefs, height, width, first_plane, below):
        self.e, self.h, self.coefs = e, h, coefs
        self.first_plane, self.width = first_plane, width
        self.own = pl.ds(PAD, height)
        self.next_row, self.last_row = pl.ds(PAD + 1, height), pl.ds(PAD - 1, height)
        lane = lax.broadcasted_iota(jnp.int32, (height, width), 1)
        self.lane_last, self.lane_first = lane == width - 1, lane == 0
        self.ghost_factor = None if below is None else COURANT * below.astype(jnp.float32)
        planes = e.shape[1]
        e[:, :, pl.ds(PAD + height, PAD)] = jnp.zeros((3, planes, PAD, width), jnp.float32)
        h[:, :, pl.ds(0, PAD)] = jnp.zeros((3, planes, PAD, width), jnp.float32)

    def fore_x(self, v):
        return jnp.where(self.lane_last, 0.0, pltpu.roll(v, self.width - 1, 1)) - v

    def back_x(self, v):
        return v - jnp.where(self.lane_first, 0.0, pltpu.roll(v, 1, 1))

    def step_h(self, z, ghost=False):
        e, h, own, up = self.e, self.h, self.own, self.next_row
        at = self.first_plane + z
        factor = self.ghost_factor if ghost else COURANT
        ex, ey, ez = e[0, at, own], e[1, at, own], e[2, at, own]
        h[0, at, own] = h[0, at, own] - factor * ((e[2, at, up] - ez) - (e[1, at + 1, own] - ey))
        h[1, at, own] = h[1, at, own] - factor * ((e[0, at + 1, own] - ex) - self.fore_x(ez))
        h[2, at, own] = h[2, at, own] - factor * (self.fore_x(ey) - (e[0, at, up] - ex))

    def step_e(self, z):
        e, h, own, down = self.e, self.h, self.own, self.last_row
        at = self.first_plane + z
        hx, hy, hz = h[0, at, own], h[1, at, own], h[2, at, own]
        keep, drive = self.coefs[0, at], self.coefs[1, at]
        e[0, at, own] = keep * e[0, at, own] + drive * (
            (hz - h[2, at, down]) - (hy - h[1, at - 1, own])
        )
        e[1, at, own] = keep * e[1, at, own] + drive * (
            (hx - h[0, at - 1, own]) - self.back_x(hz)
        )
        e[2, at, own] = keep * e[2, at, own] + drive * (self.back_x(hy) - (hx - h[0, at, down]))


def material_tables(tables, width):
    loss = [jnp.full((1, width), tables[1, k], jnp.float32) for k in range(tables.shape[1])]
    permit = [jnp.full((1, width), tables[0, k], jnp.float32) for k in range(tables.shape[1])]
    keeps = [(1.0 - x) / (1.0 + x) for x in loss]
    drives = [COURANT / (p * (1.0 + x)) for p, x in zip(permit, loss)]
    return keeps, drives


def look_up(values, which):
    total = jnp.broadcast_to(values[0], which.shape)
    for k in range(1, len(values)):
        total = jnp.where(which == k, values[k], total)
    return total


def monitor_info(info, m, monitors):
    return info[4 + m], info[4 + monitors + m], info[4 + 2 * monitors + m]


def take_sample(e, c, spot, start, extent, rows):
    height, width = e.shape[2] - 2 * PAD, e.shape[3]
    plane = pltpu.roll(e[c, spot, pl.ds(PAD, height)], height - start, 0)[:rows]
    return jnp.where(lax.broadcasted_iota(jnp.int32, (rows, width), 0) < extent, plane, 0.0)


def inner_kernel(d, first, depth, monitors, rows, info, *refs):
    if first:
        tables, e_in, h_in, m_in, e_out, h_out, coefs_out, mine_out, other_out = refs[:9]
        e, h, coefs, m_buf, sem = refs[9:]
    else:
        e_in, h_in, coefs_in, e_out, h_out, mine_out, other_out = refs[:7]
        e, h, coefs, sem = refs[7:]
    height, width = e_in.shape[2:]
    g = 1
    own, inside = pl.ds(g, depth), pl.ds(PAD, height)
    moves = [(e_in.at[c], e.at[c, own, inside]) for c in range(3)]
    moves += [(h_in.at[c], h.at[c, own, inside]) for c in range(3)]
    if first:
        moves.append((m_in, m_buf))
    else:
        moves += [(coefs_in.at[k], coefs.at[k, own]) for k in range(2)]
    copies = start_all(moves, sem)
    yee = Yee(e, h, coefs, height, width, g, None)
    if first:
        copies.pop().wait()
        keeps, drives = material_tables(tables, width)

        def fill(z, _):
            which = m_buf[z]
            coefs[0, g + z] = look_up(keeps, which)
            coefs[1, g + z] = look_up(drives, which)
            return 0

        lax.fori_loop(0, depth, fill, 0)
    for copy in copies:
        copy.wait()

    mine, other = info[0], 1 - info[0]
    group = 4
    for s in range(1, d + 1):
        low, high = s, depth - s
        yee.step_h(low - 1)

        def chunk(base, planes):
            for u in range(planes):
                yee.step_h(base + u)
            for u in range(planes):
                yee.step_e(base + u)

        whole = (high - low) // group

        def body(k, _):
            chunk(low + group * k, group)
            return 0

        lax.fori_loop(0, whole, body, 0)
        if low + group * whole < high:
            chunk(low + group * whole, high - low - group * whole)
        for m in range(monitors):
            offset, start, extent = monitor_info(info, m, monitors)
            held = jnp.logical_and(offset >= low, offset < high)
            taken = jnp.where(held, extent, 0)
            spot = g + jnp.clip(offset, 0, depth - 1)
            mine_out[m, s - 1] = take_sample(e, mine, spot, start, taken, rows)
            other_out[m, s - 1] = take_sample(e, other, spot, start, taken, rows)

    moves = [(e.at[c, own, inside], e_out.at[c]) for c in range(3)]
    moves += [(h.at[c, own, inside], h_out.at[c]) for c in range(3)]
    if first:
        moves += [(coefs.at[k, own], coefs_out.at[k]) for k in range(2)]
    for copy in start_all(moves, sem):
        copy.wait()


def edge_kernel(d, nxt, first, depth, monitors, rows, info, *refs):
    e_in, h_in, coefs_in, mine_in, other_in, far_in, near_in = refs[:7]
    refs = refs[7:]
    mats = GHOST - 1
    if first:
        tables, refs = refs[0], refs[1:]
    else:
        ghosts_in, below_in, refs = refs[0], refs[1], refs[2:]
    e_out, h_out, mine_out, other_out, refs = *refs[:4], refs[4:]
    if nxt:
        below_out, far_out, near_out, refs = *refs[:3], refs[3:]
        if first:
            ghosts_out, refs = refs[0], refs[1:]
    e, h, coefs, sem = refs
    height, width = e_in.shape[2:]
    g = GHOST
    inside = pl.ds(PAD, height)
    even = info[0] == 0
    below, above = info[1], info[2]

    moves = []
    for plane, planes in ((0, d), (depth - 1 - d, d + 1)):
        for c in range(3):
            part, place = pl.ds(plane, planes), pl.ds(g + plane, planes)
            moves.append((e_in.at[c, part], e.at[c, place, inside]))
            moves.append((h_in.at[c, part], h.at[c, place, inside]))
    for plane in (0, depth - d):
        for k in range(2):
            moves.append((coefs_in.at[k, pl.ds(plane, d)], coefs.at[k, pl.ds(g + plane, d)]))
    copies = start_all(moves, sem)
    yee = Yee(e, h, coefs, height, width, g, below)

    sides = (
        (-depth, up_pieces(d, mats if first else 0, depth, first)),
        (depth, down_pieces(d, mats if first else 0)),
    )

    def unpack(below_ref, above_ref):
        for (shift, pieces), source in zip(sides, (below_ref, above_ref)):
            for name, c, plane, planes, at in spots(pieces):
                where = pl.ds(g + plane + shift, planes)
                value = source[pl.ds(at, planes)]
                if name == "e":
                    e[c, where, inside] = value
                elif name == "h":
                    h[c, where, inside] = value
                else:
                    coefs[0, where] = value

    @pl.when(even)
    def _():
        unpack(far_in, near_in)

    @pl.when(jnp.logical_not(even))
    def _():
        unpack(near_in, far_in)

    ghost_planes = list(range(g - mats, g)) + list(range(g + depth, g + depth + mats))
    if first:
        keeps, drives = material_tables(tables, width)
        for at in ghost_planes:
            alive = (below if at < g else above).astype(jnp.float32)
            which = coefs[0, at].astype(jnp.int32)
            coefs[0, at] = look_up(keeps, which) * alive
            coefs[1, at] = look_up(drives, which) * alive
        if nxt:
            for k, at in enumerate(ghost_planes):
                ghosts_out[:, k] = coefs[:, at]
    else:
        for k, at in enumerate(ghost_planes):
            coefs[:, at] = ghosts_in[:, k]
        h[:, g - 1, inside] = below_in[...]
    for copy in copies:
        copy.wait()

    mine, other = info[0], 1 - info[0]
    for s in range(1, d + 1):
        lower = list(range(s - d, s))
        upper = list(range(depth - s, depth + d - s))
        for z in lower:
            yee.step_h(z - 1, z - 1 < 0)
        for z in upper:
            yee.step_h(z)
        for z in lower + upper:
            yee.step_e(z)
        for m in range(monitors):
            offset, start, extent = monitor_info(info, m, monitors)
            held = jnp.logical_or(
                jnp.logical_and(offset >= 0, offset < s),
                jnp.logical_and(offset >= depth - s, offset < depth),
            )
            spot = g + jnp.clip(offset, 0, depth - 1)
            for out, before, c in ((mine_out, mine_in, mine), (other_out, other_in, other)):
                fresh = take_sample(e, c, spot, start, extent, rows)
                out[m, s - 1] = jnp.where(held, fresh, before[m, s - 1])

    moves = []
    for plane in (0, depth - d):
        part, place = pl.ds(plane, d), pl.ds(g + plane, d)
        for c in range(3):
            moves.append((e.at[c, place, inside], e_out.at[c, part]))
            moves.append((h.at[c, place, inside], h_out.at[c, part]))
    copies = start_all(moves, sem)
    if nxt:
        below_out[...] = h[:, g - 1, inside]

        def pack(down_ref, up_ref):
            for pieces, out in (
                (down_pieces(nxt, 0), down_ref),
                (up_pieces(nxt, 0, depth, False), up_ref),
            ):
                for name, c, plane, planes, at in spots(pieces):
                    source = e if name == "e" else h
                    out[pl.ds(at, planes)] = source[c, pl.ds(g + plane, planes), inside]

        @pl.when(even)
        def _():
            pack(far_out, near_out)

        @pl.when(jnp.logical_not(even))
        def _():
            pack(near_out, far_out)

    for copy in copies:
        copy.wait()


def spectrum_kernel(chunks, scattered, monitors, height, info, table, *refs):
    samples = refs[: 2 * len(chunks)]
    out = refs[-1]
    rows, width = samples[0].shape[2:]
    f = pl.program_id(0)
    steps = sum(chunks)
    pad = jnp.zeros((height - rows, width), jnp.float32)
    for m in range(monitors):
        start = monitor_info(info, m, monitors)[1]
        for side in range(2):
            c = info[0] if side == 0 else 1 - info[0]
            planes = []
            for k, d in enumerate(chunks):
                at = jnp.bitwise_xor(m, info[3]) if scattered[k] else m
                planes += [samples[2 * k + side][at, t] for t in range(d)]
            for part in range(2):
                total = planes[0] * table[f, part * steps]
                for t in range(1, steps):
                    total = total + planes[t] * table[f, part * steps + t]
                out[0, part, m, c] = pltpu.roll(jnp.concatenate([total, pad], 0), start, 0)


def share(total, slabs, scatter):
    def swap(block, stride):
        return lax.ppermute(block, "slab", [(i, i ^ stride) for i in range(slabs)])

    strides = [2**k for k in range(1, slabs.bit_length() - 1)]
    if not scatter:
        for stride in strides:
            total = total + swap(total, stride)
        return total
    quarter = lax.axis_index("slab") // 4 % 4
    pieces = [
        swap(lax.dynamic_index_in_dim(total, quarter ^ x, 0, keepdims=False), 4 * x)
        for x in (1, 2, 3)
    ]
    part = lax.dynamic_index_in_dim(total, quarter, 0, keepdims=False)
    for piece in pieces:
        part = part + piece
    for stride in strides:
        if stride not in (4, 8):
            part = part + swap(part, stride)
    return jnp.stack([part] + [swap(part, 4 * x) for x in (1, 2, 3)])


def per_device(
    slabs, e_start, h_start, material, mat_permit, mat_loss, monitor_z, monitor_span, freq_bins
):
    depth, height, width = e_start.shape[1:]
    monitors = monitor_z.shape[0]
    freqs = freq_bins.shape[0]
    rows = 3 * height // 4
    mats = GHOST - 1
    me = lax.axis_index("slab")
    info = jnp.concatenate(
        [
            jnp.stack(
                [
                    me % 2,
                    (me > 0).astype(jnp.int32),
                    (me < slabs - 1).astype(jnp.int32),
                    me // 4 % 4,
                ]
            ),
            monitor_z - me * depth,
            monitor_span[:, 0],
            monitor_span[:, 1] - monitor_span[:, 0],
        ]
    ).astype(jnp.int32)
    tables = jnp.stack([mat_permit, mat_loss])
    moments = jnp.arange(1, STEPS + 1, dtype=jnp.int32)
    phase_turns = freq_bins[:, None] * moments[None, :] % PERIOD
    angles = phase_turns.astype(jnp.float32) * jnp.float32(2.0 * math.pi / PERIOD)
    phase_table = jnp.concatenate([jnp.cos(angles), -jnp.sin(angles)], 1)

    far_pairs = []
    for i in range(1, slabs - 1, 2):
        far_pairs += [(i, i + 1), (i + 1, i)]
    near_pairs = [(i, i ^ 1) for i in range(slabs)]

    def near_swap(block):
        return lax.ppermute(block, "slab", near_pairs)

    def f32(*shape):
        return jax.ShapeDtypeStruct(shape, jnp.float32)

    def scratch(ghosts):
        planes = depth + 2 * ghosts
        padded = (3, planes, height + 2 * PAD, width)
        return [pltpu.VMEM(padded, jnp.float32)] * 2 + [
            pltpu.VMEM((2, planes, height, width), jnp.float32)
        ]

    d = ROUNDS[0]
    size = message_size(d, mats, depth, True)
    copies = sum(1 for _ in spots(down_pieces(d, mats))) + sum(
        1 for _ in spots(up_pieces(d, mats, depth, True))
    )
    with jax.named_scope("first_pack"):
        far, near = pl.pallas_call(
            functools.partial(first_pack_kernel, d, mats, depth),
            out_shape=[f32(size, height, width)] * 2,
            in_specs=[HBM] * 3,
            out_specs=[VMEM] * 2,
            scratch_shapes=[
                pltpu.VMEM((2, mats, height, width), jnp.int32),
                pltpu.SemaphoreType.DMA((copies,)),
            ],
            compiler_params=params(),
            cost_estimate=cost(2),
        )(e_start, h_start, material)

    state = [f32(*e_start.shape), f32(*h_start.shape)]
    e, h = e_start, h_start
    coefs = ghosts = below = None
    chunks = []
    for k, d in enumerate(ROUNDS):
        first = k == 0
        nxt = ROUNDS[k + 1] if k + 1 < len(ROUNDS) else 0
        far = lax.ppermute(far, "slab", far_pairs)
        near = near_swap(near)
        samples = [f32(monitors, d, rows, width)] * 2
        with jax.named_scope(f"inner{k}"):
            kernel = functools.partial(inner_kernel, d, first, depth, monitors, rows)
            if first:
                e, h, coefs, mine, other = pl.pallas_call(
                    kernel,
                    out_shape=state + [f32(2, depth, height, width)] + samples,
                    in_specs=[SMEM, SMEM, HBM, HBM, HBM],
                    out_specs=[ANY] * 3 + [VMEM] * 2,
                    scratch_shapes=scratch(1)
                    + [
                        pltpu.VMEM((depth, height, width), jnp.int32),
                        pltpu.SemaphoreType.DMA((8,)),
                    ],
                    compiler_params=params(),
                    cost_estimate=cost(5),
                )(info, tables, e, h, material)
            else:
                e, h, mine, other = pl.pallas_call(
                    kernel,
                    out_shape=state + samples,
                    in_specs=[SMEM] + [ANY] * 3,
                    out_specs=[ANY] * 2 + [VMEM] * 2,
                    input_output_aliases={1: 0, 2: 1},
                    scratch_shapes=scratch(1) + [pltpu.SemaphoreType.DMA((8,))],
                    compiler_params=params(),
                    cost_estimate=cost(5),
                )(info, e, h, coefs)
        operands = [info, e, h, coefs, mine, other, far, near]
        specs = [SMEM] + [ANY] * 3 + [VMEM] * 4
        if first:
            operands += [tables]
            specs += [SMEM]
        else:
            operands += [ghosts, below]
            specs += [VMEM] * 2
        outs = state + samples
        if nxt:
            size = message_size(nxt, 0, depth, False)
            outs = outs + [f32(3, height, width)] + [f32(size, height, width)] * 2
            if first:
                outs = outs + [f32(2, 2 * mats, height, width)]
        with jax.named_scope(f"edge{k}"):
            results = pl.pallas_call(
                functools.partial(edge_kernel, d, nxt, first, depth, monitors, rows),
                out_shape=outs,
                in_specs=specs,
                out_specs=[ANY] * 2 + [VMEM] * (len(outs) - 2),
                input_output_aliases={1: 0, 2: 1},
                scratch_shapes=scratch(GHOST) + [pltpu.SemaphoreType.DMA((16,))],
                compiler_params=params(),
                cost_estimate=cost(4),
            )(*operands)
        e, h, mine, other = results[:4]
        if nxt:
            below, far, near = results[4:7]
            if first:
                ghosts = results[7]
        total = share(mine + near_swap(other), slabs, SCATTER[k])
        chunks += [total, near_swap(total)]

    with jax.named_scope("spectrum"):
        block = (1, 2, monitors, 2, height, width)
        spectrum = pl.pallas_call(
            functools.partial(spectrum_kernel, ROUNDS, SCATTER, monitors, height),
            out_shape=f32(freqs, *block[1:]),
            grid=(freqs,),
            in_specs=[SMEM, SMEM] + [VMEM] * len(chunks),
            out_specs=pl.BlockSpec(block, lambda f: (f, 0, 0, 0, 0, 0)),
            compiler_params=params(),
            cost_estimate=cost(5),
        )(info, phase_table, *chunks)
    return e, h, spectrum


def solution(mesh):
    slabs = mesh.shape["slab"]
    in_specs = (
        P(None, ("design", "slab"), None, None),
        P(None, ("design", "slab"), None, None),
        P(("design", "slab"), None, None),
        P(),
        P(),
        P(),
        P(),
        P("slab"),
    )
    out_specs = (
        P(None, ("design", "slab"), None, None),
        P(None, ("design", "slab"), None, None),
        P(("design", "slab"), None, None, None, None, None),
    )
    return jax.shard_map(
        functools.partial(per_device, slabs),
        mesh=mesh,
        in_specs=in_specs,
        out_specs=out_specs,
        check_vma=False,
    )
```

```python
import functools
import math

import jax
import jax.numpy as jnp
from jax import lax
from jax.experimental import pallas as pl
from jax.experimental.pallas import tpu as pltpu
from jax.sharding import PartitionSpec as P

STEPS = 8
PERIOD = 512
ROUNDS = (4, 4)
SCATTER = (True, True)
GHOST = max(ROUNDS)
COURANT = 0.5
VMEM = pl.BlockSpec(memory_space=pltpu.VMEM)
SMEM = pl.BlockSpec(memory_space=pltpu.SMEM)
ANY = pl.BlockSpec(memory_space=pl.ANY)
HBM = pl.BlockSpec(memory_space=pltpu.HBM)
LIMIT = 24 * 1024 * 1024
PACK_LIMIT = 60 * 1024 * 1024
PAD = 8


def params(limit=LIMIT):
    return pltpu.CompilerParams(vmem_limit_bytes=limit)


def cost(microseconds):
    return pl.CostEstimate(
        flops=0, bytes_accessed=int(microseconds * 3.0e6), transcendentals=0
    )


def down_pieces(d, mats):
    pieces = [("e", 0, 2, 0, d)]
    if d > 1:
        pieces += [("e", 2, 1, 0, d - 1), ("h", 0, 3, 0, d - 1)]
    if mats:
        pieces += [("m", 0, 1, 0, mats)]
    return pieces


def up_pieces(d, mats, depth, first):
    pieces = [("e", 0, 3, depth - d, d)]
    if first:
        pieces += [("h", 0, 2, depth - d, d)]
        if d > 1:
            pieces += [("h", 2, 1, depth - d + 1, d - 1)]
    else:
        if d > 1:
            pieces += [("h", 0, 2, depth - d, d - 1)]
        if d > 2:
            pieces += [("h", 2, 1, depth - d + 1, d - 2)]
    if mats:
        pieces += [("m", 0, 1, depth - mats, mats)]
    return pieces


def size_of(pieces):
    return sum(p[2] * p[4] for p in pieces)


def message_size(d, mats, depth, first):
    return max(size_of(down_pieces(d, mats)), size_of(up_pieces(d, mats, depth, first)))


def spots(pieces):
    at = 0
    for name, comp, comps, plane, planes in pieces:
        for c in range(comp, comp + comps):
            yield name, c, plane, planes, at
            at += planes


def start_all(pairs, sem):
    copies = [pltpu.make_async_copy(a, b, sem.at[k]) for k, (a, b) in enumerate(pairs)]
    for copy in copies:
        copy.start()
    return copies


def first_pack_kernel(d, mats, depth, e_ref, h_ref, m_ref, far_ref, near_ref, m_in, m_out, sem):
    even = lax.rem(lax.axis_index("slab"), 2) == 0

    def pack(down_ref, up_ref):
        sides = (
            (down_pieces(d, mats), down_ref),
            (up_pieces(d, mats, depth, True), up_ref),
        )
        reads, moves, writes = [], [], []
        for k, (pieces, out) in enumerate(sides):
            for name, c, plane, planes, at in spots(pieces):
                target = out.at[pl.ds(at, planes)]
                if name == "m":
                    reads.append((m_ref.at[pl.ds(plane, planes)], m_in.at[k]))
                    writes.append((m_out.at[k], target))
                else:
                    source = e_ref if name == "e" else h_ref
                    moves.append((source.at[c, pl.ds(plane, planes)], target))
        copies = start_all(reads + moves, sem)
        for copy in copies[: len(reads)]:
            copy.wait()
        for k in range(len(reads)):
            m_out[k] = m_in[k].astype(jnp.float32)
        copies = copies[len(reads) :] + start_all(writes, sem)
        for copy in copies:
            copy.wait()

    @pl.when(even)
    def _():
        pack(far_ref, near_ref)

    @pl.when(jnp.logical_not(even))
    def _():
        pack(near_ref, far_ref)


class Yee:
    def __init__(self, e, h, coefs, height, width, first_plane, below):
        self.e, self.h, self.coefs = e, h, coefs
        self.first_plane, self.width = first_plane, width
        self.own = pl.ds(PAD, height)
        self.next_row, self.last_row = pl.ds(PAD + 1, height), pl.ds(PAD - 1, height)
        lane = lax.broadcasted_iota(jnp.int32, (height, width), 1)
        self.lane_last, self.lane_first = lane == width - 1, lane == 0
        self.ghost_factor = None if below is None else COURANT * below.astype(jnp.float32)
        planes = e.shape[1]
        e[:, :, pl.ds(PAD + height, PAD)] = jnp.zeros((3, planes, PAD, width), jnp.float32)
        h[:, :, pl.ds(0, PAD)] = jnp.zeros((3, planes, PAD, width), jnp.float32)

    def fore_x(self, v):
        return jnp.where(self.lane_last, 0.0, pltpu.roll(v, self.width - 1, 1)) - v

    def back_x(self, v):
        return v - jnp.where(self.lane_first, 0.0, pltpu.roll(v, 1, 1))

    def step_h(self, z, ghost=False):
        e, h, own, up = self.e, self.h, self.own, self.next_row
        at = self.first_plane + z
        factor = self.ghost_factor if ghost else COURANT
        ex, ey, ez = e[0, at, own], e[1, at, own], e[2, at, own]
        h[0, at, own] = h[0, at, own] - factor * ((e[2, at, up] - ez) - (e[1, at + 1, own] - ey))
        h[1, at, own] = h[1, at, own] - factor * ((e[0, at + 1, own] - ex) - self.fore_x(ez))
        h[2, at, own] = h[2, at, own] - factor * (self.fore_x(ey) - (e[0, at, up] - ex))

    def step_e(self, z):
        e, h, own, down = self.e, self.h, self.own, self.last_row
        at = self.first_plane + z
        hx, hy, hz = h[0, at, own], h[1, at, own], h[2, at, own]
        keep, drive = self.coefs[0, at], self.coefs[1, at]
        e[0, at, own] = keep * e[0, at, own] + drive * (
            (hz - h[2, at, down]) - (hy - h[1, at - 1, own])
        )
        e[1, at, own] = keep * e[1, at, own] + drive * (
            (hx - h[0, at - 1, own]) - self.back_x(hz)
        )
        e[2, at, own] = keep * e[2, at, own] + drive * (self.back_x(hy) - (hx - h[0, at, down]))


def material_tables(tables, width):
    loss = [jnp.full((1, width), tables[1, k], jnp.float32) for k in range(tables.shape[1])]
    permit = [jnp.full((1, width), tables[0, k], jnp.float32) for k in range(tables.shape[1])]
    keeps = [(1.0 - x) / (1.0 + x) for x in loss]
    drives = [COURANT / (p * (1.0 + x)) for p, x in zip(permit, loss)]
    return keeps, drives


def look_up(values, which):
    total = jnp.broadcast_to(values[0], which.shape)
    for k in range(1, len(values)):
        total = jnp.where(which == k, values[k], total)
    return total


def monitor_info(info, m, monitors):
    return info[4 + m], info[4 + monitors + m], info[4 + 2 * monitors + m]


def take_sample(e, c, spot, start, extent, rows):
    height, width = e.shape[2] - 2 * PAD, e.shape[3]
    plane = pltpu.roll(e[c, spot, pl.ds(PAD, height)], height - start, 0)[:rows]
    return jnp.where(lax.broadcasted_iota(jnp.int32, (rows, width), 0) < extent, plane, 0.0)


def inner_kernel(d, before, depth, monitors, rows, info, *refs):
    first = not before
    if first:
        tables, e_in, h_in, m_in, *refs = refs
    else:
        e_in, h_in, coefs_in, fresh_in, *refs = refs
    e_out, h_out, mine_out, other_out, edge_out, *refs = refs
    if first:
        coefs_out, e, h, coefs, m_buf, sem = refs
    else:
        e, h, coefs, sem = refs
    height, width = e_in.shape[2:]
    g = 1
    own, inside = pl.ds(g, depth), pl.ds(PAD, height)
    fields = ((e_in, e), (h_in, h))
    if first:
        moves = [(x_in.at[c], x.at[c, own, inside]) for x_in, x in fields for c in range(3)]
        moves.append((m_in, m_buf))
    else:
        middle = depth - 2 * before
        moves = []
        for k, (x_in, x) in enumerate(fields):
            for source, planes, at in (
                (x_in.at[:, pl.ds(before, middle)], middle, before),
                (fresh_in.at[k, :, pl.ds(0, before)], before, 0),
                (fresh_in.at[k, :, pl.ds(before, before)], before, depth - before),
            ):
                moves.append((source, x.at[:, pl.ds(g + at, planes), inside]))
        moves += [(coefs_in.at[k], coefs.at[k, own]) for k in range(2)]
    copies = start_all(moves, sem)
    yee = Yee(e, h, coefs, height, width, g, None)
    if first:
        copies.pop().wait()
        keeps, drives = material_tables(tables, width)

        def fill(z, _):
            which = m_buf[z]
            coefs[0, g + z] = look_up(keeps, which)
            coefs[1, g + z] = look_up(drives, which)
            return 0

        lax.fori_loop(0, depth, fill, 0)
    for copy in copies:
        copy.wait()

    mine, other = info[0], 1 - info[0]
    group = 4
    for s in range(1, d + 1):
        low, high = s, depth - s
        yee.step_h(low - 1)

        def chunk(base, planes):
            for u in range(planes):
                yee.step_h(base + u)
            for u in range(planes):
                yee.step_e(base + u)

        whole = (high - low) // group

        def body(k, _):
            chunk(low + group * k, group)
            return 0

        lax.fori_loop(0, whole, body, 0)
        if low + group * whole < high:
            chunk(low + group * whole, high - low - group * whole)
        for m in range(monitors):
            offset, start, extent = monitor_info(info, m, monitors)
            held = jnp.logical_and(offset >= low, offset < high)
            taken = jnp.where(held, extent, 0)
            spot = g + jnp.clip(offset, 0, depth - 1)
            mine_out[m, s - 1] = take_sample(e, mine, spot, start, taken, rows)
            other_out[m, s - 1] = take_sample(e, other, spot, start, taken, rows)

    moves = []
    for k, (x, x_out) in enumerate(((e, e_out), (h, h_out))):
        moves.append((x.at[:, pl.ds(g, d), inside], edge_out.at[k, :, pl.ds(0, d)]))
        moves.append(
            (x.at[:, pl.ds(g + depth - 1 - d, d + 1), inside], edge_out.at[k, :, pl.ds(d, d + 1)])
        )
        moves += [(x.at[c, own, inside], x_out.at[c]) for c in range(3)]
    if first:
        moves += [(coefs.at[k, own], coefs_out.at[k]) for k in range(2)]
    for copy in start_all(moves, sem):
        copy.wait()


def edge_kernel(d, nxt, first, depth, monitors, rows, info, *refs):
    edge_in, coefs_in, mine_in, other_in, far_in, near_in, *refs = refs
    mats = GHOST - 1
    if first:
        tables, *refs = refs
    else:
        ghosts_in, below_in, _, *refs = refs
    fresh_out, mine_out, *refs = refs
    if nxt:
        below_out, far_out, near_out, *refs = refs
        if first:
            ghosts_out, *refs = refs
    else:
        other_out, *refs = refs
    e, h, coefs, sem = refs
    height, width = edge_in.shape[3:]
    g = GHOST
    inside = pl.ds(PAD, height)
    even = info[0] == 0
    below, above = info[1], info[2]

    moves = []
    for k, x in enumerate((e, h)):
        for source, planes, at in ((0, d, 0), (d, d + 1, depth - 1 - d)):
            moves.append(
                (edge_in.at[k, :, pl.ds(source, planes)], x.at[:, pl.ds(g + at, planes), inside])
            )
    for plane in (0, depth - d):
        moves.append((coefs_in.at[:, pl.ds(plane, d)], coefs.at[:, pl.ds(g + plane, d)]))
    copies = start_all(moves, sem)
    yee = Yee(e, h, coefs, height, width, g, below)

    sides = (
        (-depth, up_pieces(d, mats if first else 0, depth, first)),
        (depth, down_pieces(d, mats if first else 0)),
    )

    def unpack(below_ref, above_ref):
        for (shift, pieces), source in zip(sides, (below_ref, above_ref)):
            for name, c, plane, planes, at in spots(pieces):
                where = pl.ds(g + plane + shift, planes)
                value = source[pl.ds(at * height, planes * height)]
                value = value.reshape(planes, height, width)
                if name == "e":
                    e[c, where, inside] = value
                elif name == "h":
                    h[c, where, inside] = value
                else:
                    coefs[0, where] = value

    @pl.when(even)
    def _():
        unpack(far_in, near_in)

    @pl.when(jnp.logical_not(even))
    def _():
        unpack(near_in, far_in)

    ghost_planes = list(range(g - mats, g)) + list(range(g + depth, g + depth + mats))
    if first:
        keeps, drives = material_tables(tables, width)
        for at in ghost_planes:
            alive = (below if at < g else above).astype(jnp.float32)
            which = coefs[0, at].astype(jnp.int32)
            coefs[0, at] = look_up(keeps, which) * alive
            coefs[1, at] = look_up(drives, which) * alive
        if nxt:
            for k, at in enumerate(ghost_planes):
                ghosts_out[:, k] = coefs[:, at]
    else:
        for k, at in enumerate(ghost_planes):
            coefs[:, at] = ghosts_in[:, k]
        h[:, g - 1, inside] = below_in[...]
    for copy in copies:
        copy.wait()

    mine, other = info[0], 1 - info[0]
    for s in range(1, d + 1):
        lower = list(range(s - d, s))
        upper = list(range(depth - s, depth + d - s))
        for z in lower:
            yee.step_h(z - 1, z - 1 < 0)
        for z in upper:
            yee.step_h(z)
        for z in lower + upper:
            yee.step_e(z)
        for m in range(monitors):
            offset, start, extent = monitor_info(info, m, monitors)
            held = jnp.logical_or(
                jnp.logical_and(offset >= 0, offset < s),
                jnp.logical_and(offset >= depth - s, offset < depth),
            )
            spot = g + jnp.clip(offset, 0, depth - 1)
            mine_out[m, s - 1] = jnp.where(
                held, take_sample(e, mine, spot, start, extent, rows), mine_in[m, s - 1]
            )
            fresh = jnp.where(
                held, take_sample(e, other, spot, start, extent, rows), other_in[m, s - 1]
            )
            if nxt:
                at = near_out.shape[0] - (monitors * d - m * d - s + 1) * rows
                near_out[pl.ds(at, rows)] = fresh
            else:
                other_out[m, s - 1] = fresh

    moves = []
    for k, x in enumerate((e, h)):
        for j, plane in enumerate((0, depth - d)):
            moves.append(
                (x.at[:, pl.ds(g + plane, d), inside], fresh_out.at[k, :, pl.ds(j * d, d)])
            )
    copies = start_all(moves, sem)
    if nxt:
        below_out[...] = h[:, g - 1, inside]

        def pack(down_ref, up_ref):
            for pieces, out in (
                (down_pieces(nxt, 0), down_ref),
                (up_pieces(nxt, 0, depth, False), up_ref),
            ):
                for name, c, plane, planes, at in spots(pieces):
                    source = e if name == "e" else h
                    value = source[c, pl.ds(g + plane, planes), inside]
                    out[pl.ds(at * height, planes * height)] = value.reshape(-1, width)

        @pl.when(even)
        def _():
            pack(far_out, near_out)

        @pl.when(jnp.logical_not(even))
        def _():
            pack(near_out, far_out)

    for copy in copies:
        copy.wait()


def merge_kernel(d, depth, e_in, h_in, fresh, e_out, h_out, sem):
    moves = []
    for k, x_out in enumerate((e_out, h_out)):
        for j, plane in enumerate((0, depth - d)):
            moves.append((fresh.at[k, :, pl.ds(j * d, d)], x_out.at[:, pl.ds(plane, d)]))
    for copy in start_all(moves, sem):
        copy.wait()


def partial_kernel(d, at_step, scattered, monitors, info, table, mine, other, out):
    f = pl.program_id(0)
    steps = table.shape[1] // 2
    for m in range(monitors):
        at = jnp.bitwise_xor(m, info[3]) if scattered else m
        for side, samples in enumerate((mine, other)):
            planes = [samples[at, t] for t in range(d)]
            for part in range(2):
                total = planes[0] * table[f, part * steps + at_step]
                for t in range(1, d):
                    total = total + planes[t] * table[f, part * steps + at_step + t]
                out[f, part, m, side] = total


def spectrum_kernel(
    d, at_step, scattered, monitors, freqs, info, table, before, mine, other, out, blocks, sem
):
    rows, width = mine.shape[2:]
    height = blocks.shape[4]
    steps = table.shape[1] // 2
    pad = jnp.zeros((height - rows, width), jnp.float32)

    def body(f, _):
        for m in range(monitors):
            start = monitor_info(info, m, monitors)[1]
            at = jnp.bitwise_xor(m, info[3]) if scattered else m
            for side, samples in enumerate((mine, other)):
                c = info[0] if side == 0 else 1 - info[0]
                planes = [samples[at, t] for t in range(d)]
                for part in range(2):
                    total = before[f, part, m, side]
                    for t in range(d):
                        total = total + planes[t] * table[f, part * steps + at_step + t]
                    blocks[f, part, m, c] = pltpu.roll(
                        jnp.concatenate([total, pad], 0), start, 0
                    )
        pltpu.make_async_copy(blocks.at[f], out.at[f], sem.at[f]).start()
        return 0

    lax.fori_loop(0, freqs, body, 0)
    for f in range(freqs):
        pltpu.make_async_copy(blocks.at[f], out.at[f], sem.at[f]).wait()


def share(total, slabs, scatter):
    def swap(block, stride):
        return lax.ppermute(block, "slab", [(i, i ^ stride) for i in range(slabs)])

    strides = [2**k for k in range(1, slabs.bit_length() - 1)]
    if not scatter:
        total = total + swap(total, strides[0])

        def rest():
            result = total
            for stride in strides[1:]:
                result = result + swap(result, stride)
            return result

        return total, rest
    quarter = lax.axis_index("slab") // 4 % 4
    pieces = [
        swap(lax.dynamic_index_in_dim(total, quarter ^ x, 0, keepdims=False), 4 * x)
        for x in (1, 2, 3)
    ]
    part = lax.dynamic_index_in_dim(total, quarter, 0, keepdims=False)
    for piece in pieces:
        part = part + piece

    def rest():
        result = part
        for stride in strides:
            if stride not in (4, 8):
                result = result + swap(result, stride)
        return jnp.stack([result] + [swap(result, 4 * x) for x in (1, 2, 3)])

    return part, rest


def per_device(
    slabs, e_start, h_start, material, mat_permit, mat_loss, monitor_z, monitor_span, freq_bins
):
    depth, height, width = e_start.shape[1:]
    monitors = monitor_z.shape[0]
    freqs = freq_bins.shape[0]
    rows = 3 * height // 4
    mats = GHOST - 1
    me = lax.axis_index("slab")
    info = jnp.concatenate(
        [
            jnp.stack(
                [
                    me % 2,
                    (me > 0).astype(jnp.int32),
                    (me < slabs - 1).astype(jnp.int32),
                    me // 4 % 4,
                ]
            ),
            monitor_z - me * depth,
            monitor_span[:, 0],
            monitor_span[:, 1] - monitor_span[:, 0],
        ]
    ).astype(jnp.int32)
    tables = jnp.stack([mat_permit, mat_loss])
    moments = jnp.arange(1, STEPS + 1, dtype=jnp.int32)
    phase_turns = freq_bins[:, None] * moments[None, :] % PERIOD
    angles = phase_turns.astype(jnp.float32) * jnp.float32(2.0 * math.pi / PERIOD)
    phase_table = jnp.concatenate([jnp.cos(angles), -jnp.sin(angles)], 1)

    far_pairs = []
    for i in range(1, slabs - 1, 2):
        far_pairs += [(i, i + 1), (i + 1, i)]
    near_pairs = [(i, i ^ 1) for i in range(slabs)]

    def near_swap(block):
        return lax.ppermute(block, "slab", near_pairs)

    def f32(*shape):
        return jax.ShapeDtypeStruct(shape, jnp.float32)

    def scratch(ghosts):
        planes = depth + 2 * ghosts
        padded = (3, planes, height + 2 * PAD, width)
        return [pltpu.VMEM(padded, jnp.float32)] * 2 + [
            pltpu.VMEM((2, planes, height, width), jnp.float32)
        ]

    d = ROUNDS[0]
    size = message_size(d, mats, depth, True)
    copies = sum(1 for _ in spots(down_pieces(d, mats))) + sum(
        1 for _ in spots(up_pieces(d, mats, depth, True))
    )
    with jax.named_scope("first_pack"):
        far, near = pl.pallas_call(
            functools.partial(first_pack_kernel, d, mats, depth),
            out_shape=[f32(size, height, width)] * 2,
            in_specs=[HBM] * 3,
            out_specs=[HBM] * 2,
            scratch_shapes=[
                pltpu.VMEM((2, mats, height, width), jnp.int32),
                pltpu.VMEM((2, mats, height, width), jnp.float32),
                pltpu.SemaphoreType.DMA((copies,)),
            ],
            compiler_params=params(PACK_LIMIT),
            cost_estimate=cost(2),
        )(e_start, h_start, material)
    far, near = far.reshape(-1, width), near.reshape(-1, width)

    state = [f32(*e_start.shape), f32(*h_start.shape)]
    e, h = e_start, h_start
    coefs = ghosts = below = fresh = None
    chunks = []
    mine = None
    for k, d in enumerate(ROUNDS):
        first = k == 0
        nxt = ROUNDS[k + 1] if k + 1 < len(ROUNDS) else 0
        extra = near.shape[0] - far.shape[0]
        far = lax.ppermute(far, "slab", far_pairs)
        near = near_swap(near)
        if not first:
            theirs = near[-extra:].reshape(mine.shape)
            part, rest = share(mine + theirs, slabs, SCATTER[k - 1])
        samples = [f32(monitors, d, rows, width)] * 2
        edge = f32(2, 3, 2 * d + 1, height, width)
        with jax.named_scope(f"inner{k}"):
            kernel = functools.partial(
                inner_kernel, d, 0 if first else ROUNDS[k - 1], depth, monitors, rows
            )
            if first:
                e, h, mine, other, edge, coefs = pl.pallas_call(
                    kernel,
                    out_shape=state + samples + [edge, f32(2, depth, height, width)],
                    in_specs=[SMEM, SMEM, HBM, HBM, HBM],
                    out_specs=[ANY] * 2 + [VMEM] * 3 + [ANY],
                    scratch_shapes=scratch(1)
                    + [
                        pltpu.VMEM((depth, height, width), jnp.int32),
                        pltpu.SemaphoreType.DMA((12,)),
                    ],
                    compiler_params=params(),
                    cost_estimate=cost(5),
                )(info, tables, e, h, material)
            else:
                e, h, mine, other, edge = pl.pallas_call(
                    kernel,
                    out_shape=state + samples + [edge],
                    in_specs=[SMEM] + [ANY] * 3 + [VMEM],
                    out_specs=[ANY] * 2 + [VMEM] * 3,
                    scratch_shapes=scratch(1) + [pltpu.SemaphoreType.DMA((12,))],
                    compiler_params=params(),
                    cost_estimate=cost(5),
                )(info, e, h, coefs, fresh)
        operands = [info, edge, coefs, mine, other, far, near]
        specs = [SMEM, VMEM, ANY] + [VMEM] * 4
        if first:
            operands += [tables]
            specs += [SMEM]
        else:
            operands += [ghosts, below, part]
            specs += [VMEM] * 2 + [ANY]
        outs = [f32(2, 3, 2 * d, height, width), samples[0]]
        if nxt:
            size = message_size(nxt, 0, depth, False) * height
            extra = monitors * d * rows
            outs += [f32(3, height, width), f32(size, width), f32(size + extra, width)]
            if first:
                outs += [f32(2, 2 * mats, height, width)]
        else:
            outs += [samples[0]]
        with jax.named_scope(f"edge{k}"):
            results = pl.pallas_call(
                functools.partial(edge_kernel, d, nxt, first, depth, monitors, rows),
                out_shape=outs,
                in_specs=specs,
                out_specs=[VMEM] * len(outs),
                scratch_shapes=scratch(GHOST) + [pltpu.SemaphoreType.DMA((8,))],
                compiler_params=params(),
                cost_estimate=cost(4),
            )(*operands)
        fresh, mine = results[:2]
        if nxt:
            below, far, near = results[2:5]
            if first:
                ghosts = results[5]
        else:
            other = results[2]
        if not first:
            total = rest()
            chunks.append((total, near_swap(total)))
    with jax.named_scope("merge"):
        e, h = pl.pallas_call(
            functools.partial(merge_kernel, d, depth),
            out_shape=state,
            in_specs=[ANY, ANY, VMEM],
            out_specs=[ANY, ANY],
            input_output_aliases={0: 0, 1: 1},
            scratch_shapes=[pltpu.SemaphoreType.DMA((4,))],
            compiler_params=params(),
            cost_estimate=cost(1),
        )(e, h, fresh)
    total = share(mine + near_swap(other), slabs, SCATTER[-1])[1]()
    chunks.append((total, near_swap(total)))

    done = 0
    sums = None
    for k, d in enumerate(ROUNDS[:-1]):
        with jax.named_scope(f"partial{k}"):
            sums = pl.pallas_call(
                functools.partial(partial_kernel, d, done, SCATTER[k], monitors),
                out_shape=f32(freqs, 2, monitors, 2, rows, width),
                grid=(freqs,),
                in_specs=[SMEM, SMEM] + [VMEM] * 2,
                out_specs=VMEM,
                compiler_params=params(),
                cost_estimate=cost(3),
            )(info, phase_table, *chunks[k])
        done += d
    with jax.named_scope("spectrum"):
        block = (2, monitors, 2, height, width)
        spectrum = pl.pallas_call(
            functools.partial(
                spectrum_kernel, ROUNDS[-1], done, SCATTER[-1], monitors, freqs
            ),
            out_shape=f32(freqs, *block),
            in_specs=[SMEM, SMEM] + [VMEM] * 3,
            out_specs=HBM,
            scratch_shapes=[
                pltpu.VMEM((freqs, *block), jnp.float32),
                pltpu.SemaphoreType.DMA((freqs,)),
            ],
            compiler_params=params(),
            cost_estimate=cost(4),
        )(info, phase_table, sums, *chunks[-1])
    return e, h, spectrum


def solution(mesh):
    slabs = mesh.shape["slab"]
    in_specs = (
        P(None, ("design", "slab"), None, None),
        P(None, ("design", "slab"), None, None),
        P(("design", "slab"), None, None),
        P(),
        P(),
        P(),
        P(),
        P("slab"),
    )
    out_specs = (
        P(None, ("design", "slab"), None, None),
        P(None, ("design", "slab"), None, None),
        P(("design", "slab"), None, None, None, None, None),
    )
    return jax.shard_map(
        functools.partial(per_device, slabs),
        mesh=mesh,
        in_specs=in_specs,
        out_specs=out_specs,
        check_vma=False,
    )
```

```python
import functools
import math

import jax
import jax.numpy as jnp
from jax import lax
from jax.experimental import pallas as pl
from jax.experimental.pallas import tpu as pltpu
from jax.sharding import PartitionSpec as P

STEPS = 8
PERIOD = 512
ROUNDS = (4, 4)
DEEP = (False, False)
GHOST = max(ROUNDS)
COURANT = 0.5
VMEM = pl.BlockSpec(memory_space=pltpu.VMEM)
SMEM = pl.BlockSpec(memory_space=pltpu.SMEM)
ANY = pl.BlockSpec(memory_space=pl.ANY)
HBM = pl.BlockSpec(memory_space=pltpu.HBM)
LIMIT = 12 * 1024 * 1024
PACK_LIMIT = 58 * 1024 * 1024
PAD = 8


def params(limit=LIMIT):
    return pltpu.CompilerParams(vmem_limit_bytes=limit)


def cost(microseconds):
    return pl.CostEstimate(
        flops=0, bytes_accessed=int(microseconds * 3.0e6), transcendentals=0
    )


def down_pieces(d, mats):
    pieces = [("e", 0, 2, 0, d)]
    if d > 1:
        pieces += [("e", 2, 1, 0, d - 1), ("h", 0, 3, 0, d - 1)]
    if mats:
        pieces += [("m", 0, 1, 0, mats)]
    return pieces


def up_pieces(d, mats, depth, first):
    pieces = [("e", 0, 3, depth - d, d)]
    if first:
        pieces += [("h", 0, 2, depth - d, d)]
        if d > 1:
            pieces += [("h", 2, 1, depth - d + 1, d - 1)]
    else:
        if d > 1:
            pieces += [("h", 0, 2, depth - d, d - 1)]
        if d > 2:
            pieces += [("h", 2, 1, depth - d + 1, d - 2)]
    if mats:
        pieces += [("m", 0, 1, depth - mats, mats)]
    return pieces


def size_of(pieces):
    return sum(p[2] * p[4] for p in pieces)


def message_size(d, mats, depth, first):
    return max(size_of(down_pieces(d, mats)), size_of(up_pieces(d, mats, depth, first)))


def spots(pieces):
    at = 0
    for name, comp, comps, plane, planes in pieces:
        for c in range(comp, comp + comps):
            yield name, c, plane, planes, at
            at += planes


def start_all(pairs, sem):
    copies = [pltpu.make_async_copy(a, b, sem.at[k]) for k, (a, b) in enumerate(pairs)]
    for copy in copies:
        copy.start()
    return copies


def first_pack_kernel(d, mats, depth, e_ref, h_ref, m_ref, far_ref, near_ref, m_in, sem):
    even = lax.rem(lax.axis_index("slab"), 2) == 0

    def pack(down_ref, up_ref):
        sides = (
            (down_pieces(d, mats), down_ref),
            (up_pieces(d, mats, depth, True), up_ref),
        )
        moves, mats_at = [], []
        for k, (pieces, out) in enumerate(sides):
            for name, c, plane, planes, at in spots(pieces):
                if name == "m":
                    moves.append((m_ref.at[pl.ds(plane, planes)], m_in.at[k]))
                    mats_at.append((k, out, at))
                else:
                    source = e_ref if name == "e" else h_ref
                    moves.append((source.at[c, pl.ds(plane, planes)], out.at[pl.ds(at, planes)]))
        for copy in start_all(moves, sem):
            copy.wait()
        for k, out, at in mats_at:
            out[pl.ds(at, mats)] = m_in[k].astype(jnp.float32)

    @pl.when(even)
    def _():
        pack(far_ref, near_ref)

    @pl.when(jnp.logical_not(even))
    def _():
        pack(near_ref, far_ref)


class Yee:
    def __init__(self, e, h, coefs, height, width, first_plane, below):
        self.e, self.h, self.coefs = e, h, coefs
        self.first_plane, self.width = first_plane, width
        self.own = pl.ds(PAD, height)
        self.next_row, self.last_row = pl.ds(PAD + 1, height), pl.ds(PAD - 1, height)
        lane = lax.broadcasted_iota(jnp.int32, (height, width), 1)
        self.lane_last, self.lane_first = lane == width - 1, lane == 0
        self.ghost_factor = None if below is None else COURANT * below.astype(jnp.float32)
        planes = e.shape[1]
        e[:, :, pl.ds(PAD + height, PAD)] = jnp.zeros((3, planes, PAD, width), jnp.float32)
        h[:, :, pl.ds(0, PAD)] = jnp.zeros((3, planes, PAD, width), jnp.float32)

    def fore_x(self, v):
        return jnp.where(self.lane_last, 0.0, pltpu.roll(v, self.width - 1, 1)) - v

    def back_x(self, v):
        return v - jnp.where(self.lane_first, 0.0, pltpu.roll(v, 1, 1))

    def step_h(self, z, ghost=False):
        e, h, own, up = self.e, self.h, self.own, self.next_row
        at = self.first_plane + z
        factor = self.ghost_factor if ghost else COURANT
        ex, ey, ez = e[0, at, own], e[1, at, own], e[2, at, own]
        h[0, at, own] = h[0, at, own] - factor * ((e[2, at, up] - ez) - (e[1, at + 1, own] - ey))
        h[1, at, own] = h[1, at, own] - factor * ((e[0, at + 1, own] - ex) - self.fore_x(ez))
        h[2, at, own] = h[2, at, own] - factor * (self.fore_x(ey) - (e[0, at, up] - ex))

    def step_e(self, z):
        e, h, own, down = self.e, self.h, self.own, self.last_row
        at = self.first_plane + z
        hx, hy, hz = h[0, at, own], h[1, at, own], h[2, at, own]
        keep, drive = self.coefs[0, at], self.coefs[1, at]
        e[0, at, own] = keep * e[0, at, own] + drive * (
            (hz - h[2, at, down]) - (hy - h[1, at - 1, own])
        )
        e[1, at, own] = keep * e[1, at, own] + drive * (
            (hx - h[0, at - 1, own]) - self.back_x(hz)
        )
        e[2, at, own] = keep * e[2, at, own] + drive * (self.back_x(hy) - (hx - h[0, at, down]))


def material_tables(tables, width):
    loss = [jnp.full((1, width), tables[1, k], jnp.float32) for k in range(tables.shape[1])]
    permit = [jnp.full((1, width), tables[0, k], jnp.float32) for k in range(tables.shape[1])]
    keeps = [(1.0 - x) / (1.0 + x) for x in loss]
    drives = [COURANT / (p * (1.0 + x)) for p, x in zip(permit, loss)]
    return keeps, drives


def look_up(values, which):
    total = jnp.broadcast_to(values[0], which.shape)
    for k in range(1, len(values)):
        total = jnp.where(which == k, values[k], total)
    return total


def monitor_info(info, m, monitors):
    return info[4 + m], info[4 + monitors + m], info[4 + 2 * monitors + m]


def take_sample(e, c, spot, start, extent, rows):
    height, width = e.shape[2] - 2 * PAD, e.shape[3]
    plane = pltpu.roll(e[c, spot, pl.ds(PAD, height)], height - start, 0)[:rows]
    return jnp.where(lax.broadcasted_iota(jnp.int32, (rows, width), 0) < extent, plane, 0.0)


def inner_kernel(d, first, depth, monitors, rows, info, *refs):
    if first:
        tables, e_in, h_in, m_in, *refs = refs
    else:
        e_in, h_in, coefs_in, *refs = refs
    e_out, h_out, mine_out, other_out, edge_out, *refs = refs
    if first:
        coefs_out, e, h, coefs, m_buf, sem = refs
    else:
        e, h, coefs, sem = refs
    height, width = e_in.shape[2:]
    g = 1
    own, inside = pl.ds(g, depth), pl.ds(PAD, height)
    fields = ((e_in, e), (h_in, h))
    moves = [(x_in.at[c], x.at[c, own, inside]) for x_in, x in fields for c in range(3)]
    if first:
        moves.append((m_in, m_buf))
    else:
        moves += [(coefs_in.at[k], coefs.at[k, own]) for k in range(2)]
    copies = start_all(moves, sem)
    yee = Yee(e, h, coefs, height, width, g, None)
    if first:
        copies.pop().wait()
        keeps, drives = material_tables(tables, width)

        def fill(z, _):
            which = m_buf[z]
            coefs[0, g + z] = look_up(keeps, which)
            coefs[1, g + z] = look_up(drives, which)
            return 0

        lax.fori_loop(0, depth, fill, 0)
    for copy in copies:
        copy.wait()

    mine, other = info[0], 1 - info[0]
    group = 4
    for s in range(1, d + 1):
        low, high = s, depth - s
        yee.step_h(low - 1)

        def chunk(base, planes):
            for u in range(planes):
                yee.step_h(base + u)
            for u in range(planes):
                yee.step_e(base + u)

        whole = (high - low) // group

        def body(k, _):
            chunk(low + group * k, group)
            return 0

        lax.fori_loop(0, whole, body, 0)
        if low + group * whole < high:
            chunk(low + group * whole, high - low - group * whole)
        for m in range(monitors):
            offset, start, extent = monitor_info(info, m, monitors)
            held = jnp.logical_and(offset >= low, offset < high)
            taken = jnp.where(held, extent, 0)
            spot = g + jnp.clip(offset, 0, depth - 1)
            mine_out[m, s - 1] = take_sample(e, mine, spot, start, taken, rows)
            other_out[m, s - 1] = take_sample(e, other, spot, start, taken, rows)

    moves = []
    for k, (x, x_out) in enumerate(((e, e_out), (h, h_out))):
        moves.append((x.at[:, pl.ds(g, d), inside], edge_out.at[k, :, pl.ds(0, d)]))
        moves.append(
            (x.at[:, pl.ds(g + depth - 1 - d, d + 1), inside], edge_out.at[k, :, pl.ds(d, d + 1)])
        )
        moves += [(x.at[c, own, inside], x_out.at[c]) for c in range(3)]
    if first:
        moves += [(coefs.at[k, own], coefs_out.at[k]) for k in range(2)]
    for copy in start_all(moves, sem):
        copy.wait()


def edge_kernel(d, nxt, first, depth, monitors, rows, info, *refs):
    edge_in, coefs_in, mine_in, other_in, far_in, near_in, *refs = refs
    mats = GHOST - 1
    if first:
        tables, *refs = refs
    else:
        ghosts_in, below_in, *refs = refs
    if nxt:
        _, _, e_out, h_out, mine_out, other_out, below_out, far_out, near_out, *refs = refs
        if first:
            ghosts_out, *refs = refs
    else:
        fresh_out, mine_out, other_out, *refs = refs
    e, h, coefs, sem = refs
    height, width = edge_in.shape[3:]
    g = GHOST
    inside = pl.ds(PAD, height)
    even = info[0] == 0
    below, above = info[1], info[2]

    moves = []
    for k, x in enumerate((e, h)):
        for source, planes, at in ((0, d, 0), (d, d + 1, depth - 1 - d)):
            moves.append(
                (edge_in.at[k, :, pl.ds(source, planes)], x.at[:, pl.ds(g + at, planes), inside])
            )
    for plane in (0, depth - d):
        moves.append((coefs_in.at[:, pl.ds(plane, d)], coefs.at[:, pl.ds(g + plane, d)]))
    if not first:
        moves.append((below_in, h.at[:, g - 1, inside]))
    copies = start_all(moves, sem)
    yee = Yee(e, h, coefs, height, width, g, below)

    sides = (
        (-depth, up_pieces(d, mats if first else 0, depth, first)),
        (depth, down_pieces(d, mats if first else 0)),
    )

    def unpack(below_ref, above_ref):
        for (shift, pieces), source in zip(sides, (below_ref, above_ref)):
            for name, c, plane, planes, at in spots(pieces):
                where = pl.ds(g + plane + shift, planes)
                value = source[pl.ds(at * height, planes * height)]
                value = value.reshape(planes, height, width)
                if name == "e":
                    e[c, where, inside] = value
                elif name == "h":
                    h[c, where, inside] = value
                else:
                    coefs[0, where] = value

    @pl.when(even)
    def _():
        unpack(far_in, near_in)

    @pl.when(jnp.logical_not(even))
    def _():
        unpack(near_in, far_in)

    ghost_planes = list(range(g - mats, g)) + list(range(g + depth, g + depth + mats))
    if first:
        keeps, drives = material_tables(tables, width)
        for at in ghost_planes:
            alive = (below if at < g else above).astype(jnp.float32)
            which = coefs[0, at].astype(jnp.int32)
            coefs[0, at] = look_up(keeps, which) * alive
            coefs[1, at] = look_up(drives, which) * alive
        if nxt:
            for k, at in enumerate(ghost_planes):
                ghosts_out[:, k] = coefs[:, at]
    else:
        for k, at in enumerate(ghost_planes):
            coefs[:, at] = ghosts_in[:, k]
    for copy in copies:
        copy.wait()

    mine, other = info[0], 1 - info[0]
    for s in range(1, d + 1):
        lower = list(range(s - d, s))
        upper = list(range(depth - s, depth + d - s))
        for z in lower:
            yee.step_h(z - 1, z - 1 < 0)
        for z in upper:
            yee.step_h(z)
        for z in lower + upper:
            yee.step_e(z)
        for m in range(monitors):
            offset, start, extent = monitor_info(info, m, monitors)
            held = jnp.logical_or(
                jnp.logical_and(offset >= 0, offset < s),
                jnp.logical_and(offset >= depth - s, offset < depth),
            )
            spot = g + jnp.clip(offset, 0, depth - 1)
            mine_out[m, s - 1] = jnp.where(
                held, take_sample(e, mine, spot, start, extent, rows), mine_in[m, s - 1]
            )
            fresh = jnp.where(
                held, take_sample(e, other, spot, start, extent, rows), other_in[m, s - 1]
            )
            other_out[m, s - 1] = fresh

    moves = []
    for k, x in enumerate((e, h)):
        for j, plane in enumerate((0, depth - d)):
            source = x.at[:, pl.ds(g + plane, d), inside]
            if nxt:
                moves.append((source, (e_out, h_out)[k].at[:, pl.ds(plane, d)]))
            else:
                moves.append((source, fresh_out.at[k, :, pl.ds(j * d, d)]))
    if nxt:
        moves.append((h.at[:, g - 1, inside], below_out))
    copies = start_all(moves, sem)
    if nxt:

        def pack(down_ref, up_ref):
            for pieces, out in (
                (down_pieces(nxt, 0), down_ref),
                (up_pieces(nxt, 0, depth, False), up_ref),
            ):
                for name, c, plane, planes, at in spots(pieces):
                    source = e if name == "e" else h
                    value = source[c, pl.ds(g + plane, planes), inside]
                    out[pl.ds(at * height, planes * height)] = value.reshape(-1, width)

        @pl.when(even)
        def _():
            pack(far_out, near_out)

        @pl.when(jnp.logical_not(even))
        def _():
            pack(near_out, far_out)

    for copy in copies:
        copy.wait()


def merge_kernel(d, depth, e_in, h_in, fresh, e_out, h_out, sem):
    moves = []
    for k, x_out in enumerate((e_out, h_out)):
        for j, plane in enumerate((0, depth - d)):
            moves.append((fresh.at[k, :, pl.ds(j * d, d)], x_out.at[:, pl.ds(plane, d)]))
    for copy in start_all(moves, sem):
        copy.wait()


def partial_kernel(d, at_step, monitors, info, table, mine, other, out):
    f = pl.program_id(0)
    steps = table.shape[1] // 2
    for m in range(monitors):
        at = jnp.bitwise_xor(m, info[3])
        for side, samples in enumerate((mine, other)):
            planes = [samples[at, t] for t in range(d)]
            for part in range(2):
                total = planes[0] * table[f, part * steps + at_step]
                for t in range(1, d):
                    total = total + planes[t] * table[f, part * steps + at_step + t]
                out[f, part, m, side] = total


def spectrum_kernel(
    d, at_step, monitors, freqs, info, table, before, mine, other, out, blocks, sem
):
    rows, width = mine.shape[2:]
    height = blocks.shape[4]
    steps = table.shape[1] // 2
    pad = jnp.zeros((height - rows, width), jnp.float32)

    def body(f, _):
        for m in range(monitors):
            start = monitor_info(info, m, monitors)[1]
            at = jnp.bitwise_xor(m, info[3])
            for side, samples in enumerate((mine, other)):
                c = info[0] if side == 0 else 1 - info[0]
                planes = [samples[at, t] for t in range(d)]
                for part in range(2):
                    total = before[f, part, m, side]
                    for t in range(d):
                        total = total + planes[t] * table[f, part * steps + at_step + t]
                    blocks[f, part, m, c] = pltpu.roll(
                        jnp.concatenate([total, pad], 0), start, 0
                    )
        pltpu.make_async_copy(blocks.at[f], out.at[f], sem.at[f]).start()
        return 0

    lax.fori_loop(0, freqs, body, 0)
    for f in range(freqs):
        pltpu.make_async_copy(blocks.at[f], out.at[f], sem.at[f]).wait()


class Sharing:
    def __init__(self, slabs, deep):
        self.slabs, self.deep = slabs, deep
        me = lax.axis_index("slab")
        self.low, self.high = me // 4 % 2, me // 8 % 2
        self.others = [
            2**k for k in range(1, slabs.bit_length() - 1) if 2**k not in (4, 8)
        ]

    def swap(self, block, stride):
        return lax.ppermute(block, "slab", [(i, i ^ stride) for i in range(self.slabs)])

    def scatter(self, total, hold):
        if self.deep:
            total = total.reshape(2, 2, *total.shape[1:])
            sent = lax.dynamic_index_in_dim(total, 1 - self.low, 0, keepdims=False)
            total = lax.dynamic_index_in_dim(total, self.low, 0, keepdims=False)
            total = total + self.swap(sent, 4)
            sent = lax.dynamic_index_in_dim(total, 1 - self.high, 0, keepdims=False)
            total = lax.dynamic_index_in_dim(total, self.high, 0, keepdims=False)
            return add(total, self.swap(sent, 8), hold=hold)
        quarter = 2 * self.low + self.high
        pieces = [
            lax.dynamic_index_in_dim(total, quarter ^ x, 0, keepdims=False) for x in range(4)
        ]
        pieces = pieces[:1] + [self.swap(pieces[x], s) for x, s in ((1, 8), (2, 4), (3, 12))]
        return add(*pieces, hold=hold)

    def spread(self, part, hold):
        for stride in self.others:
            part = add(part, self.swap(part, stride), hold=hold)
        return part

    def gather_near(self, part):
        return jnp.stack([part, self.swap(part, 8)]) if self.deep else part

    def gather_far(self, part):
        if self.deep:
            return jnp.concatenate([part, self.swap(part, 4)])
        return jnp.stack([part] + [self.swap(part, stride) for stride in (8, 4, 12)])


def add_kernel(*refs):
    *ins, _, out = refs
    total = ins[0][...]
    for more in ins[1:]:
        total = total + more[...]
    out[...] = total


def add(*blocks, hold):
    if hold is None:
        return sum(blocks[1:], blocks[0])
    with jax.named_scope("add"):
        return pl.pallas_call(
            add_kernel,
            out_shape=jax.ShapeDtypeStruct(blocks[0].shape, jnp.float32),
            in_specs=[VMEM] * len(blocks) + [ANY],
            out_specs=VMEM,
            compiler_params=params(),
            cost_estimate=cost(0.3),
        )(*blocks, hold)


def per_device(
    slabs, e_start, h_start, material, mat_permit, mat_loss, monitor_z, monitor_span, freq_bins
):
    depth, height, width = e_start.shape[1:]
    monitors = monitor_z.shape[0]
    freqs = freq_bins.shape[0]
    rows = 3 * height // 4
    mats = GHOST - 1
    me = lax.axis_index("slab")
    info = jnp.concatenate(
        [
            jnp.stack(
                [
                    me % 2,
                    (me > 0).astype(jnp.int32),
                    (me < slabs - 1).astype(jnp.int32),
                    2 * (me // 4 % 2) + me // 8 % 2,
                ]
            ),
            monitor_z - me * depth,
            monitor_span[:, 0],
            monitor_span[:, 1] - monitor_span[:, 0],
        ]
    ).astype(jnp.int32)
    tables = jnp.stack([mat_permit, mat_loss])
    moments = jnp.arange(1, STEPS + 1, dtype=jnp.int32)
    phase_turns = freq_bins[:, None] * moments[None, :] % PERIOD
    angles = phase_turns.astype(jnp.float32) * jnp.float32(2.0 * math.pi / PERIOD)
    phase_table = jnp.concatenate([jnp.cos(angles), -jnp.sin(angles)], 1)

    far_pairs = []
    for i in range(1, slabs - 1, 2):
        far_pairs += [(i, i + 1), (i + 1, i)]
    near_pairs = [(i, i ^ 1) for i in range(slabs)]

    def near_swap(block):
        return lax.ppermute(block, "slab", near_pairs)

    def f32(*shape):
        return jax.ShapeDtypeStruct(shape, jnp.float32)

    def scratch(ghosts):
        planes = depth + 2 * ghosts
        padded = (3, planes, height + 2 * PAD, width)
        return [pltpu.VMEM(padded, jnp.float32)] * 2 + [
            pltpu.VMEM((2, planes, height, width), jnp.float32)
        ]

    d = ROUNDS[0]
    size = message_size(d, mats, depth, True)
    copies = sum(1 for _ in spots(down_pieces(d, mats))) + sum(
        1 for _ in spots(up_pieces(d, mats, depth, True))
    )
    with jax.named_scope("first_pack"):
        far, near = pl.pallas_call(
            functools.partial(first_pack_kernel, d, mats, depth),
            out_shape=[f32(size, height, width)] * 2,
            in_specs=[HBM] * 3,
            out_specs=[VMEM] * 2,
            scratch_shapes=[
                pltpu.VMEM((2, mats, height, width), jnp.int32),
                pltpu.SemaphoreType.DMA((copies,)),
            ],
            compiler_params=params(PACK_LIMIT),
            cost_estimate=cost(2),
        )(e_start, h_start, material)
    far, near = far.reshape(-1, width), near.reshape(-1, width)

    state = [f32(*e_start.shape), f32(*h_start.shape)]
    e, h = e_start, h_start
    coefs = ghosts = below = fresh = None
    mine = None
    for k, d in enumerate(ROUNDS):
        first = k == 0
        nxt = ROUNDS[k + 1] if k + 1 < len(ROUNDS) else 0
        far = lax.ppermute(far, "slab", far_pairs)
        near = near_swap(near)
        if not first:
            early = Sharing(slabs, DEEP[k - 1])
            part = early.scatter(mine + near_swap(other), None)
        samples = [f32(monitors, d, rows, width)] * 2
        edge = f32(2, 3, 2 * d + 1, height, width)
        with jax.named_scope(f"inner{k}"):
            kernel = functools.partial(inner_kernel, d, first, depth, monitors, rows)
            if first:
                e, h, mine, other, edge, coefs = pl.pallas_call(
                    kernel,
                    out_shape=state + samples + [edge, f32(2, depth, height, width)],
                    in_specs=[SMEM, SMEM, HBM, HBM, HBM],
                    out_specs=[HBM] * 2 + [VMEM] * 3 + [ANY],
                    scratch_shapes=scratch(1)
                    + [
                        pltpu.VMEM((depth, height, width), jnp.int32),
                        pltpu.SemaphoreType.DMA((12,)),
                    ],
                    compiler_params=params(),
                    cost_estimate=cost(5),
                )(info, tables, e, h, material)
            else:
                e, h, mine, other, edge = pl.pallas_call(
                    kernel,
                    out_shape=state + samples + [edge],
                    in_specs=[SMEM, HBM, HBM, ANY],
                    out_specs=[HBM] * 2 + [VMEM] * 3,
                    input_output_aliases={1: 0, 2: 1},
                    scratch_shapes=scratch(1) + [pltpu.SemaphoreType.DMA((12,))],
                    compiler_params=params(),
                    cost_estimate=cost(5),
                )(info, e, h, coefs)
        operands = [info, edge, coefs, mine, other, far, near]
        specs = [SMEM, VMEM, ANY] + [VMEM] * 4
        if first:
            operands += [tables]
            specs += [SMEM]
        else:
            operands += [ghosts, below]
            specs += [VMEM, HBM]
        outs = [f32(2, 3, 2 * d, height, width)] + samples
        kinds = [VMEM] * 3
        aliases = {}
        if nxt:
            outs = state + samples
            kinds = [HBM] * 2 + [VMEM] * 2
            aliases = {len(operands): 0, len(operands) + 1: 1}
            operands += [e, h]
            specs += [HBM] * 2
            size = message_size(nxt, 0, depth, False) * height
            outs += [f32(3, height, width), f32(size, width), f32(size, width)]
            kinds += [HBM]
            if first:
                outs += [f32(2, 2 * mats, height, width)]
        with jax.named_scope(f"edge{k}"):
            results = pl.pallas_call(
                functools.partial(edge_kernel, d, nxt, first, depth, monitors, rows),
                out_shape=outs,
                in_specs=specs,
                out_specs=kinds + [VMEM] * (len(outs) - len(kinds)),
                input_output_aliases=aliases,
                scratch_shapes=scratch(GHOST) + [pltpu.SemaphoreType.DMA((8,))],
                compiler_params=params(),
                cost_estimate=cost(4),
            )(*operands)
        if nxt:
            e, h, mine, other, below, far, near = results[:7]
            if first:
                ghosts = results[7]
        else:
            fresh, mine, other = results
    with jax.named_scope("merge"):
        e, h = pl.pallas_call(
            functools.partial(merge_kernel, d, depth),
            out_shape=state,
            in_specs=[ANY, ANY, VMEM],
            out_specs=[ANY, ANY],
            input_output_aliases={0: 0, 1: 1},
            scratch_shapes=[pltpu.SemaphoreType.DMA((4,))],
            compiler_params=params(),
            cost_estimate=cost(1),
        )(e, h, fresh)
    late = Sharing(slabs, DEEP[-1])
    part = early.gather_far(early.gather_near(early.spread(part, None)))
    chunks = [(part, near_swap(part))]
    total = late.spread(late.scatter(mine + near_swap(other), None), None)
    total = late.gather_far(late.gather_near(total))
    chunks.append((total, near_swap(total)))

    done = 0
    sums = None
    for k, d in enumerate(ROUNDS[:-1]):
        with jax.named_scope(f"partial{k}"):
            sums = pl.pallas_call(
                functools.partial(partial_kernel, d, done, monitors),
                out_shape=f32(freqs, 2, monitors, 2, rows, width),
                grid=(freqs,),
                in_specs=[SMEM, SMEM] + [VMEM] * 2,
                out_specs=VMEM,
                compiler_params=params(),
                cost_estimate=cost(3),
            )(info, phase_table, *chunks[k])
        done += d
    with jax.named_scope("spectrum"):
        block = (2, monitors, 2, height, width)
        spectrum = pl.pallas_call(
            functools.partial(spectrum_kernel, ROUNDS[-1], done, monitors, freqs),
            out_shape=f32(freqs, *block),
            in_specs=[SMEM, SMEM] + [VMEM] * 3,
            out_specs=HBM,
            scratch_shapes=[
                pltpu.VMEM((freqs, *block), jnp.float32),
                pltpu.SemaphoreType.DMA((freqs,)),
            ],
            compiler_params=params(),
            cost_estimate=cost(4),
        )(info, phase_table, sums, *chunks[-1])
    return e, h, spectrum


def solution(mesh):
    slabs = mesh.shape["slab"]
    in_specs = (
        P(None, ("design", "slab"), None, None),
        P(None, ("design", "slab"), None, None),
        P(("design", "slab"), None, None),
        P(),
        P(),
        P(),
        P(),
        P("slab"),
    )
    out_specs = (
        P(None, ("design", "slab"), None, None),
        P(None, ("design", "slab"), None, None),
        P(("design", "slab"), None, None, None, None, None),
    )
    return jax.shard_map(
        functools.partial(per_device, slabs),
        mesh=mesh,
        in_specs=in_specs,
        out_specs=out_specs,
        check_vma=False,
    )
```

```python
import functools
import math

import jax
import jax.numpy as jnp
from jax import lax
from jax.experimental import pallas as pl
from jax.experimental.pallas import tpu as pltpu
from jax.sharding import PartitionSpec as P

STEPS = 8
PERIOD = 512
ROUNDS = (4, 4)
ROWS_WHEN = ("", "before")
GHOST = max(ROUNDS)
COURANT = 0.5
VMEM = pl.BlockSpec(memory_space=pltpu.VMEM)
SMEM = pl.BlockSpec(memory_space=pltpu.SMEM)
ANY = pl.BlockSpec(memory_space=pl.ANY)
HBM = pl.BlockSpec(memory_space=pltpu.HBM)
LIMIT = 12 * 1024 * 1024
PACK_LIMIT = 58 * 1024 * 1024
PAD = 8


def params(limit=LIMIT):
    return pltpu.CompilerParams(vmem_limit_bytes=limit)


def cost(microseconds):
    return pl.CostEstimate(
        flops=0, bytes_accessed=int(microseconds * 3.0e6), transcendentals=0
    )


def down_pieces(d, mats):
    pieces = [("e", 0, 2, 0, d)]
    if d > 1:
        pieces += [("e", 2, 1, 0, d - 1), ("h", 0, 3, 0, d - 1)]
    if mats:
        pieces += [("m", 0, 1, 0, mats)]
    return pieces


def up_pieces(d, mats, depth, first):
    pieces = [("e", 0, 3, depth - d, d)]
    if first:
        pieces += [("h", 0, 2, depth - d, d)]
        if d > 1:
            pieces += [("h", 2, 1, depth - d + 1, d - 1)]
    else:
        if d > 1:
            pieces += [("h", 0, 2, depth - d, d - 1)]
        if d > 2:
            pieces += [("h", 2, 1, depth - d + 1, d - 2)]
    if mats:
        pieces += [("m", 0, 1, depth - mats, mats)]
    return pieces


def size_of(pieces):
    return sum(p[2] * p[4] for p in pieces)


def message_size(d, mats, depth, first):
    return max(size_of(down_pieces(d, mats)), size_of(up_pieces(d, mats, depth, first)))


def spots(pieces):
    at = 0
    for name, comp, comps, plane, planes in pieces:
        for c in range(comp, comp + comps):
            yield name, c, plane, planes, at
            at += planes


def start_all(pairs, sem):
    copies = [pltpu.make_async_copy(a, b, sem.at[k]) for k, (a, b) in enumerate(pairs)]
    for copy in copies:
        copy.start()
    return copies


def first_pack_kernel(d, mats, depth, e_ref, h_ref, m_ref, far_ref, near_ref, m_in, sem):
    even = lax.rem(lax.axis_index("slab"), 2) == 0

    def pack(down_ref, up_ref):
        sides = (
            (down_pieces(d, mats), down_ref),
            (up_pieces(d, mats, depth, True), up_ref),
        )
        moves, mats_at = [], []
        for k, (pieces, out) in enumerate(sides):
            for name, c, plane, planes, at in spots(pieces):
                if name == "m":
                    moves.append((m_ref.at[pl.ds(plane, planes)], m_in.at[k]))
                    mats_at.append((k, out, at))
                else:
                    source = e_ref if name == "e" else h_ref
                    moves.append((source.at[c, pl.ds(plane, planes)], out.at[pl.ds(at, planes)]))
        for copy in start_all(moves, sem):
            copy.wait()
        for k, out, at in mats_at:
            out[pl.ds(at, mats)] = m_in[k].astype(jnp.float32)

    @pl.when(even)
    def _():
        pack(far_ref, near_ref)

    @pl.when(jnp.logical_not(even))
    def _():
        pack(near_ref, far_ref)


class Yee:
    def __init__(self, e, h, coefs, height, width, first_plane, below):
        self.e, self.h, self.coefs = e, h, coefs
        self.first_plane, self.width = first_plane, width
        self.own = pl.ds(PAD, height)
        self.next_row, self.last_row = pl.ds(PAD + 1, height), pl.ds(PAD - 1, height)
        lane = lax.broadcasted_iota(jnp.int32, (height, width), 1)
        self.lane_last, self.lane_first = lane == width - 1, lane == 0
        self.ghost_factor = None if below is None else COURANT * below.astype(jnp.float32)
        planes = e.shape[1]
        e[:, :, pl.ds(PAD + height, PAD)] = jnp.zeros((3, planes, PAD, width), jnp.float32)
        h[:, :, pl.ds(0, PAD)] = jnp.zeros((3, planes, PAD, width), jnp.float32)

    def fore_x(self, v):
        return jnp.where(self.lane_last, 0.0, pltpu.roll(v, self.width - 1, 1)) - v

    def back_x(self, v):
        return v - jnp.where(self.lane_first, 0.0, pltpu.roll(v, 1, 1))

    def step_h(self, z, ghost=False):
        e, h, own, up = self.e, self.h, self.own, self.next_row
        at = self.first_plane + z
        factor = self.ghost_factor if ghost else COURANT
        ex, ey, ez = e[0, at, own], e[1, at, own], e[2, at, own]
        h[0, at, own] = h[0, at, own] - factor * ((e[2, at, up] - ez) - (e[1, at + 1, own] - ey))
        h[1, at, own] = h[1, at, own] - factor * ((e[0, at + 1, own] - ex) - self.fore_x(ez))
        h[2, at, own] = h[2, at, own] - factor * (self.fore_x(ey) - (e[0, at, up] - ex))

    def step_e(self, z):
        e, h, own, down = self.e, self.h, self.own, self.last_row
        at = self.first_plane + z
        hx, hy, hz = h[0, at, own], h[1, at, own], h[2, at, own]
        keep, drive = self.coefs[0, at], self.coefs[1, at]
        e[0, at, own] = keep * e[0, at, own] + drive * (
            (hz - h[2, at, down]) - (hy - h[1, at - 1, own])
        )
        e[1, at, own] = keep * e[1, at, own] + drive * (
            (hx - h[0, at - 1, own]) - self.back_x(hz)
        )
        e[2, at, own] = keep * e[2, at, own] + drive * (self.back_x(hy) - (hx - h[0, at, down]))


def material_tables(tables, width):
    loss = [jnp.full((1, width), tables[1, k], jnp.float32) for k in range(tables.shape[1])]
    permit = [jnp.full((1, width), tables[0, k], jnp.float32) for k in range(tables.shape[1])]
    keeps = [(1.0 - x) / (1.0 + x) for x in loss]
    drives = [COURANT / (p * (1.0 + x)) for p, x in zip(permit, loss)]
    return keeps, drives


def look_up(values, which):
    total = jnp.broadcast_to(values[0], which.shape)
    for k in range(1, len(values)):
        total = jnp.where(which == k, values[k], total)
    return total


def monitor_info(info, m, monitors):
    return info[4 + m], info[4 + monitors + m], info[4 + 2 * monitors + m]


def take_sample(e, c, spot, start, extent, rows):
    height, width = e.shape[2] - 2 * PAD, e.shape[3]
    plane = pltpu.roll(e[c, spot, pl.ds(PAD, height)], height - start, 0)[:rows]
    return jnp.where(lax.broadcasted_iota(jnp.int32, (rows, width), 0) < extent, plane, 0.0)


def inner_kernel(d, first, depth, monitors, rows, info, *refs):
    if first:
        tables, e_in, h_in, m_in, *refs = refs
    else:
        e_in, h_in, coefs_in, *refs = refs
    e_out, h_out, mine_out, other_out, edge_out, *refs = refs
    if first:
        coefs_out, e, h, coefs, m_buf, sem = refs
    else:
        e, h, coefs, sem = refs
    height, width = e_in.shape[2:]
    g = 1
    own, inside = pl.ds(g, depth), pl.ds(PAD, height)
    fields = ((e_in, e), (h_in, h))
    moves = [(x_in.at[c], x.at[c, own, inside]) for x_in, x in fields for c in range(3)]
    if first:
        moves.append((m_in, m_buf))
    else:
        moves += [(coefs_in.at[k], coefs.at[k, own]) for k in range(2)]
    copies = start_all(moves, sem)
    yee = Yee(e, h, coefs, height, width, g, None)
    if first:
        copies.pop().wait()
        keeps, drives = material_tables(tables, width)

        def fill(z, _):
            which = m_buf[z]
            coefs[0, g + z] = look_up(keeps, which)
            coefs[1, g + z] = look_up(drives, which)
            return 0

        lax.fori_loop(0, depth, fill, 0)
    for copy in copies:
        copy.wait()

    mine, other = info[0], 1 - info[0]
    group = 4
    for s in range(1, d + 1):
        low, high = s, depth - s
        yee.step_h(low - 1)

        def chunk(base, planes):
            for u in range(planes):
                yee.step_h(base + u)
            for u in range(planes):
                yee.step_e(base + u)

        whole = (high - low) // group

        def body(k, _):
            chunk(low + group * k, group)
            return 0

        lax.fori_loop(0, whole, body, 0)
        if low + group * whole < high:
            chunk(low + group * whole, high - low - group * whole)
        for m in range(monitors):
            offset, start, extent = monitor_info(info, m, monitors)
            held = jnp.logical_and(offset >= low, offset < high)
            taken = jnp.where(held, extent, 0)
            spot = g + jnp.clip(offset, 0, depth - 1)
            mine_out[m, s - 1] = take_sample(e, mine, spot, start, taken, rows)
            other_out[m, s - 1] = take_sample(e, other, spot, start, taken, rows)

    moves = []
    for k, (x, x_out) in enumerate(((e, e_out), (h, h_out))):
        moves.append((x.at[:, pl.ds(g, d), inside], edge_out.at[k, :, pl.ds(0, d)]))
        moves.append(
            (x.at[:, pl.ds(g + depth - 1 - d, d + 1), inside], edge_out.at[k, :, pl.ds(d, d + 1)])
        )
        moves += [(x.at[c, own, inside], x_out.at[c]) for c in range(3)]
    if first:
        moves += [(coefs.at[k, own], coefs_out.at[k]) for k in range(2)]
    for copy in start_all(moves, sem):
        copy.wait()


def edge_kernel(d, nxt, first, depth, monitors, rows, info, *refs):
    edge_in, coefs_in, mine_in, other_in, far_in, near_in, *refs = refs
    mats = GHOST - 1
    if first:
        tables, *refs = refs
    else:
        ghosts_in, below_in, _, _, *refs = refs
    if nxt:
        _, _, e_out, h_out, mine_out, other_out, below_out, far_out, near_out, *refs = refs
        if first:
            ghosts_out, *refs = refs
    else:
        fresh_out, mine_out, other_out, _, _, *refs = refs
    e, h, coefs, sem = refs
    height, width = edge_in.shape[3:]
    g = GHOST
    inside = pl.ds(PAD, height)
    even = info[0] == 0
    below, above = info[1], info[2]

    moves = []
    for k, x in enumerate((e, h)):
        for source, planes, at in ((0, d, 0), (d, d + 1, depth - 1 - d)):
            moves.append(
                (edge_in.at[k, :, pl.ds(source, planes)], x.at[:, pl.ds(g + at, planes), inside])
            )
    for plane in (0, depth - d):
        moves.append((coefs_in.at[:, pl.ds(plane, d)], coefs.at[:, pl.ds(g + plane, d)]))
    if not first:
        moves.append((below_in, h.at[:, g - 1, inside]))
    copies = start_all(moves, sem)
    yee = Yee(e, h, coefs, height, width, g, below)

    sides = (
        (-depth, up_pieces(d, mats if first else 0, depth, first)),
        (depth, down_pieces(d, mats if first else 0)),
    )

    def unpack(below_ref, above_ref):
        for (shift, pieces), source in zip(sides, (below_ref, above_ref)):
            for name, c, plane, planes, at in spots(pieces):
                where = pl.ds(g + plane + shift, planes)
                value = source[pl.ds(at * height, planes * height)]
                value = value.reshape(planes, height, width)
                if name == "e":
                    e[c, where, inside] = value
                elif name == "h":
                    h[c, where, inside] = value
                else:
                    coefs[0, where] = value

    @pl.when(even)
    def _():
        unpack(far_in, near_in)

    @pl.when(jnp.logical_not(even))
    def _():
        unpack(near_in, far_in)

    ghost_planes = list(range(g - mats, g)) + list(range(g + depth, g + depth + mats))
    if first:
        keeps, drives = material_tables(tables, width)
        for at in ghost_planes:
            alive = (below if at < g else above).astype(jnp.float32)
            which = coefs[0, at].astype(jnp.int32)
            coefs[0, at] = look_up(keeps, which) * alive
            coefs[1, at] = look_up(drives, which) * alive
        if nxt:
            for k, at in enumerate(ghost_planes):
                ghosts_out[:, k] = coefs[:, at]
    else:
        for k, at in enumerate(ghost_planes):
            coefs[:, at] = ghosts_in[:, k]
    for copy in copies:
        copy.wait()

    mine, other = info[0], 1 - info[0]
    for s in range(1, d + 1):
        lower = list(range(s - d, s))
        upper = list(range(depth - s, depth + d - s))
        for z in lower:
            yee.step_h(z - 1, z - 1 < 0)
        for z in upper:
            yee.step_h(z)
        for z in lower + upper:
            yee.step_e(z)
        for m in range(monitors):
            offset, start, extent = monitor_info(info, m, monitors)
            held = jnp.logical_or(
                jnp.logical_and(offset >= 0, offset < s),
                jnp.logical_and(offset >= depth - s, offset < depth),
            )
            spot = g + jnp.clip(offset, 0, depth - 1)
            mine_out[m, s - 1] = jnp.where(
                held, take_sample(e, mine, spot, start, extent, rows), mine_in[m, s - 1]
            )
            fresh = jnp.where(
                held, take_sample(e, other, spot, start, extent, rows), other_in[m, s - 1]
            )
            other_out[m, s - 1] = fresh

    moves = []
    for k, x in enumerate((e, h)):
        for j, plane in enumerate((0, depth - d)):
            source = x.at[:, pl.ds(g + plane, d), inside]
            if nxt:
                moves.append((source, (e_out, h_out)[k].at[:, pl.ds(plane, d)]))
            else:
                moves.append((source, fresh_out.at[k, :, pl.ds(j * d, d)]))
    if nxt:
        moves.append((h.at[:, g - 1, inside], below_out))
    copies = start_all(moves, sem)
    if nxt:

        def pack(down_ref, up_ref):
            for pieces, out in (
                (down_pieces(nxt, 0), down_ref),
                (up_pieces(nxt, 0, depth, False), up_ref),
            ):
                for name, c, plane, planes, at in spots(pieces):
                    source = e if name == "e" else h
                    value = source[c, pl.ds(g + plane, planes), inside]
                    out[pl.ds(at * height, planes * height)] = value.reshape(-1, width)

        @pl.when(even)
        def _():
            pack(far_out, near_out)

        @pl.when(jnp.logical_not(even))
        def _():
            pack(near_out, far_out)

    for copy in copies:
        copy.wait()


def merge_kernel(d, depth, e_in, h_in, fresh, e_out, h_out, sem):
    moves = []
    for k, x_out in enumerate((e_out, h_out)):
        for j, plane in enumerate((0, depth - d)):
            moves.append((fresh.at[k, :, pl.ds(j * d, d)], x_out.at[:, pl.ds(plane, d)]))
    for copy in start_all(moves, sem):
        copy.wait()


def partial_kernel(d, at_step, monitors, info, table, mine, other, out):
    f = pl.program_id(0)
    steps = table.shape[1] // 2
    for m in range(monitors):
        at = jnp.bitwise_xor(m, info[3])
        for side, samples in enumerate((mine, other)):
            planes = [samples[at, t] for t in range(d)]
            for part in range(2):
                total = planes[0] * table[f, part * steps + at_step]
                for t in range(1, d):
                    total = total + planes[t] * table[f, part * steps + at_step + t]
                out[f, part, m, side] = total


def spectrum_kernel(
    d, at_step, monitors, freqs, info, table, before, mine, other, out, blocks, sem
):
    rows, width = mine.shape[2:]
    height = blocks.shape[4]
    steps = table.shape[1] // 2
    pad = jnp.zeros((height - rows, width), jnp.float32)

    def body(f, _):
        for m in range(monitors):
            start = monitor_info(info, m, monitors)[1]
            at = jnp.bitwise_xor(m, info[3])
            for side, samples in enumerate((mine, other)):
                c = info[0] if side == 0 else 1 - info[0]
                planes = [samples[at, t] for t in range(d)]
                for part in range(2):
                    total = before[f, part, m, side]
                    for t in range(d):
                        total = total + planes[t] * table[f, part * steps + at_step + t]
                    blocks[f, part, m, c] = pltpu.roll(
                        jnp.concatenate([total, pad], 0), start, 0
                    )
        pltpu.make_async_copy(blocks.at[f], out.at[f], sem.at[f]).start()
        return 0

    lax.fori_loop(0, freqs, body, 0)
    for f in range(freqs):
        pltpu.make_async_copy(blocks.at[f], out.at[f], sem.at[f]).wait()


class Sharing:
    def __init__(self, slabs, rows_when):
        self.slabs, self.rows_when = slabs, rows_when
        me = lax.axis_index("slab")
        self.quarter = 2 * (me // 4 % 2) + me // 8 % 2
        self.half = me // 2 % 2
        self.others = [2**k for k in range(1, slabs.bit_length() - 1)]
        self.others = [k for k in self.others if k not in ((4, 8) if not rows_when else (2, 4, 8))]

    def swap(self, block, stride):
        return lax.ppermute(block, "slab", [(i, i ^ stride) for i in range(self.slabs)])

    def halve(self, total, axis):
        sent = lax.dynamic_index_in_dim(total, 1 - self.half, axis, keepdims=False)
        kept = lax.dynamic_index_in_dim(total, self.half, axis, keepdims=False)
        return kept + self.swap(sent, 2)

    def scatter(self, total):
        if self.rows_when:
            total = total.reshape(total.shape[0], 2, -1, total.shape[-1])
        if self.rows_when == "before":
            total = self.halve(total, 1)
        pieces = [
            lax.dynamic_index_in_dim(total, self.quarter ^ x, 0, keepdims=False)
            for x in range(4)
        ]
        part = pieces[0]
        for x, stride in ((1, 8), (2, 4), (3, 12)):
            part = part + self.swap(pieces[x], stride)
        if self.rows_when == "after":
            part = self.halve(part, 0)
        for stride in self.others:
            part = part + self.swap(part, stride)
        return part

    def gather(self, part, shape):
        total = jnp.stack([part] + [self.swap(part, stride) for stride in (8, 4, 12)])
        if self.rows_when:
            theirs = self.swap(total, 2)
            first = self.half == 0
            total = jnp.stack(
                [jnp.where(first, total, theirs), jnp.where(first, theirs, total)], 1
            )
        return total.reshape(shape)


def per_device(
    slabs, e_start, h_start, material, mat_permit, mat_loss, monitor_z, monitor_span, freq_bins
):
    depth, height, width = e_start.shape[1:]
    monitors = monitor_z.shape[0]
    freqs = freq_bins.shape[0]
    rows = 3 * height // 4
    mats = GHOST - 1
    me = lax.axis_index("slab")
    info = jnp.concatenate(
        [
            jnp.stack(
                [
                    me % 2,
                    (me > 0).astype(jnp.int32),
                    (me < slabs - 1).astype(jnp.int32),
                    2 * (me // 4 % 2) + me // 8 % 2,
                ]
            ),
            monitor_z - me * depth,
            monitor_span[:, 0],
            monitor_span[:, 1] - monitor_span[:, 0],
        ]
    ).astype(jnp.int32)
    tables = jnp.stack([mat_permit, mat_loss])
    moments = jnp.arange(1, STEPS + 1, dtype=jnp.int32)
    phase_turns = freq_bins[:, None] * moments[None, :] % PERIOD
    angles = phase_turns.astype(jnp.float32) * jnp.float32(2.0 * math.pi / PERIOD)
    phase_table = jnp.concatenate([jnp.cos(angles), -jnp.sin(angles)], 1)

    far_pairs = []
    for i in range(1, slabs - 1, 2):
        far_pairs += [(i, i + 1), (i + 1, i)]
    near_pairs = [(i, i ^ 1) for i in range(slabs)]

    def near_swap(block):
        return lax.ppermute(block, "slab", near_pairs)

    def f32(*shape):
        return jax.ShapeDtypeStruct(shape, jnp.float32)

    def scratch(ghosts):
        planes = depth + 2 * ghosts
        padded = (3, planes, height + 2 * PAD, width)
        return [pltpu.VMEM(padded, jnp.float32)] * 2 + [
            pltpu.VMEM((2, planes, height, width), jnp.float32)
        ]

    d = ROUNDS[0]
    size = message_size(d, mats, depth, True)
    copies = sum(1 for _ in spots(down_pieces(d, mats))) + sum(
        1 for _ in spots(up_pieces(d, mats, depth, True))
    )
    with jax.named_scope("first_pack"):
        far, near = pl.pallas_call(
            functools.partial(first_pack_kernel, d, mats, depth),
            out_shape=[f32(size, height, width)] * 2,
            in_specs=[HBM] * 3,
            out_specs=[VMEM] * 2,
            scratch_shapes=[
                pltpu.VMEM((2, mats, height, width), jnp.int32),
                pltpu.SemaphoreType.DMA((copies,)),
            ],
            compiler_params=params(PACK_LIMIT),
            cost_estimate=cost(2),
        )(e_start, h_start, material)
    far, near = far.reshape(-1, width), near.reshape(-1, width)

    state = [f32(*e_start.shape), f32(*h_start.shape)]
    e, h = e_start, h_start
    coefs = ghosts = below = fresh = None
    mine = None
    for k, d in enumerate(ROUNDS):
        first = k == 0
        nxt = ROUNDS[k + 1] if k + 1 < len(ROUNDS) else 0
        far = lax.ppermute(far, "slab", far_pairs)
        near = near_swap(near)
        if not first:
            before = mine, other
        samples = [f32(monitors, d, rows, width)] * 2
        edge = f32(2, 3, 2 * d + 1, height, width)
        with jax.named_scope(f"inner{k}"):
            kernel = functools.partial(inner_kernel, d, first, depth, monitors, rows)
            if first:
                e, h, mine, other, edge, coefs = pl.pallas_call(
                    kernel,
                    out_shape=state + samples + [edge, f32(2, depth, height, width)],
                    in_specs=[SMEM, SMEM, HBM, HBM, HBM],
                    out_specs=[HBM] * 2 + [VMEM] * 3 + [ANY],
                    scratch_shapes=scratch(1)
                    + [
                        pltpu.VMEM((depth, height, width), jnp.int32),
                        pltpu.SemaphoreType.DMA((12,)),
                    ],
                    compiler_params=params(),
                    cost_estimate=cost(5),
                )(info, tables, e, h, material)
            else:
                e, h, mine, other, edge = pl.pallas_call(
                    kernel,
                    out_shape=state + samples + [edge],
                    in_specs=[SMEM, HBM, HBM, ANY],
                    out_specs=[HBM] * 2 + [VMEM] * 3,
                    input_output_aliases={1: 0, 2: 1},
                    scratch_shapes=scratch(1) + [pltpu.SemaphoreType.DMA((12,))],
                    compiler_params=params(),
                    cost_estimate=cost(5),
                )(info, e, h, coefs)
        operands = [info, edge, coefs, mine, other, far, near]
        specs = [SMEM, VMEM, ANY] + [VMEM] * 4
        if first:
            operands += [tables]
            specs += [SMEM]
        else:
            operands += [ghosts, below, *before]
            specs += [VMEM, HBM, ANY, ANY]
        outs = [f32(2, 3, 2 * d, height, width)] + samples
        kinds = [VMEM] * 3
        aliases = {}
        if not first:
            aliases = {len(operands) - 2: 3, len(operands) - 1: 4}
            outs += [f32(*before[0].shape)] * 2
            kinds += [ANY] * 2
        if nxt:
            outs = state + samples
            kinds = [HBM] * 2 + [VMEM] * 2
            aliases = {len(operands): 0, len(operands) + 1: 1}
            operands += [e, h]
            specs += [HBM] * 2
            size = message_size(nxt, 0, depth, False) * height
            outs += [f32(3, height, width), f32(size, width), f32(size, width)]
            kinds += [HBM]
            if first:
                outs += [f32(2, 2 * mats, height, width)]
        with jax.named_scope(f"edge{k}"):
            results = pl.pallas_call(
                functools.partial(edge_kernel, d, nxt, first, depth, monitors, rows),
                out_shape=outs,
                in_specs=specs,
                out_specs=kinds + [VMEM] * (len(outs) - len(kinds)),
                input_output_aliases=aliases,
                scratch_shapes=scratch(GHOST) + [pltpu.SemaphoreType.DMA((8,))],
                compiler_params=params(),
                cost_estimate=cost(4),
            )(*operands)
        if nxt:
            e, h, mine, other, below, far, near = results[:7]
            if first:
                ghosts = results[7]
        else:
            fresh, mine, other, *before = results
            early = Sharing(slabs, ROWS_WHEN[k - 1])
            part = early.scatter(before[0] + near_swap(before[1]))
    with jax.named_scope("merge"):
        e, h = pl.pallas_call(
            functools.partial(merge_kernel, d, depth),
            out_shape=state,
            in_specs=[ANY, ANY, VMEM],
            out_specs=[ANY, ANY],
            input_output_aliases={0: 0, 1: 1},
            scratch_shapes=[pltpu.SemaphoreType.DMA((4,))],
            compiler_params=params(),
            cost_estimate=cost(1),
        )(e, h, fresh)
    late = Sharing(slabs, ROWS_WHEN[-1])
    total = mine + near_swap(other)
    chunks = []
    for sharing, block in ((early, part), (late, late.scatter(total))):
        block = sharing.gather(block, total.shape)
        chunks.append((block, near_swap(block)))

    done = 0
    sums = None
    for k, d in enumerate(ROUNDS[:-1]):
        with jax.named_scope(f"partial{k}"):
            sums = pl.pallas_call(
                functools.partial(partial_kernel, d, done, monitors),
                out_shape=f32(freqs, 2, monitors, 2, rows, width),
                grid=(freqs,),
                in_specs=[SMEM, SMEM] + [VMEM] * 2,
                out_specs=VMEM,
                compiler_params=params(),
                cost_estimate=cost(3),
            )(info, phase_table, *chunks[k])
        done += d
    with jax.named_scope("spectrum"):
        block = (2, monitors, 2, height, width)
        spectrum = pl.pallas_call(
            functools.partial(spectrum_kernel, ROUNDS[-1], done, monitors, freqs),
            out_shape=f32(freqs, *block),
            in_specs=[SMEM, SMEM] + [VMEM] * 3,
            out_specs=HBM,
            scratch_shapes=[
                pltpu.VMEM((freqs, *block), jnp.float32),
                pltpu.SemaphoreType.DMA((freqs,)),
            ],
            compiler_params=params(),
            cost_estimate=cost(4),
        )(info, phase_table, sums, *chunks[-1])
    return e, h, spectrum


def solution(mesh):
    slabs = mesh.shape["slab"]
    in_specs = (
        P(None, ("design", "slab"), None, None),
        P(None, ("design", "slab"), None, None),
        P(("design", "slab"), None, None),
        P(),
        P(),
        P(),
        P(),
        P("slab"),
    )
    out_specs = (
        P(None, ("design", "slab"), None, None),
        P(None, ("design", "slab"), None, None),
        P(("design", "slab"), None, None, None, None, None),
    )
    return jax.shard_map(
        functools.partial(per_device, slabs),
        mesh=mesh,
        in_specs=in_specs,
        out_specs=out_specs,
        check_vma=False,
    )
```

```python
import functools
import math

import jax
import jax.numpy as jnp
from jax import lax
from jax.experimental import pallas as pl
from jax.experimental.pallas import tpu as pltpu
from jax.sharding import PartitionSpec as P

STEPS = 8
PERIOD = 512
ROUNDS = (4, 4)
ROWS_WHEN = ("", "before")
GHOST = max(ROUNDS)
COURANT = 0.5
VMEM = pl.BlockSpec(memory_space=pltpu.VMEM)
SMEM = pl.BlockSpec(memory_space=pltpu.SMEM)
ANY = pl.BlockSpec(memory_space=pl.ANY)
HBM = pl.BlockSpec(memory_space=pltpu.HBM)
LIMIT = 12 * 1024 * 1024
PAD = 8


def params(limit=LIMIT):
    return pltpu.CompilerParams(vmem_limit_bytes=limit)


def cost(microseconds):
    return pl.CostEstimate(
        flops=0, bytes_accessed=int(microseconds * 3.0e6), transcendentals=0
    )


def down_pieces(d, mats):
    pieces = [("e", 0, 2, 0, d)]
    if d > 1:
        pieces += [("e", 2, 1, 0, d - 1), ("h", 0, 3, 0, d - 1)]
    if mats:
        pieces += [("m", 0, 1, 0, mats)]
    return pieces


def up_pieces(d, mats, depth, first):
    pieces = [("e", 0, 3, depth - d, d)]
    if first:
        pieces += [("h", 0, 2, depth - d, d)]
        if d > 1:
            pieces += [("h", 2, 1, depth - d + 1, d - 1)]
    else:
        if d > 1:
            pieces += [("h", 0, 2, depth - d, d - 1)]
        if d > 2:
            pieces += [("h", 2, 1, depth - d + 1, d - 2)]
    if mats:
        pieces += [("m", 0, 1, depth - mats, mats)]
    return pieces


def size_of(pieces):
    return sum(p[2] * p[4] for p in pieces)


def message_size(d, mats, depth, first):
    return max(size_of(down_pieces(d, mats)), size_of(up_pieces(d, mats, depth, first)))


def spots(pieces):
    at = 0
    for name, comp, comps, plane, planes in pieces:
        for c in range(comp, comp + comps):
            yield name, c, plane, planes, at
            at += planes


def start_all(pairs, sem):
    copies = [pltpu.make_async_copy(a, b, sem.at[k]) for k, (a, b) in enumerate(pairs)]
    for copy in copies:
        copy.start()
    return copies


def first_pack_kernel(d, mats, depth, e_ref, h_ref, m_ref, far_ref, near_ref, m_in, sem):
    even = lax.rem(lax.axis_index("slab"), 2) == 0

    def pack(down_ref, up_ref):
        sides = (
            (down_pieces(d, mats), down_ref),
            (up_pieces(d, mats, depth, True), up_ref),
        )
        moves, mats_at = [], []
        for k, (pieces, out) in enumerate(sides):
            for name, c, plane, planes, at in spots(pieces):
                if name == "m":
                    moves.append((m_ref.at[pl.ds(plane, planes)], m_in.at[k]))
                    mats_at.append((k, out, at))
                else:
                    source = e_ref if name == "e" else h_ref
                    moves.append((source.at[c, pl.ds(plane, planes)], out.at[pl.ds(at, planes)]))
        for copy in start_all(moves, sem):
            copy.wait()
        for k, out, at in mats_at:
            out[pl.ds(at, mats)] = m_in[k].astype(jnp.float32)

    @pl.when(even)
    def _():
        pack(far_ref, near_ref)

    @pl.when(jnp.logical_not(even))
    def _():
        pack(near_ref, far_ref)


class Yee:
    def __init__(self, e, h, coefs, height, width, first_plane, below):
        self.e, self.h, self.coefs = e, h, coefs
        self.first_plane, self.width = first_plane, width
        self.own = pl.ds(PAD, height)
        self.next_row, self.last_row = pl.ds(PAD + 1, height), pl.ds(PAD - 1, height)
        lane = lax.broadcasted_iota(jnp.int32, (height, width), 1)
        self.lane_last, self.lane_first = lane == width - 1, lane == 0
        self.ghost_factor = None if below is None else COURANT * below.astype(jnp.float32)
        planes = e.shape[1]
        e[:, :, pl.ds(PAD + height, PAD)] = jnp.zeros((3, planes, PAD, width), jnp.float32)
        h[:, :, pl.ds(0, PAD)] = jnp.zeros((3, planes, PAD, width), jnp.float32)

    def fore_x(self, v):
        return jnp.where(self.lane_last, 0.0, pltpu.roll(v, self.width - 1, 1)) - v

    def back_x(self, v):
        return v - jnp.where(self.lane_first, 0.0, pltpu.roll(v, 1, 1))

    def step_h(self, z, ghost=False):
        e, h, own, up = self.e, self.h, self.own, self.next_row
        at = self.first_plane + z
        factor = self.ghost_factor if ghost else COURANT
        ex, ey, ez = e[0, at, own], e[1, at, own], e[2, at, own]
        h[0, at, own] = h[0, at, own] - factor * ((e[2, at, up] - ez) - (e[1, at + 1, own] - ey))
        h[1, at, own] = h[1, at, own] - factor * ((e[0, at + 1, own] - ex) - self.fore_x(ez))
        h[2, at, own] = h[2, at, own] - factor * (self.fore_x(ey) - (e[0, at, up] - ex))

    def step_e(self, z):
        e, h, own, down = self.e, self.h, self.own, self.last_row
        at = self.first_plane + z
        hx, hy, hz = h[0, at, own], h[1, at, own], h[2, at, own]
        keep, drive = self.coefs[0, at], self.coefs[1, at]
        e[0, at, own] = keep * e[0, at, own] + drive * (
            (hz - h[2, at, down]) - (hy - h[1, at - 1, own])
        )
        e[1, at, own] = keep * e[1, at, own] + drive * (
            (hx - h[0, at - 1, own]) - self.back_x(hz)
        )
        e[2, at, own] = keep * e[2, at, own] + drive * (self.back_x(hy) - (hx - h[0, at, down]))


def material_tables(tables, width):
    loss = [jnp.full((1, width), tables[1, k], jnp.float32) for k in range(tables.shape[1])]
    permit = [jnp.full((1, width), tables[0, k], jnp.float32) for k in range(tables.shape[1])]
    keeps = [(1.0 - x) / (1.0 + x) for x in loss]
    drives = [COURANT / (p * (1.0 + x)) for p, x in zip(permit, loss)]
    return keeps, drives


def look_up(values, which):
    total = jnp.broadcast_to(values[0], which.shape)
    for k in range(1, len(values)):
        total = jnp.where(which == k, values[k], total)
    return total


def monitor_info(info, m, monitors):
    return info[4 + m], info[4 + monitors + m], info[4 + 2 * monitors + m]


def take_sample(e, c, spot, start, extent, rows):
    height, width = e.shape[2] - 2 * PAD, e.shape[3]
    plane = pltpu.roll(e[c, spot, pl.ds(PAD, height)], height - start, 0)[:rows]
    return jnp.where(lax.broadcasted_iota(jnp.int32, (rows, width), 0) < extent, plane, 0.0)


def inner_kernel(d, first, depth, monitors, rows, info, *refs):
    if first:
        tables, e_in, h_in, m_in, *refs = refs
    else:
        e_in, h_in, coefs_in, *refs = refs
    e_out, h_out, mine_out, other_out, edge_out, *refs = refs
    if first:
        coefs_out, e, h, coefs, m_buf, sem = refs
    else:
        e, h, coefs, sem = refs
    height, width = e_in.shape[2:]
    g = 1
    own, inside = pl.ds(g, depth), pl.ds(PAD, height)
    fields = ((e_in, e), (h_in, h))
    moves = [(x_in.at[c], x.at[c, own, inside]) for x_in, x in fields for c in range(3)]
    if first:
        moves.append((m_in, m_buf))
    else:
        moves += [(coefs_in.at[k], coefs.at[k, own]) for k in range(2)]
    copies = start_all(moves, sem)
    yee = Yee(e, h, coefs, height, width, g, None)
    if first:
        copies.pop().wait()
        keeps, drives = material_tables(tables, width)

        def fill(z, _):
            which = m_buf[z]
            coefs[0, g + z] = look_up(keeps, which)
            coefs[1, g + z] = look_up(drives, which)
            return 0

        lax.fori_loop(0, depth, fill, 0)
    for copy in copies:
        copy.wait()

    mine, other = info[0], 1 - info[0]
    group = 4
    for s in range(1, d + 1):
        low, high = s, depth - s
        yee.step_h(low - 1)

        def chunk(base, planes):
            for u in range(planes):
                yee.step_h(base + u)
            for u in range(planes):
                yee.step_e(base + u)

        whole = (high - low) // group

        def body(k, _):
            chunk(low + group * k, group)
            return 0

        lax.fori_loop(0, whole, body, 0)
        if low + group * whole < high:
            chunk(low + group * whole, high - low - group * whole)
        for m in range(monitors):
            offset, start, extent = monitor_info(info, m, monitors)
            held = jnp.logical_and(offset >= low, offset < high)
            taken = jnp.where(held, extent, 0)
            spot = g + jnp.clip(offset, 0, depth - 1)
            mine_out[m, s - 1] = take_sample(e, mine, spot, start, taken, rows)
            other_out[m, s - 1] = take_sample(e, other, spot, start, taken, rows)

    moves = []
    for k, (x, x_out) in enumerate(((e, e_out), (h, h_out))):
        moves.append((x.at[:, pl.ds(g, d), inside], edge_out.at[k, :, pl.ds(0, d)]))
        moves.append(
            (x.at[:, pl.ds(g + depth - 1 - d, d + 1), inside], edge_out.at[k, :, pl.ds(d, d + 1)])
        )
        moves += [(x.at[c, own, inside], x_out.at[c]) for c in range(3)]
    if first:
        moves += [(coefs.at[k, own], coefs_out.at[k]) for k in range(2)]
    for copy in start_all(moves, sem):
        copy.wait()


def edge_kernel(d, nxt, first, depth, monitors, rows, info, *refs):
    edge_in, coefs_in, mine_in, other_in, far_in, near_in, *refs = refs
    mats = GHOST - 1
    if first:
        tables, *refs = refs
    else:
        ghosts_in, below_in, _, *refs = refs
    if nxt:
        _, _, e_out, h_out, mine_out, other_out, below_out, far_out, near_out, *refs = refs
        if first:
            ghosts_out, *refs = refs
    else:
        fresh_out, mine_out, other_out, _, *refs = refs
    e, h, coefs, sem = refs
    height, width = edge_in.shape[3:]
    g = GHOST
    inside = pl.ds(PAD, height)
    even = info[0] == 0
    below, above = info[1], info[2]

    moves = []
    for k, x in enumerate((e, h)):
        for source, planes, at in ((0, d, 0), (d, d + 1, depth - 1 - d)):
            moves.append(
                (edge_in.at[k, :, pl.ds(source, planes)], x.at[:, pl.ds(g + at, planes), inside])
            )
    for plane in (0, depth - d):
        moves.append((coefs_in.at[:, pl.ds(plane, d)], coefs.at[:, pl.ds(g + plane, d)]))
    if not first:
        moves.append((below_in, h.at[:, g - 1, inside]))
    copies = start_all(moves, sem)
    yee = Yee(e, h, coefs, height, width, g, below)

    sides = (
        (-depth, up_pieces(d, mats if first else 0, depth, first)),
        (depth, down_pieces(d, mats if first else 0)),
    )

    def unpack(below_ref, above_ref):
        for (shift, pieces), source in zip(sides, (below_ref, above_ref)):
            for name, c, plane, planes, at in spots(pieces):
                where = pl.ds(g + plane + shift, planes)
                value = source[pl.ds(at * height, planes * height)]
                value = value.reshape(planes, height, width)
                if name == "e":
                    e[c, where, inside] = value
                elif name == "h":
                    h[c, where, inside] = value
                else:
                    coefs[0, where] = value

    @pl.when(even)
    def _():
        unpack(far_in, near_in)

    @pl.when(jnp.logical_not(even))
    def _():
        unpack(near_in, far_in)

    ghost_planes = list(range(g - mats, g)) + list(range(g + depth, g + depth + mats))
    if first:
        keeps, drives = material_tables(tables, width)
        for at in ghost_planes:
            alive = (below if at < g else above).astype(jnp.float32)
            which = coefs[0, at].astype(jnp.int32)
            coefs[0, at] = look_up(keeps, which) * alive
            coefs[1, at] = look_up(drives, which) * alive
        if nxt:
            for k, at in enumerate(ghost_planes):
                ghosts_out[:, k] = coefs[:, at]
    else:
        for k, at in enumerate(ghost_planes):
            coefs[:, at] = ghosts_in[:, k]
    for copy in copies:
        copy.wait()

    mine, other = info[0], 1 - info[0]
    for s in range(1, d + 1):
        lower = list(range(s - d, s))
        upper = list(range(depth - s, depth + d - s))
        for z in lower:
            yee.step_h(z - 1, z - 1 < 0)
        for z in upper:
            yee.step_h(z)
        for z in lower + upper:
            yee.step_e(z)
        for m in range(monitors):
            offset, start, extent = monitor_info(info, m, monitors)
            held = jnp.logical_or(
                jnp.logical_and(offset >= 0, offset < s),
                jnp.logical_and(offset >= depth - s, offset < depth),
            )
            spot = g + jnp.clip(offset, 0, depth - 1)
            mine_out[m, s - 1] = jnp.where(
                held, take_sample(e, mine, spot, start, extent, rows), mine_in[m, s - 1]
            )
            fresh = jnp.where(
                held, take_sample(e, other, spot, start, extent, rows), other_in[m, s - 1]
            )
            other_out[m, s - 1] = fresh

    moves = []
    for k, x in enumerate((e, h)):
        for j, plane in enumerate((0, depth - d)):
            source = x.at[:, pl.ds(g + plane, d), inside]
            if nxt:
                moves.append((source, (e_out, h_out)[k].at[:, pl.ds(plane, d)]))
            else:
                moves.append((source, fresh_out.at[k, :, pl.ds(j * d, d)]))
    if nxt:
        moves.append((h.at[:, g - 1, inside], below_out))
    copies = start_all(moves, sem)
    if nxt:

        def pack(down_ref, up_ref):
            for pieces, out in (
                (down_pieces(nxt, 0), down_ref),
                (up_pieces(nxt, 0, depth, False), up_ref),
            ):
                for name, c, plane, planes, at in spots(pieces):
                    source = e if name == "e" else h
                    value = source[c, pl.ds(g + plane, planes), inside]
                    out[pl.ds(at * height, planes * height)] = value.reshape(-1, width)

        @pl.when(even)
        def _():
            pack(far_out, near_out)

        @pl.when(jnp.logical_not(even))
        def _():
            pack(near_out, far_out)

    for copy in copies:
        copy.wait()


def merge_kernel(d, depth, e_in, h_in, fresh, e_out, h_out, sem):
    moves = []
    for k, x_out in enumerate((e_out, h_out)):
        for j, plane in enumerate((0, depth - d)):
            moves.append((fresh.at[k, :, pl.ds(j * d, d)], x_out.at[:, pl.ds(plane, d)]))
    for copy in start_all(moves, sem):
        copy.wait()


def partial_kernel(d, at_step, monitors, info, table, mine, other, out):
    f = pl.program_id(0)
    steps = table.shape[1] // 2
    for m in range(monitors):
        at = jnp.bitwise_xor(m, info[3])
        for side, samples in enumerate((mine, other)):
            planes = [samples[at, t] for t in range(d)]
            for part in range(2):
                total = planes[0] * table[f, part * steps + at_step]
                for t in range(1, d):
                    total = total + planes[t] * table[f, part * steps + at_step + t]
                out[f, part, m, side] = total


def spectrum_kernel(
    d, at_step, monitors, freqs, info, table, before, mine, other, out, blocks, sem
):
    rows, width = mine.shape[2:]
    height = blocks.shape[4]
    steps = table.shape[1] // 2
    pad = jnp.zeros((height - rows, width), jnp.float32)

    def body(f, _):
        for m in range(monitors):
            start = monitor_info(info, m, monitors)[1]
            at = jnp.bitwise_xor(m, info[3])
            for side, samples in enumerate((mine, other)):
                c = info[0] if side == 0 else 1 - info[0]
                planes = [samples[at, t] for t in range(d)]
                for part in range(2):
                    total = before[f, part, m, side]
                    for t in range(d):
                        total = total + planes[t] * table[f, part * steps + at_step + t]
                    blocks[f, part, m, c] = pltpu.roll(
                        jnp.concatenate([total, pad], 0), start, 0
                    )
        pltpu.make_async_copy(blocks.at[f], out.at[f], sem.at[f]).start()
        return 0

    lax.fori_loop(0, freqs, body, 0)
    for f in range(freqs):
        pltpu.make_async_copy(blocks.at[f], out.at[f], sem.at[f]).wait()


class Sharing:
    def __init__(self, slabs, rows_when):
        self.slabs, self.rows_when = slabs, rows_when
        me = lax.axis_index("slab")
        self.quarter = 2 * (me // 4 % 2) + me // 8 % 2
        self.half = me // 2 % 2
        self.others = [2**k for k in range(1, slabs.bit_length() - 1)]
        self.others = [k for k in self.others if k not in ((4, 8) if not rows_when else (2, 4, 8))]

    def swap(self, block, stride):
        return lax.ppermute(block, "slab", [(i, i ^ stride) for i in range(self.slabs)])

    def halve(self, total, axis):
        sent = lax.dynamic_index_in_dim(total, 1 - self.half, axis, keepdims=False)
        kept = lax.dynamic_index_in_dim(total, self.half, axis, keepdims=False)
        return kept + self.swap(sent, 2)

    def scatter(self, total):
        if self.rows_when:
            total = total.reshape(total.shape[0], 2, -1, total.shape[-1])
        if self.rows_when == "before":
            total = self.halve(total, 1)
        pieces = [
            lax.dynamic_index_in_dim(total, self.quarter ^ x, 0, keepdims=False)
            for x in range(4)
        ]
        part = pieces[0]
        for x, stride in ((1, 8), (2, 4), (3, 12)):
            part = part + self.swap(pieces[x], stride)
        if self.rows_when == "after":
            part = self.halve(part, 0)
        for stride in self.others:
            part = part + self.swap(part, stride)
        return part

    def gather(self, part, shape):
        total = jnp.stack([part] + [self.swap(part, stride) for stride in (8, 4, 12)])
        if self.rows_when:
            theirs = self.swap(total, 2)
            first = self.half == 0
            total = jnp.stack(
                [jnp.where(first, total, theirs), jnp.where(first, theirs, total)], 1
            )
        return total.reshape(shape)


def per_device(
    slabs, e_start, h_start, material, mat_permit, mat_loss, monitor_z, monitor_span, freq_bins
):
    depth, height, width = e_start.shape[1:]
    monitors = monitor_z.shape[0]
    freqs = freq_bins.shape[0]
    rows = 3 * height // 4
    mats = GHOST - 1
    me = lax.axis_index("slab")
    info = jnp.concatenate(
        [
            jnp.stack(
                [
                    me % 2,
                    (me > 0).astype(jnp.int32),
                    (me < slabs - 1).astype(jnp.int32),
                    2 * (me // 4 % 2) + me // 8 % 2,
                ]
            ),
            monitor_z - me * depth,
            monitor_span[:, 0],
            monitor_span[:, 1] - monitor_span[:, 0],
        ]
    ).astype(jnp.int32)
    tables = jnp.stack([mat_permit, mat_loss])
    moments = jnp.arange(1, STEPS + 1, dtype=jnp.int32)
    phase_turns = freq_bins[:, None] * moments[None, :] % PERIOD
    angles = phase_turns.astype(jnp.float32) * jnp.float32(2.0 * math.pi / PERIOD)
    phase_table = jnp.concatenate([jnp.cos(angles), -jnp.sin(angles)], 1)

    far_pairs = []
    for i in range(1, slabs - 1, 2):
        far_pairs += [(i, i + 1), (i + 1, i)]
    near_pairs = [(i, i ^ 1) for i in range(slabs)]

    def near_swap(block):
        return lax.ppermute(block, "slab", near_pairs)

    def f32(*shape):
        return jax.ShapeDtypeStruct(shape, jnp.float32)

    def vmem(*shape):
        return pltpu.VMEM(shape, jnp.float32)

    def in_hbm(*arrays):
        return [pltpu.with_memory_space_constraint(x, pltpu.HBM) for x in arrays]

    def in_vmem(*arrays):
        return [pltpu.with_memory_space_constraint(x, pltpu.VMEM) for x in arrays]

    def scratch(ghosts):
        planes = depth + 2 * ghosts
        padded = (3, planes, height + 2 * PAD, width)
        return [pltpu.VMEM(padded, jnp.float32)] * 2 + [
            pltpu.VMEM((2, planes, height, width), jnp.float32)
        ]

    d = ROUNDS[0]
    size = message_size(d, mats, depth, True)
    copies = sum(1 for _ in spots(down_pieces(d, mats))) + sum(
        1 for _ in spots(up_pieces(d, mats, depth, True))
    )
    with jax.named_scope("first_pack"):
        far, near = pl.pallas_call(
            functools.partial(first_pack_kernel, d, mats, depth),
            out_shape=[vmem(size, height, width)] * 2,
            in_specs=[HBM] * 3,
            out_specs=[VMEM] * 2,
            scratch_shapes=[
                pltpu.VMEM((2, mats, height, width), jnp.int32),
                pltpu.SemaphoreType.DMA((copies,)),
            ],
            compiler_params=params(),
            cost_estimate=cost(2),
        )(*in_hbm(e_start, h_start, material))
    far, near = far.reshape(-1, width), near.reshape(-1, width)

    state = [f32(*e_start.shape), f32(*h_start.shape)]
    e, h = e_start, h_start
    coefs = ghosts = below = fresh = None
    mine = None
    for k, d in enumerate(ROUNDS):
        first = k == 0
        nxt = ROUNDS[k + 1] if k + 1 < len(ROUNDS) else 0
        far = lax.ppermute(far, "slab", far_pairs)
        near = near_swap(near)
        if not first:
            before = mine + near_swap(other)
        samples = [vmem(monitors, d, rows, width)] * 2
        edge = vmem(2, 3, 2 * d + 1, height, width)
        with jax.named_scope(f"inner{k}"):
            kernel = functools.partial(inner_kernel, d, first, depth, monitors, rows)
            if first:
                e, h, mine, other, edge, coefs = pl.pallas_call(
                    kernel,
                    out_shape=state + samples + [edge, vmem(2, depth, height, width)],
                    in_specs=[SMEM, SMEM, HBM, HBM, HBM],
                    out_specs=[HBM] * 2 + [VMEM] * 3 + [ANY],
                    scratch_shapes=scratch(1)
                    + [
                        pltpu.VMEM((depth, height, width), jnp.int32),
                        pltpu.SemaphoreType.DMA((12,)),
                    ],
                    compiler_params=params(),
                    cost_estimate=cost(5),
                )(info, tables, *in_hbm(e, h, material))
            else:
                e, h, mine, other, edge = pl.pallas_call(
                    kernel,
                    out_shape=state + samples + [edge],
                    in_specs=[SMEM, HBM, HBM, ANY],
                    out_specs=[HBM] * 2 + [VMEM] * 3,
                    input_output_aliases={1: 0, 2: 1},
                    scratch_shapes=scratch(1) + [pltpu.SemaphoreType.DMA((12,))],
                    compiler_params=params(),
                    cost_estimate=cost(5),
                )(info, *in_hbm(e, h), *in_vmem(coefs))
        operands = [info, *in_vmem(edge, coefs, mine, other, far, near)]
        specs = [SMEM, VMEM, ANY] + [VMEM] * 4
        if first:
            operands += [tables]
            specs += [SMEM]
        else:
            operands += in_vmem(ghosts, below, before)
            specs += [VMEM, VMEM, ANY]
        outs = [vmem(2, 3, 2 * d, height, width)] + samples
        kinds = [VMEM] * 3
        aliases = {}
        if not first:
            aliases = {len(operands) - 1: 3}
            outs += [vmem(*before.shape)]
            kinds += [ANY]
        if nxt:
            outs = state + samples
            kinds = [HBM] * 2 + [VMEM] * 2
            aliases = {len(operands): 0, len(operands) + 1: 1}
            operands += [e, h]
            specs += [HBM] * 2
            size = message_size(nxt, 0, depth, False) * height
            outs += [vmem(3, height, width), vmem(size, width), vmem(size, width)]
            kinds += [VMEM]
            if first:
                outs += [vmem(2, 2 * mats, height, width)]
        with jax.named_scope(f"edge{k}"):
            results = pl.pallas_call(
                functools.partial(edge_kernel, d, nxt, first, depth, monitors, rows),
                out_shape=outs,
                in_specs=specs,
                out_specs=kinds + [VMEM] * (len(outs) - len(kinds)),
                input_output_aliases=aliases,
                scratch_shapes=scratch(GHOST) + [pltpu.SemaphoreType.DMA((8,))],
                compiler_params=params(),
                cost_estimate=cost(4),
            )(*operands)
        if nxt:
            e, h, mine, other, below, far, near = results[:7]
            if first:
                ghosts = results[7]
        else:
            fresh, mine, other, before = results
            early = Sharing(slabs, ROWS_WHEN[k - 1])
            part = early.scatter(before)
    with jax.named_scope("merge"):
        e, h = pl.pallas_call(
            functools.partial(merge_kernel, d, depth),
            out_shape=state,
            in_specs=[ANY, ANY, VMEM],
            out_specs=[ANY, ANY],
            input_output_aliases={0: 0, 1: 1},
            scratch_shapes=[pltpu.SemaphoreType.DMA((4,))],
            compiler_params=params(),
            cost_estimate=cost(1),
        )(*in_hbm(e, h), *in_vmem(fresh))
    late = Sharing(slabs, ROWS_WHEN[-1])
    total = mine + near_swap(other)
    chunks = []
    for sharing, block in ((early, part), (late, late.scatter(total))):
        block = sharing.gather(block, total.shape)
        chunks.append((block, near_swap(block)))

    done = 0
    sums = None
    for k, d in enumerate(ROUNDS[:-1]):
        with jax.named_scope(f"partial{k}"):
            sums = pl.pallas_call(
                functools.partial(partial_kernel, d, done, monitors),
                out_shape=vmem(freqs, 2, monitors, 2, rows, width),
                grid=(freqs,),
                in_specs=[SMEM, SMEM] + [VMEM] * 2,
                out_specs=VMEM,
                compiler_params=params(),
                cost_estimate=cost(3),
            )(info, phase_table, *in_vmem(*chunks[k]))
        done += d
    with jax.named_scope("spectrum"):
        block = (2, monitors, 2, height, width)
        spectrum = pl.pallas_call(
            functools.partial(spectrum_kernel, ROUNDS[-1], done, monitors, freqs),
            out_shape=f32(freqs, *block),
            in_specs=[SMEM, SMEM] + [VMEM] * 3,
            out_specs=HBM,
            scratch_shapes=[
                pltpu.VMEM((freqs, *block), jnp.float32),
                pltpu.SemaphoreType.DMA((freqs,)),
            ],
            compiler_params=params(),
            cost_estimate=cost(4),
        )(info, phase_table, *in_vmem(sums, *chunks[-1]))
    return e, h, spectrum


def solution(mesh):
    slabs = mesh.shape["slab"]
    in_specs = (
        P(None, ("design", "slab"), None, None),
        P(None, ("design", "slab"), None, None),
        P(("design", "slab"), None, None),
        P(),
        P(),
        P(),
        P(),
        P("slab"),
    )
    out_specs = (
        P(None, ("design", "slab"), None, None),
        P(None, ("design", "slab"), None, None),
        P(("design", "slab"), None, None, None, None, None),
    )
    return jax.shard_map(
        functools.partial(per_device, slabs),
        mesh=mesh,
        in_specs=in_specs,
        out_specs=out_specs,
        check_vma=False,
    )
```

```python
import functools
import math

import jax
import jax.numpy as jnp
from jax import lax
from jax.experimental import pallas as pl
from jax.experimental.pallas import tpu as pltpu
from jax.sharding import PartitionSpec as P

STEPS = 8
PERIOD = 512
ROUNDS = (4, 4)
ROWS_WHEN = ("", "before")
GHOST = max(ROUNDS)
COURANT = 0.5
VMEM = pl.BlockSpec(memory_space=pltpu.VMEM)
SMEM = pl.BlockSpec(memory_space=pltpu.SMEM)
ANY = pl.BlockSpec(memory_space=pl.ANY)
HBM = pl.BlockSpec(memory_space=pltpu.HBM)
LIMIT = 12 * 1024 * 1024
PAD = 8


def params(limit=LIMIT):
    return pltpu.CompilerParams(vmem_limit_bytes=limit)


def cost(microseconds):
    return pl.CostEstimate(
        flops=0, bytes_accessed=int(microseconds * 3.0e6), transcendentals=0
    )


def down_pieces(d, mats):
    pieces = [("e", 0, 2, 0, d)]
    if d > 1:
        pieces += [("e", 2, 1, 0, d - 1), ("h", 0, 3, 0, d - 1)]
    if mats:
        pieces += [("m", 0, 1, 0, mats)]
    return pieces


def up_pieces(d, mats, depth, first):
    pieces = [("e", 0, 3, depth - d, d)]
    if first:
        pieces += [("h", 0, 2, depth - d, d)]
        if d > 1:
            pieces += [("h", 2, 1, depth - d + 1, d - 1)]
    else:
        if d > 1:
            pieces += [("h", 0, 2, depth - d, d - 1)]
        if d > 2:
            pieces += [("h", 2, 1, depth - d + 1, d - 2)]
    if mats:
        pieces += [("m", 0, 1, depth - mats, mats)]
    return pieces


def size_of(pieces):
    return sum(p[2] * p[4] for p in pieces)


def message_size(d, mats, depth, first):
    return max(size_of(down_pieces(d, mats)), size_of(up_pieces(d, mats, depth, first)))


def spots(pieces):
    at = 0
    for name, comp, comps, plane, planes in pieces:
        for c in range(comp, comp + comps):
            yield name, c, plane, planes, at
            at += planes


def start_all(pairs, sem):
    copies = [pltpu.make_async_copy(a, b, sem.at[k]) for k, (a, b) in enumerate(pairs)]
    for copy in copies:
        copy.start()
    return copies


def first_pack_kernel(d, mats, depth, e_ref, h_ref, m_ref, far_ref, near_ref, m_in, sem):
    even = lax.rem(lax.axis_index("slab"), 2) == 0

    def pack(down_ref, up_ref):
        sides = (
            (down_pieces(d, mats), down_ref),
            (up_pieces(d, mats, depth, True), up_ref),
        )
        moves, mats_at = [], []
        for k, (pieces, out) in enumerate(sides):
            for name, c, plane, planes, at in spots(pieces):
                if name == "m":
                    moves.append((m_ref.at[pl.ds(plane, planes)], m_in.at[k]))
                    mats_at.append((k, out, at))
                else:
                    source = e_ref if name == "e" else h_ref
                    moves.append((source.at[c, pl.ds(plane, planes)], out.at[pl.ds(at, planes)]))
        for copy in start_all(moves, sem):
            copy.wait()
        for k, out, at in mats_at:
            out[pl.ds(at, mats)] = m_in[k].astype(jnp.float32)

    @pl.when(even)
    def _():
        pack(far_ref, near_ref)

    @pl.when(jnp.logical_not(even))
    def _():
        pack(near_ref, far_ref)


class Yee:
    def __init__(self, e, h, coefs, height, width, first_plane, below):
        self.e, self.h, self.coefs = e, h, coefs
        self.first_plane, self.width = first_plane, width
        self.own = pl.ds(PAD, height)
        self.next_row, self.last_row = pl.ds(PAD + 1, height), pl.ds(PAD - 1, height)
        lane = lax.broadcasted_iota(jnp.int32, (height, width), 1)
        self.lane_last, self.lane_first = lane == width - 1, lane == 0
        self.ghost_factor = None if below is None else COURANT * below.astype(jnp.float32)
        planes = e.shape[1]
        e[:, :, pl.ds(PAD + height, PAD)] = jnp.zeros((3, planes, PAD, width), jnp.float32)
        h[:, :, pl.ds(0, PAD)] = jnp.zeros((3, planes, PAD, width), jnp.float32)

    def fore_x(self, v):
        return jnp.where(self.lane_last, 0.0, pltpu.roll(v, self.width - 1, 1)) - v

    def back_x(self, v):
        return v - jnp.where(self.lane_first, 0.0, pltpu.roll(v, 1, 1))

    def step_h(self, z, ghost=False):
        e, h, own, up = self.e, self.h, self.own, self.next_row
        at = self.first_plane + z
        factor = self.ghost_factor if ghost else COURANT
        ex, ey, ez = e[0, at, own], e[1, at, own], e[2, at, own]
        h[0, at, own] = h[0, at, own] - factor * ((e[2, at, up] - ez) - (e[1, at + 1, own] - ey))
        h[1, at, own] = h[1, at, own] - factor * ((e[0, at + 1, own] - ex) - self.fore_x(ez))
        h[2, at, own] = h[2, at, own] - factor * (self.fore_x(ey) - (e[0, at, up] - ex))

    def step_e(self, z):
        e, h, own, down = self.e, self.h, self.own, self.last_row
        at = self.first_plane + z
        hx, hy, hz = h[0, at, own], h[1, at, own], h[2, at, own]
        keep, drive = self.coefs[0, at], self.coefs[1, at]
        e[0, at, own] = keep * e[0, at, own] + drive * (
            (hz - h[2, at, down]) - (hy - h[1, at - 1, own])
        )
        e[1, at, own] = keep * e[1, at, own] + drive * (
            (hx - h[0, at - 1, own]) - self.back_x(hz)
        )
        e[2, at, own] = keep * e[2, at, own] + drive * (self.back_x(hy) - (hx - h[0, at, down]))


def material_tables(tables, width):
    loss = [jnp.full((1, width), tables[1, k], jnp.float32) for k in range(tables.shape[1])]
    permit = [jnp.full((1, width), tables[0, k], jnp.float32) for k in range(tables.shape[1])]
    keeps = [(1.0 - x) / (1.0 + x) for x in loss]
    drives = [COURANT / (p * (1.0 + x)) for p, x in zip(permit, loss)]
    return keeps, drives


def look_up(values, which):
    total = jnp.broadcast_to(values[0], which.shape)
    for k in range(1, len(values)):
        total = jnp.where(which == k, values[k], total)
    return total


def monitor_info(info, m, monitors):
    return info[4 + m], info[4 + monitors + m], info[4 + 2 * monitors + m]


def take_sample(e, c, spot, start, extent, rows):
    height, width = e.shape[2] - 2 * PAD, e.shape[3]
    plane = pltpu.roll(e[c, spot, pl.ds(PAD, height)], height - start, 0)[:rows]
    return jnp.where(lax.broadcasted_iota(jnp.int32, (rows, width), 0) < extent, plane, 0.0)


def inner_kernel(d, first, depth, monitors, rows, info, *refs):
    if first:
        tables, e_in, h_in, m_in, *refs = refs
    else:
        e_in, h_in, coefs_in, *refs = refs
    e_out, h_out, mine_out, other_out, edge_out, *refs = refs
    if first:
        coefs_out, e, h, coefs, m_buf, sem = refs
    else:
        e, h, coefs, sem = refs
    height, width = e_in.shape[2:]
    g = 1
    own, inside = pl.ds(g, depth), pl.ds(PAD, height)
    fields = ((e_in, e), (h_in, h))
    moves = [(x_in.at[c], x.at[c, own, inside]) for x_in, x in fields for c in range(3)]
    if first:
        moves.append((m_in, m_buf))
    else:
        moves += [(coefs_in.at[k], coefs.at[k, own]) for k in range(2)]
    copies = start_all(moves, sem)
    yee = Yee(e, h, coefs, height, width, g, None)
    if first:
        copies.pop().wait()
        keeps, drives = material_tables(tables, width)

        def fill(z, _):
            which = m_buf[z]
            coefs[0, g + z] = look_up(keeps, which)
            coefs[1, g + z] = look_up(drives, which)
            return 0

        lax.fori_loop(0, depth, fill, 0)
    for copy in copies:
        copy.wait()

    mine, other = info[0], 1 - info[0]
    group = 4
    for s in range(1, d + 1):
        low, high = s, depth - s
        yee.step_h(low - 1)

        def chunk(base, planes):
            for u in range(planes):
                yee.step_h(base + u)
            for u in range(planes):
                yee.step_e(base + u)

        whole = (high - low) // group

        def body(k, _):
            chunk(low + group * k, group)
            return 0

        lax.fori_loop(0, whole, body, 0)
        if low + group * whole < high:
            chunk(low + group * whole, high - low - group * whole)
        for m in range(monitors):
            offset, start, extent = monitor_info(info, m, monitors)
            held = jnp.logical_and(offset >= low, offset < high)
            taken = jnp.where(held, extent, 0)
            spot = g + jnp.clip(offset, 0, depth - 1)
            mine_out[m, s - 1] = take_sample(e, mine, spot, start, taken, rows)
            other_out[m, s - 1] = take_sample(e, other, spot, start, taken, rows)

    moves = []
    for k, (x, x_out) in enumerate(((e, e_out), (h, h_out))):
        moves.append((x.at[:, pl.ds(g, d), inside], edge_out.at[k, :, pl.ds(0, d)]))
        moves.append(
            (x.at[:, pl.ds(g + depth - 1 - d, d + 1), inside], edge_out.at[k, :, pl.ds(d, d + 1)])
        )
        moves += [(x.at[c, own, inside], x_out.at[c]) for c in range(3)]
    if first:
        moves += [(coefs.at[k, own], coefs_out.at[k]) for k in range(2)]
    for copy in start_all(moves, sem):
        copy.wait()


def edge_kernel(d, nxt, first, depth, monitors, rows, info, *refs):
    edge_in, coefs_in, mine_in, other_in, far_in, near_in, *refs = refs
    mats = GHOST - 1
    if first:
        tables, *refs = refs
    else:
        ghosts_in, below_in, _, *refs = refs
    if nxt:
        _, _, e_out, h_out, mine_out, other_out, below_out, far_out, near_out, *refs = refs
        if first:
            ghosts_out, *refs = refs
    else:
        fresh_out, mine_out, other_out, _, *refs = refs
    e, h, coefs, sem = refs
    height, width = edge_in.shape[3:]
    g = GHOST
    inside = pl.ds(PAD, height)
    even = info[0] == 0
    below, above = info[1], info[2]

    moves = []
    for k, x in enumerate((e, h)):
        for source, planes, at in ((0, d, 0), (d, d + 1, depth - 1 - d)):
            moves.append(
                (edge_in.at[k, :, pl.ds(source, planes)], x.at[:, pl.ds(g + at, planes), inside])
            )
    for plane in (0, depth - d):
        moves.append((coefs_in.at[:, pl.ds(plane, d)], coefs.at[:, pl.ds(g + plane, d)]))
    if not first:
        moves.append((below_in, h.at[:, g - 1, inside]))
    copies = start_all(moves, sem)
    yee = Yee(e, h, coefs, height, width, g, below)

    sides = (
        (-depth, up_pieces(d, mats if first else 0, depth, first)),
        (depth, down_pieces(d, mats if first else 0)),
    )

    def unpack(below_ref, above_ref):
        for (shift, pieces), source in zip(sides, (below_ref, above_ref)):
            for name, c, plane, planes, at in spots(pieces):
                where = pl.ds(g + plane + shift, planes)
                value = source[pl.ds(at * height, planes * height)]
                value = value.reshape(planes, height, width)
                if name == "e":
                    e[c, where, inside] = value
                elif name == "h":
                    h[c, where, inside] = value
                else:
                    coefs[0, where] = value

    @pl.when(even)
    def _():
        unpack(far_in, near_in)

    @pl.when(jnp.logical_not(even))
    def _():
        unpack(near_in, far_in)

    ghost_planes = list(range(g - mats, g)) + list(range(g + depth, g + depth + mats))
    if first:
        keeps, drives = material_tables(tables, width)
        for at in ghost_planes:
            alive = (below if at < g else above).astype(jnp.float32)
            which = coefs[0, at].astype(jnp.int32)
            coefs[0, at] = look_up(keeps, which) * alive
            coefs[1, at] = look_up(drives, which) * alive
        if nxt:
            for k, at in enumerate(ghost_planes):
                ghosts_out[:, k] = coefs[:, at]
    else:
        for k, at in enumerate(ghost_planes):
            coefs[:, at] = ghosts_in[:, k]
    for copy in copies:
        copy.wait()

    mine, other = info[0], 1 - info[0]
    for s in range(1, d + 1):
        lower = list(range(s - d, s))
        upper = list(range(depth - s, depth + d - s))
        for z in lower:
            yee.step_h(z - 1, z - 1 < 0)
        for z in upper:
            yee.step_h(z)
        for z in lower + upper:
            yee.step_e(z)
        for m in range(monitors):
            offset, start, extent = monitor_info(info, m, monitors)
            held = jnp.logical_or(
                jnp.logical_and(offset >= 0, offset < s),
                jnp.logical_and(offset >= depth - s, offset < depth),
            )
            spot = g + jnp.clip(offset, 0, depth - 1)
            mine_out[m, s - 1] = jnp.where(
                held, take_sample(e, mine, spot, start, extent, rows), mine_in[m, s - 1]
            )
            fresh = jnp.where(
                held, take_sample(e, other, spot, start, extent, rows), other_in[m, s - 1]
            )
            other_out[m, s - 1] = fresh

    moves = []
    for k, x in enumerate((e, h)):
        for j, plane in enumerate((0, depth - d)):
            source = x.at[:, pl.ds(g + plane, d), inside]
            if nxt:
                moves.append((source, (e_out, h_out)[k].at[:, pl.ds(plane, d)]))
            else:
                moves.append((source, fresh_out.at[k, :, pl.ds(j * d, d)]))
    if nxt:
        moves.append((h.at[:, g - 1, inside], below_out))
    copies = start_all(moves, sem)
    if nxt:

        def pack(down_ref, up_ref):
            for pieces, out in (
                (down_pieces(nxt, 0), down_ref),
                (up_pieces(nxt, 0, depth, False), up_ref),
            ):
                for name, c, plane, planes, at in spots(pieces):
                    source = e if name == "e" else h
                    value = source[c, pl.ds(g + plane, planes), inside]
                    out[pl.ds(at * height, planes * height)] = value.reshape(-1, width)

        @pl.when(even)
        def _():
            pack(far_out, near_out)

        @pl.when(jnp.logical_not(even))
        def _():
            pack(near_out, far_out)

    for copy in copies:
        copy.wait()


def spectrum_kernel(side, chunks, monitors, freqs, info, table, *refs):
    samples, (blocks, sem) = refs[: len(chunks)], refs[-2:]
    if side == 0:
        fresh, _, _, out, *state = refs[len(chunks) : -2]
        edge = fresh.shape[2] // 2
        moves = []
        for k, x_out in enumerate(state):
            for j, plane in enumerate((0, x_out.shape[1] - edge)):
                moves.append(
                    (fresh.at[k, :, pl.ds(j * edge, edge)], x_out.at[:, pl.ds(plane, edge)])
                )
        copies = start_all(moves, sem)
    else:
        out = refs[-3]
        copies = []
    rows, width = samples[0].shape[2:]
    steps = sum(chunks)
    blocks[...] = jnp.zeros(blocks.shape, jnp.float32)
    c = info[0] if side == 0 else 1 - info[0]

    def copy(f):
        return pltpu.make_async_copy(blocks.at[f], out.at[f, :, :, c], sem.at[4 + f])

    def body(f, _):
        for m in range(monitors):
            start = monitor_info(info, m, monitors)[1]
            at = jnp.bitwise_xor(m, info[3])
            planes = [chunk[at, t] for chunk, d in zip(samples, chunks) for t in range(d)]
            for part in range(2):
                total = planes[0] * table[f, part * steps]
                for t in range(1, steps):
                    total = total + planes[t] * table[f, part * steps + t]
                blocks[f, part, m, pl.ds(start, rows)] = total
        copy(f).start()
        return 0

    lax.fori_loop(0, freqs, body, 0)
    for f in range(freqs):
        copy(f).wait()
    for move in copies:
        move.wait()


class Sharing:
    def __init__(self, slabs, rows_when):
        self.slabs, self.rows_when = slabs, rows_when
        me = lax.axis_index("slab")
        self.quarter = 2 * (me // 4 % 2) + me // 8 % 2
        self.half = me // 2 % 2
        self.others = [2**k for k in range(1, slabs.bit_length() - 1)]
        self.others = [k for k in self.others if k not in ((4, 8) if not rows_when else (2, 4, 8))]

    def swap(self, block, stride):
        return lax.ppermute(block, "slab", [(i, i ^ stride) for i in range(self.slabs)])

    def halve(self, total, axis):
        sent = lax.dynamic_index_in_dim(total, 1 - self.half, axis, keepdims=False)
        kept = lax.dynamic_index_in_dim(total, self.half, axis, keepdims=False)
        return kept + self.swap(sent, 2)

    def scatter(self, total):
        if self.rows_when:
            total = total.reshape(total.shape[0], 2, -1, total.shape[-1])
        if self.rows_when == "before":
            total = self.halve(total, 1)
        pieces = [
            lax.dynamic_index_in_dim(total, self.quarter ^ x, 0, keepdims=False)
            for x in range(4)
        ]
        part = pieces[0]
        for x, stride in ((1, 8), (2, 4), (3, 12)):
            part = part + self.swap(pieces[x], stride)
        if self.rows_when == "after":
            part = self.halve(part, 0)
        for stride in self.others:
            part = part + self.swap(part, stride)
        return part

    def gather(self, part, shape):
        total = jnp.stack([part] + [self.swap(part, stride) for stride in (8, 4, 12)])
        if self.rows_when:
            theirs = self.swap(total, 2)
            first = self.half == 0
            total = jnp.stack(
                [jnp.where(first, total, theirs), jnp.where(first, theirs, total)], 1
            )
        return total.reshape(shape)


def per_device(
    slabs, e_start, h_start, material, mat_permit, mat_loss, monitor_z, monitor_span, freq_bins
):
    depth, height, width = e_start.shape[1:]
    monitors = monitor_z.shape[0]
    freqs = freq_bins.shape[0]
    rows = 3 * height // 4
    mats = GHOST - 1
    me = lax.axis_index("slab")
    info = jnp.concatenate(
        [
            jnp.stack(
                [
                    me % 2,
                    (me > 0).astype(jnp.int32),
                    (me < slabs - 1).astype(jnp.int32),
                    2 * (me // 4 % 2) + me // 8 % 2,
                ]
            ),
            monitor_z - me * depth,
            monitor_span[:, 0],
            monitor_span[:, 1] - monitor_span[:, 0],
        ]
    ).astype(jnp.int32)
    tables = jnp.stack([mat_permit, mat_loss])
    moments = jnp.arange(1, STEPS + 1, dtype=jnp.int32)
    phase_turns = freq_bins[:, None] * moments[None, :] % PERIOD
    angles = phase_turns.astype(jnp.float32) * jnp.float32(2.0 * math.pi / PERIOD)
    phase_table = jnp.concatenate([jnp.cos(angles), -jnp.sin(angles)], 1)

    far_pairs = []
    for i in range(1, slabs - 1, 2):
        far_pairs += [(i, i + 1), (i + 1, i)]
    near_pairs = [(i, i ^ 1) for i in range(slabs)]

    def near_swap(block):
        return lax.ppermute(block, "slab", near_pairs)

    def f32(*shape):
        return jax.ShapeDtypeStruct(shape, jnp.float32)

    def vmem(*shape):
        return pltpu.VMEM(shape, jnp.float32)

    def in_hbm(*arrays):
        return [pltpu.with_memory_space_constraint(x, pltpu.HBM) for x in arrays]

    def in_vmem(*arrays):
        return [pltpu.with_memory_space_constraint(x, pltpu.VMEM) for x in arrays]

    def scratch(ghosts):
        planes = depth + 2 * ghosts
        padded = (3, planes, height + 2 * PAD, width)
        return [pltpu.VMEM(padded, jnp.float32)] * 2 + [
            pltpu.VMEM((2, planes, height, width), jnp.float32)
        ]

    d = ROUNDS[0]
    size = message_size(d, mats, depth, True)
    copies = sum(1 for _ in spots(down_pieces(d, mats))) + sum(
        1 for _ in spots(up_pieces(d, mats, depth, True))
    )
    with jax.named_scope("first_pack"):
        far, near = pl.pallas_call(
            functools.partial(first_pack_kernel, d, mats, depth),
            out_shape=[vmem(size, height, width)] * 2,
            in_specs=[HBM] * 3,
            out_specs=[VMEM] * 2,
            scratch_shapes=[
                pltpu.VMEM((2, mats, height, width), jnp.int32),
                pltpu.SemaphoreType.DMA((copies,)),
            ],
            compiler_params=params(),
            cost_estimate=cost(2),
        )(*in_hbm(e_start, h_start, material))
    far, near = far.reshape(-1, width), near.reshape(-1, width)

    state = [f32(*e_start.shape), f32(*h_start.shape)]
    e, h = e_start, h_start
    coefs = ghosts = below = fresh = None
    mine = None
    for k, d in enumerate(ROUNDS):
        first = k == 0
        nxt = ROUNDS[k + 1] if k + 1 < len(ROUNDS) else 0
        far = lax.ppermute(far, "slab", far_pairs)
        near = near_swap(near)
        if not first:
            before = mine + near_swap(other)
        samples = [vmem(monitors, d, rows, width)] * 2
        edge = vmem(2, 3, 2 * d + 1, height, width)
        with jax.named_scope(f"inner{k}"):
            kernel = functools.partial(inner_kernel, d, first, depth, monitors, rows)
            if first:
                e, h, mine, other, edge, coefs = pl.pallas_call(
                    kernel,
                    out_shape=state + samples + [edge, vmem(2, depth, height, width)],
                    in_specs=[SMEM, SMEM, HBM, HBM, HBM],
                    out_specs=[HBM] * 2 + [VMEM] * 3 + [ANY],
                    scratch_shapes=scratch(1)
                    + [
                        pltpu.VMEM((depth, height, width), jnp.int32),
                        pltpu.SemaphoreType.DMA((12,)),
                    ],
                    compiler_params=params(),
                    cost_estimate=cost(5),
                )(info, tables, *in_hbm(e, h, material))
            else:
                e, h, mine, other, edge = pl.pallas_call(
                    kernel,
                    out_shape=state + samples + [edge],
                    in_specs=[SMEM, HBM, HBM, ANY],
                    out_specs=[HBM] * 2 + [VMEM] * 3,
                    input_output_aliases={1: 0, 2: 1},
                    scratch_shapes=scratch(1) + [pltpu.SemaphoreType.DMA((12,))],
                    compiler_params=params(),
                    cost_estimate=cost(5),
                )(info, *in_hbm(e, h), *in_vmem(coefs))
        operands = [info, *in_vmem(edge, coefs, mine, other, far, near)]
        specs = [SMEM, VMEM, ANY] + [VMEM] * 4
        if first:
            operands += [tables]
            specs += [SMEM]
        else:
            operands += in_vmem(ghosts, below, before)
            specs += [VMEM, VMEM, ANY]
        outs = [vmem(2, 3, 2 * d, height, width)] + samples
        kinds = [VMEM] * 3
        aliases = {}
        if not first:
            aliases = {len(operands) - 1: 3}
            outs += [vmem(*before.shape)]
            kinds += [ANY]
        if nxt:
            outs = state + samples
            kinds = [HBM] * 2 + [VMEM] * 2
            aliases = {len(operands): 0, len(operands) + 1: 1}
            operands += [e, h]
            specs += [HBM] * 2
            size = message_size(nxt, 0, depth, False) * height
            outs += [vmem(3, height, width), vmem(size, width), vmem(size, width)]
            kinds += [VMEM]
            if first:
                outs += [vmem(2, 2 * mats, height, width)]
        with jax.named_scope(f"edge{k}"):
            results = pl.pallas_call(
                functools.partial(edge_kernel, d, nxt, first, depth, monitors, rows),
                out_shape=outs,
                in_specs=specs,
                out_specs=kinds + [VMEM] * (len(outs) - len(kinds)),
                input_output_aliases=aliases,
                scratch_shapes=scratch(GHOST) + [pltpu.SemaphoreType.DMA((8,))],
                compiler_params=params(),
                cost_estimate=cost(4),
            )(*operands)
        if nxt:
            e, h, mine, other, below, far, near = results[:7]
            if first:
                ghosts = results[7]
        else:
            fresh, mine, other, before = results
            early = Sharing(slabs, ROWS_WHEN[k - 1])
            part = early.scatter(before)
    late = Sharing(slabs, ROWS_WHEN[-1])
    total = mine + near_swap(other)
    sums = []
    for sharing, block in ((early, part), (late, late.scatter(total))):
        sums.append(sharing.gather(block, total.shape))
    spectrum = []
    for side, chunks in enumerate((sums, [near_swap(block) for block in sums])):
        operands = [info, phase_table, *in_vmem(*chunks)]
        if side == 0:
            operands += in_vmem(fresh) + in_hbm(e, h)
        else:
            operands += in_hbm(*spectrum)
        last = len(operands)
        with jax.named_scope(f"spectrum{side}"):
            results = pl.pallas_call(
                functools.partial(spectrum_kernel, side, ROUNDS, monitors, freqs),
                out_shape=[f32(freqs, 2, monitors, 2, height, width)] + state * (1 - side),
                in_specs=[SMEM, SMEM]
                + [VMEM] * (len(chunks) + 1 - side)
                + [HBM] * (2 - side),
                out_specs=[HBM] * (3 - 2 * side),
                input_output_aliases={last - 1: 0} if side else {last - 2: 1, last - 1: 2},
                scratch_shapes=[
                    pltpu.VMEM((freqs, 2, monitors, height, width), jnp.float32),
                    pltpu.SemaphoreType.DMA((4 + freqs,)),
                ],
                compiler_params=params(),
                cost_estimate=cost(2),
            )(*operands)
        spectrum = results[:1]
        if side == 0:
            e, h = results[1:]
    (spectrum,) = spectrum
    return e, h, spectrum


def solution(mesh):
    slabs = mesh.shape["slab"]
    in_specs = (
        P(None, ("design", "slab"), None, None),
        P(None, ("design", "slab"), None, None),
        P(("design", "slab"), None, None),
        P(),
        P(),
        P(),
        P(),
        P("slab"),
    )
    out_specs = (
        P(None, ("design", "slab"), None, None),
        P(None, ("design", "slab"), None, None),
        P(("design", "slab"), None, None, None, None, None),
    )
    return jax.shard_map(
        functools.partial(per_device, slabs),
        mesh=mesh,
        in_specs=in_specs,
        out_specs=out_specs,
        check_vma=False,
    )
```

```python
import functools
import math

import jax
import jax.numpy as jnp
from jax import lax
from jax.experimental import pallas as pl
from jax.experimental.pallas import tpu as pltpu
from jax.sharding import PartitionSpec as P

STEPS = 8
PERIOD = 512
ROUNDS = (4, 4)
ROWS_WHEN = ("", "before")
GHOST = max(ROUNDS)
COURANT = 0.5
VMEM = pl.BlockSpec(memory_space=pltpu.VMEM)
SMEM = pl.BlockSpec(memory_space=pltpu.SMEM)
ANY = pl.BlockSpec(memory_space=pl.ANY)
HBM = pl.BlockSpec(memory_space=pltpu.HBM)
LIMIT = 12 * 1024 * 1024
PAD = 8


def params(limit=LIMIT):
    return pltpu.CompilerParams(vmem_limit_bytes=limit)


def cost(microseconds):
    return pl.CostEstimate(
        flops=0, bytes_accessed=int(microseconds * 3.0e6), transcendentals=0
    )


def down_pieces(d, mats):
    pieces = [("e", 0, 2, 0, d)]
    if d > 1:
        pieces += [("e", 2, 1, 0, d - 1), ("h", 0, 3, 0, d - 1)]
    if mats:
        pieces += [("m", 0, 1, 0, mats)]
    return pieces


def up_pieces(d, mats, depth, first):
    pieces = [("e", 0, 3, depth - d, d)]
    if first:
        pieces += [("h", 0, 2, depth - d, d)]
        if d > 1:
            pieces += [("h", 2, 1, depth - d + 1, d - 1)]
    else:
        if d > 1:
            pieces += [("h", 0, 2, depth - d, d - 1)]
        if d > 2:
            pieces += [("h", 2, 1, depth - d + 1, d - 2)]
    if mats:
        pieces += [("m", 0, 1, depth - mats, mats)]
    return pieces


def size_of(pieces):
    return sum(p[2] * p[4] for p in pieces)


def message_size(d, mats, depth, first):
    return max(size_of(down_pieces(d, mats)), size_of(up_pieces(d, mats, depth, first)))


def spots(pieces):
    at = 0
    for name, comp, comps, plane, planes in pieces:
        for c in range(comp, comp + comps):
            yield name, c, plane, planes, at
            at += planes


def start_all(pairs, sem):
    copies = [pltpu.make_async_copy(a, b, sem.at[k]) for k, (a, b) in enumerate(pairs)]
    for copy in copies:
        copy.start()
    return copies


def first_pack_kernel(d, mats, depth, e_ref, h_ref, m_ref, far_ref, near_ref, m_in, sem):
    even = lax.rem(lax.axis_index("slab"), 2) == 0

    def pack(down_ref, up_ref):
        sides = (
            (down_pieces(d, mats), down_ref),
            (up_pieces(d, mats, depth, True), up_ref),
        )
        moves, mats_at = [], []
        for k, (pieces, out) in enumerate(sides):
            for name, c, plane, planes, at in spots(pieces):
                if name == "m":
                    moves.append((m_ref.at[pl.ds(plane, planes)], m_in.at[k]))
                    mats_at.append((k, out, at))
                else:
                    source = e_ref if name == "e" else h_ref
                    moves.append((source.at[c, pl.ds(plane, planes)], out.at[pl.ds(at, planes)]))
        for copy in start_all(moves, sem):
            copy.wait()
        for k, out, at in mats_at:
            out[pl.ds(at, mats)] = m_in[k].astype(jnp.float32)

    @pl.when(even)
    def _():
        pack(far_ref, near_ref)

    @pl.when(jnp.logical_not(even))
    def _():
        pack(near_ref, far_ref)


class Yee:
    def __init__(self, e, h, coefs, height, width, first_plane, below):
        self.e, self.h, self.coefs = e, h, coefs
        self.first_plane, self.width = first_plane, width
        self.own = pl.ds(PAD, height)
        self.next_row, self.last_row = pl.ds(PAD + 1, height), pl.ds(PAD - 1, height)
        lane = lax.broadcasted_iota(jnp.int32, (height, width), 1)
        self.lane_last, self.lane_first = lane == width - 1, lane == 0
        self.ghost_factor = None if below is None else COURANT * below.astype(jnp.float32)
        planes = e.shape[1]
        e[:, :, pl.ds(PAD + height, PAD)] = jnp.zeros((3, planes, PAD, width), jnp.float32)
        h[:, :, pl.ds(0, PAD)] = jnp.zeros((3, planes, PAD, width), jnp.float32)

    def fore_x(self, v):
        return jnp.where(self.lane_last, 0.0, pltpu.roll(v, self.width - 1, 1)) - v

    def back_x(self, v):
        return v - jnp.where(self.lane_first, 0.0, pltpu.roll(v, 1, 1))

    def step_h(self, z, ghost=False):
        e, h, own, up = self.e, self.h, self.own, self.next_row
        at = self.first_plane + z
        factor = self.ghost_factor if ghost else COURANT
        ex, ey, ez = e[0, at, own], e[1, at, own], e[2, at, own]
        h[0, at, own] = h[0, at, own] - factor * ((e[2, at, up] - ez) - (e[1, at + 1, own] - ey))
        h[1, at, own] = h[1, at, own] - factor * ((e[0, at + 1, own] - ex) - self.fore_x(ez))
        h[2, at, own] = h[2, at, own] - factor * (self.fore_x(ey) - (e[0, at, up] - ex))

    def step_e(self, z):
        e, h, own, down = self.e, self.h, self.own, self.last_row
        at = self.first_plane + z
        hx, hy, hz = h[0, at, own], h[1, at, own], h[2, at, own]
        keep, drive = self.coefs[0, at], self.coefs[1, at]
        e[0, at, own] = keep * e[0, at, own] + drive * (
            (hz - h[2, at, down]) - (hy - h[1, at - 1, own])
        )
        e[1, at, own] = keep * e[1, at, own] + drive * (
            (hx - h[0, at - 1, own]) - self.back_x(hz)
        )
        e[2, at, own] = keep * e[2, at, own] + drive * (self.back_x(hy) - (hx - h[0, at, down]))


def material_tables(tables, width):
    loss = [jnp.full((1, width), tables[1, k], jnp.float32) for k in range(tables.shape[1])]
    permit = [jnp.full((1, width), tables[0, k], jnp.float32) for k in range(tables.shape[1])]
    keeps = [(1.0 - x) / (1.0 + x) for x in loss]
    drives = [COURANT / (p * (1.0 + x)) for p, x in zip(permit, loss)]
    return keeps, drives


def look_up(values, which):
    total = jnp.broadcast_to(values[0], which.shape)
    for k in range(1, len(values)):
        total = jnp.where(which == k, values[k], total)
    return total


def monitor_info(info, m, monitors):
    return info[4 + m], info[4 + monitors + m], info[4 + 2 * monitors + m]


def take_sample(e, c, spot, start, extent, rows):
    height, width = e.shape[2] - 2 * PAD, e.shape[3]
    plane = pltpu.roll(e[c, spot, pl.ds(PAD, height)], height - start, 0)[:rows]
    return jnp.where(lax.broadcasted_iota(jnp.int32, (rows, width), 0) < extent, plane, 0.0)


def inner_kernel(d, first, depth, monitors, rows, info, *refs):
    if first:
        tables, e_in, h_in, m_in, *refs = refs
    else:
        e_in, h_in, coefs_in, *refs = refs
    e_out, h_out, mine_out, other_out, edge_out, *refs = refs
    if first:
        coefs_out, e, h, coefs, m_buf, sem = refs
    else:
        e, h, coefs, sem = refs
    height, width = e_in.shape[2:]
    g = 1
    own, inside = pl.ds(g, depth), pl.ds(PAD, height)
    fields = ((e_in, e), (h_in, h))
    moves = [(x_in.at[c], x.at[c, own, inside]) for x_in, x in fields for c in range(3)]
    if first:
        moves.append((m_in, m_buf))
    else:
        moves += [(coefs_in.at[k], coefs.at[k, own]) for k in range(2)]
    copies = start_all(moves, sem)
    yee = Yee(e, h, coefs, height, width, g, None)
    if first:
        copies.pop().wait()
        keeps, drives = material_tables(tables, width)

        def fill(z, _):
            which = m_buf[z]
            coefs[0, g + z] = look_up(keeps, which)
            coefs[1, g + z] = look_up(drives, which)
            return 0

        lax.fori_loop(0, depth, fill, 0)
    for copy in copies:
        copy.wait()

    mine, other = info[0], 1 - info[0]
    group = 4
    for s in range(1, d + 1):
        low, high = s, depth - s
        yee.step_h(low - 1)

        def chunk(base, planes):
            for u in range(planes):
                yee.step_h(base + u)
            for u in range(planes):
                yee.step_e(base + u)

        whole = (high - low) // group

        def body(k, _):
            chunk(low + group * k, group)
            return 0

        lax.fori_loop(0, whole, body, 0)
        if low + group * whole < high:
            chunk(low + group * whole, high - low - group * whole)
        for m in range(monitors):
            offset, start, extent = monitor_info(info, m, monitors)
            held = jnp.logical_and(offset >= low, offset < high)
            taken = jnp.where(held, extent, 0)
            spot = g + jnp.clip(offset, 0, depth - 1)
            mine_out[m, s - 1] = take_sample(e, mine, spot, start, taken, rows)
            other_out[m, s - 1] = take_sample(e, other, spot, start, taken, rows)

    moves = []
    for k, (x, x_out) in enumerate(((e, e_out), (h, h_out))):
        moves += [(x.at[c, own, inside], x_out.at[c]) for c in range(3)]
    copies = start_all(moves, sem)
    for k, x in enumerate((e, h)):
        for c in range(3):
            edge_out[k, c, pl.ds(0, d)] = x[c, pl.ds(g, d), inside]
            edge_out[k, c, pl.ds(d, d + 1)] = x[c, pl.ds(g + depth - 1 - d, d + 1), inside]
    if first:
        for k in range(2):
            coefs_out[k] = coefs[k, own]
    for copy in copies:
        copy.wait()


def edge_kernel(d, nxt, first, depth, monitors, rows, info, *refs):
    edge_in, coefs_in, mine_in, other_in, far_in, near_in, *refs = refs
    mats = GHOST - 1
    if first:
        tables, *refs = refs
    else:
        ghosts_in, below_in, _, *refs = refs
    if nxt:
        _, _, e_out, h_out, mine_out, other_out, below_out, far_out, near_out, *refs = refs
        if first:
            ghosts_out, *refs = refs
    else:
        fresh_out, mine_out, other_out, _, *refs = refs
    e, h, coefs, sem = refs
    height, width = edge_in.shape[3:]
    g = GHOST
    inside = pl.ds(PAD, height)
    even = info[0] == 0
    below, above = info[1], info[2]

    yee = Yee(e, h, coefs, height, width, g, below)
    for k, x in enumerate((e, h)):
        for source, planes, at in ((0, d, 0), (d, d + 1, depth - 1 - d)):
            for c in range(3):
                part = edge_in[k, c, pl.ds(source, planes)]
                x[c, pl.ds(g + at, planes), inside] = part
    for plane in (0, depth - d):
        for k in range(2):
            coefs[k, pl.ds(g + plane, d)] = coefs_in[k, pl.ds(plane, d)]
    if not first:
        h[:, g - 1, inside] = below_in[...]

    sides = (
        (-depth, up_pieces(d, mats if first else 0, depth, first)),
        (depth, down_pieces(d, mats if first else 0)),
    )

    def unpack(below_ref, above_ref):
        for (shift, pieces), source in zip(sides, (below_ref, above_ref)):
            for name, c, plane, planes, at in spots(pieces):
                where = pl.ds(g + plane + shift, planes)
                value = source[pl.ds(at * height, planes * height)]
                value = value.reshape(planes, height, width)
                if name == "e":
                    e[c, where, inside] = value
                elif name == "h":
                    h[c, where, inside] = value
                else:
                    coefs[0, where] = value

    @pl.when(even)
    def _():
        unpack(far_in, near_in)

    @pl.when(jnp.logical_not(even))
    def _():
        unpack(near_in, far_in)

    ghost_planes = list(range(g - mats, g)) + list(range(g + depth, g + depth + mats))
    if first:
        keeps, drives = material_tables(tables, width)
        for at in ghost_planes:
            alive = (below if at < g else above).astype(jnp.float32)
            which = coefs[0, at].astype(jnp.int32)
            coefs[0, at] = look_up(keeps, which) * alive
            coefs[1, at] = look_up(drives, which) * alive
        if nxt:
            for k, at in enumerate(ghost_planes):
                ghosts_out[:, k] = coefs[:, at]
    else:
        for k, at in enumerate(ghost_planes):
            coefs[:, at] = ghosts_in[:, k]

    mine, other = info[0], 1 - info[0]
    for s in range(1, d + 1):
        lower = list(range(s - d, s))
        upper = list(range(depth - s, depth + d - s))
        for z in lower:
            yee.step_h(z - 1, z - 1 < 0)
        for z in upper:
            yee.step_h(z)
        for z in lower + upper:
            yee.step_e(z)
        for m in range(monitors):
            offset, start, extent = monitor_info(info, m, monitors)
            held = jnp.logical_or(
                jnp.logical_and(offset >= 0, offset < s),
                jnp.logical_and(offset >= depth - s, offset < depth),
            )
            spot = g + jnp.clip(offset, 0, depth - 1)
            mine_out[m, s - 1] = jnp.where(
                held, take_sample(e, mine, spot, start, extent, rows), mine_in[m, s - 1]
            )
            fresh = jnp.where(
                held, take_sample(e, other, spot, start, extent, rows), other_in[m, s - 1]
            )
            other_out[m, s - 1] = fresh

    copies = []
    if nxt:
        moves = []
        for x, x_out in ((e, e_out), (h, h_out)):
            for plane in (0, depth - d):
                source = x.at[:, pl.ds(g + plane, d), inside]
                moves.append((source, x_out.at[:, pl.ds(plane, d)]))
        copies = start_all(moves, sem)
    else:
        for k, x in enumerate((e, h)):
            for j, plane in enumerate((0, depth - d)):
                for c in range(3):
                    part = x[c, pl.ds(g + plane, d), inside]
                    fresh_out[k, c, pl.ds(j * d, d)] = part
    if nxt:
        below_out[...] = h[:, g - 1, inside]

        def pack(down_ref, up_ref):
            for pieces, out in (
                (down_pieces(nxt, 0), down_ref),
                (up_pieces(nxt, 0, depth, False), up_ref),
            ):
                for name, c, plane, planes, at in spots(pieces):
                    source = e if name == "e" else h
                    value = source[c, pl.ds(g + plane, planes), inside]
                    out[pl.ds(at * height, planes * height)] = value.reshape(-1, width)

        @pl.when(even)
        def _():
            pack(far_out, near_out)

        @pl.when(jnp.logical_not(even))
        def _():
            pack(near_out, far_out)

    for copy in copies:
        copy.wait()


def spectrum_kernel(side, chunks, monitors, freqs, info, table, *refs):
    samples, (blocks, sem) = refs[: len(chunks)], refs[-2:]
    if side == 0:
        fresh, _, _, out, *state = refs[len(chunks) : -2]
        edge = fresh.shape[2] // 2
        moves = []
        for k, x_out in enumerate(state):
            for j, plane in enumerate((0, x_out.shape[1] - edge)):
                moves.append(
                    (fresh.at[k, :, pl.ds(j * edge, edge)], x_out.at[:, pl.ds(plane, edge)])
                )
        copies = start_all(moves, sem)
    else:
        out = refs[-3]
        copies = []
    rows, width = samples[0].shape[2:]
    steps = sum(chunks)
    c = info[0] if side == 0 else 1 - info[0]

    def copy(f):
        return pltpu.make_async_copy(blocks.at[f], out.at[f, :, :, c], sem.at[4 + f])

    def body(f, _):
        for m in range(monitors):
            start = monitor_info(info, m, monitors)[1]
            at = jnp.bitwise_xor(m, info[3])
            planes = [chunk[at, t] for chunk, d in zip(samples, chunks) for t in range(d)]
            for part in range(2):
                total = planes[0] * table[f, part * steps]
                for t in range(1, steps):
                    total = total + planes[t] * table[f, part * steps + t]
                blocks[f, part, m, pl.ds(0, (blocks.shape[3] - rows))] = jnp.zeros(((blocks.shape[3] - rows), width), jnp.float32)
                blocks[f, part, m, pl.ds(rows, (blocks.shape[3] - rows))] = jnp.zeros(((blocks.shape[3] - rows), width), jnp.float32)
                blocks[f, part, m, pl.ds(start, rows)] = total
        copy(f).start()
        return 0

    lax.fori_loop(0, freqs, body, 0)
    for f in range(freqs):
        copy(f).wait()
    for move in copies:
        move.wait()


class Sharing:
    def __init__(self, slabs, rows_when):
        self.slabs, self.rows_when = slabs, rows_when
        me = lax.axis_index("slab")
        self.quarter = 2 * (me // 4 % 2) + me // 8 % 2
        self.half = me // 2 % 2
        self.others = [2**k for k in range(1, slabs.bit_length() - 1)]
        self.others = [k for k in self.others if k not in ((4, 8) if not rows_when else (2, 4, 8))]

    def swap(self, block, stride):
        return lax.ppermute(block, "slab", [(i, i ^ stride) for i in range(self.slabs)])

    def halve(self, total, axis):
        sent = lax.dynamic_index_in_dim(total, 1 - self.half, axis, keepdims=False)
        kept = lax.dynamic_index_in_dim(total, self.half, axis, keepdims=False)
        return kept + self.swap(sent, 2)

    def scatter(self, total):
        if self.rows_when:
            total = total.reshape(total.shape[0], 2, -1, total.shape[-1])
        if self.rows_when == "before":
            total = self.halve(total, 1)
        pieces = [
            lax.dynamic_index_in_dim(total, self.quarter ^ x, 0, keepdims=False)
            for x in range(4)
        ]
        part = pieces[0]
        for x, stride in ((1, 8), (2, 4), (3, 12)):
            part = part + self.swap(pieces[x], stride)
        if self.rows_when == "after":
            part = self.halve(part, 0)
        for stride in self.others:
            part = part + self.swap(part, stride)
        return part

    def gather(self, part, shape):
        total = jnp.stack([part] + [self.swap(part, stride) for stride in (8, 4, 12)])
        if self.rows_when:
            theirs = self.swap(total, 2)
            first = self.half == 0
            total = jnp.stack(
                [jnp.where(first, total, theirs), jnp.where(first, theirs, total)], 1
            )
        return total.reshape(shape)


def per_device(
    slabs, e_start, h_start, material, mat_permit, mat_loss, monitor_z, monitor_span, freq_bins
):
    depth, height, width = e_start.shape[1:]
    monitors = monitor_z.shape[0]
    freqs = freq_bins.shape[0]
    rows = 3 * height // 4
    mats = GHOST - 1
    me = lax.axis_index("slab")
    info = jnp.concatenate(
        [
            jnp.stack(
                [
                    me % 2,
                    (me > 0).astype(jnp.int32),
                    (me < slabs - 1).astype(jnp.int32),
                    2 * (me // 4 % 2) + me // 8 % 2,
                ]
            ),
            monitor_z - me * depth,
            monitor_span[:, 0],
            monitor_span[:, 1] - monitor_span[:, 0],
        ]
    ).astype(jnp.int32)
    tables = jnp.stack([mat_permit, mat_loss])
    moments = jnp.arange(1, STEPS + 1, dtype=jnp.int32)
    phase_turns = freq_bins[:, None] * moments[None, :] % PERIOD
    angles = phase_turns.astype(jnp.float32) * jnp.float32(2.0 * math.pi / PERIOD)
    phase_table = jnp.concatenate([jnp.cos(angles), -jnp.sin(angles)], 1)

    far_pairs = []
    for i in range(1, slabs - 1, 2):
        far_pairs += [(i, i + 1), (i + 1, i)]
    near_pairs = [(i, i ^ 1) for i in range(slabs)]

    def near_swap(block):
        return lax.ppermute(block, "slab", near_pairs)

    def f32(*shape):
        return jax.ShapeDtypeStruct(shape, jnp.float32)

    def vmem(*shape):
        return pltpu.VMEM(shape, jnp.float32)

    def in_hbm(*arrays):
        return [pltpu.with_memory_space_constraint(x, pltpu.HBM) for x in arrays]

    def in_vmem(*arrays):
        return [pltpu.with_memory_space_constraint(x, pltpu.VMEM) for x in arrays]

    def scratch(ghosts):
        planes = depth + 2 * ghosts
        padded = (3, planes, height + 2 * PAD, width)
        return [pltpu.VMEM(padded, jnp.float32)] * 2 + [
            pltpu.VMEM((2, planes, height, width), jnp.float32)
        ]

    d = ROUNDS[0]
    size = message_size(d, mats, depth, True)
    copies = sum(1 for _ in spots(down_pieces(d, mats))) + sum(
        1 for _ in spots(up_pieces(d, mats, depth, True))
    )
    with jax.named_scope("first_pack"):
        far, near = pl.pallas_call(
            functools.partial(first_pack_kernel, d, mats, depth),
            out_shape=[vmem(size, height, width)] * 2,
            in_specs=[HBM] * 3,
            out_specs=[VMEM] * 2,
            scratch_shapes=[
                pltpu.VMEM((2, mats, height, width), jnp.int32),
                pltpu.SemaphoreType.DMA((copies,)),
            ],
            compiler_params=params(),
            cost_estimate=cost(2),
        )(*in_hbm(e_start, h_start, material))
    far, near = far.reshape(-1, width), near.reshape(-1, width)

    state = [f32(*e_start.shape), f32(*h_start.shape)]
    e, h = e_start, h_start
    coefs = ghosts = below = fresh = None
    mine = None
    for k, d in enumerate(ROUNDS):
        first = k == 0
        nxt = ROUNDS[k + 1] if k + 1 < len(ROUNDS) else 0
        far = lax.ppermute(far, "slab", far_pairs)
        near = near_swap(near)
        if not first:
            before = mine + near_swap(other)
        samples = [vmem(monitors, d, rows, width)] * 2
        edge = vmem(2, 3, 2 * d + 1, height, width)
        with jax.named_scope(f"inner{k}"):
            kernel = functools.partial(inner_kernel, d, first, depth, monitors, rows)
            if first:
                e, h, mine, other, edge, coefs = pl.pallas_call(
                    kernel,
                    out_shape=state + samples + [edge, vmem(2, depth, height, width)],
                    in_specs=[SMEM, SMEM, HBM, HBM, HBM],
                    out_specs=[HBM] * 2 + [VMEM] * 4,
                    scratch_shapes=scratch(1)
                    + [
                        pltpu.VMEM((depth, height, width), jnp.int32),
                        pltpu.SemaphoreType.DMA((12,)),
                    ],
                    compiler_params=params(),
                    cost_estimate=cost(5),
                )(info, tables, *in_hbm(e, h, material))
            else:
                e, h, mine, other, edge = pl.pallas_call(
                    kernel,
                    out_shape=state + samples + [edge],
                    in_specs=[SMEM, HBM, HBM, ANY],
                    out_specs=[HBM] * 2 + [VMEM] * 3,
                    input_output_aliases={1: 0, 2: 1},
                    scratch_shapes=scratch(1) + [pltpu.SemaphoreType.DMA((12,))],
                    compiler_params=params(),
                    cost_estimate=cost(5),
                )(info, *in_hbm(e, h), *in_vmem(coefs))
        operands = [info, *in_vmem(edge, coefs, mine, other, far, near)]
        specs = [SMEM] + [VMEM] * 6
        if first:
            operands += [tables]
            specs += [SMEM]
        else:
            operands += in_vmem(ghosts, below, before)
            specs += [VMEM, VMEM, ANY]
        outs = [vmem(2, 3, 2 * d, height, width)] + samples
        kinds = [VMEM] * 3
        aliases = {}
        if not first:
            aliases = {len(operands) - 1: 3}
            outs += [vmem(*before.shape)]
            kinds += [ANY]
        if nxt:
            outs = state + samples
            kinds = [HBM] * 2 + [VMEM] * 2
            aliases = {len(operands): 0, len(operands) + 1: 1}
            operands += [e, h]
            specs += [HBM] * 2
            size = message_size(nxt, 0, depth, False) * height
            outs += [vmem(3, height, width), vmem(size, width), vmem(size, width)]
            kinds += [VMEM]
            if first:
                outs += [vmem(2, 2 * mats, height, width)]
        with jax.named_scope(f"edge{k}"):
            results = pl.pallas_call(
                functools.partial(edge_kernel, d, nxt, first, depth, monitors, rows),
                out_shape=outs,
                in_specs=specs,
                out_specs=kinds + [VMEM] * (len(outs) - len(kinds)),
                input_output_aliases=aliases,
                scratch_shapes=scratch(GHOST) + [pltpu.SemaphoreType.DMA((8,))],
                compiler_params=params(),
                cost_estimate=cost(4),
            )(*operands)
        if nxt:
            e, h, mine, other, below, far, near = results[:7]
            if first:
                ghosts = results[7]
        else:
            fresh, mine, other, before = results
            early = Sharing(slabs, ROWS_WHEN[k - 1])
            part = early.scatter(before)
    late = Sharing(slabs, ROWS_WHEN[-1])
    total = mine + near_swap(other)
    sums = []
    for sharing, block in ((early, part), (late, late.scatter(total))):
        sums.append(sharing.gather(block, total.shape))
    spectrum = []
    for side, chunks in enumerate((sums, [near_swap(block) for block in sums])):
        operands = [info, phase_table, *in_vmem(*chunks)]
        if side == 0:
            operands += in_vmem(fresh) + in_hbm(e, h)
        else:
            operands += in_hbm(*spectrum)
        last = len(operands)
        with jax.named_scope(f"spectrum{side}"):
            results = pl.pallas_call(
                functools.partial(spectrum_kernel, side, ROUNDS, monitors, freqs),
                out_shape=[f32(freqs, 2, monitors, 2, height, width)] + state * (1 - side),
                in_specs=[SMEM, SMEM]
                + [VMEM] * (len(chunks) + 1 - side)
                + [HBM] * (2 - side),
                out_specs=[HBM] * (3 - 2 * side),
                input_output_aliases={last - 1: 0} if side else {last - 2: 1, last - 1: 2},
                scratch_shapes=[
                    pltpu.VMEM((freqs, 2, monitors, height, width), jnp.float32),
                    pltpu.SemaphoreType.DMA((4 + freqs,)),
                ],
                compiler_params=params(),
                cost_estimate=cost(2),
            )(*operands)
        spectrum = results[:1]
        if side == 0:
            e, h = results[1:]
    (spectrum,) = spectrum
    return e, h, spectrum


def solution(mesh):
    slabs = mesh.shape["slab"]
    in_specs = (
        P(None, ("design", "slab"), None, None),
        P(None, ("design", "slab"), None, None),
        P(("design", "slab"), None, None),
        P(),
        P(),
        P(),
        P(),
        P("slab"),
    )
    out_specs = (
        P(None, ("design", "slab"), None, None),
        P(None, ("design", "slab"), None, None),
        P(("design", "slab"), None, None, None, None, None),
    )
    return jax.shard_map(
        functools.partial(per_device, slabs),
        mesh=mesh,
        in_specs=in_specs,
        out_specs=out_specs,
        check_vma=False,
    )
```

```python
import functools
import math

import jax
import jax.numpy as jnp
from jax import lax
from jax.experimental import pallas as pl
from jax.experimental.pallas import tpu as pltpu
from jax.sharding import PartitionSpec as P

STEPS = 8
PERIOD = 512
ROUNDS = (4, 4)
ROWS_WHEN = ("", "before")
GHOST = max(ROUNDS)
COURANT = 0.5
VMEM = pl.BlockSpec(memory_space=pltpu.VMEM)
SMEM = pl.BlockSpec(memory_space=pltpu.SMEM)
ANY = pl.BlockSpec(memory_space=pl.ANY)
HBM = pl.BlockSpec(memory_space=pltpu.HBM)
LIMIT = 12 * 1024 * 1024
PAD = 8


def params(limit=LIMIT):
    return pltpu.CompilerParams(vmem_limit_bytes=limit)


def cost(microseconds):
    return pl.CostEstimate(
        flops=0, bytes_accessed=int(microseconds * 3.0e6), transcendentals=0
    )


def down_pieces(d, mats):
    pieces = [("e", 0, 2, 0, d)]
    if d > 1:
        pieces += [("e", 2, 1, 0, d - 1), ("h", 0, 3, 0, d - 1)]
    if mats:
        pieces += [("m", 0, 1, 0, mats)]
    return pieces


def up_pieces(d, mats, depth, first):
    pieces = [("e", 0, 3, depth - d, d)]
    if first:
        pieces += [("h", 0, 2, depth - d, d)]
        if d > 1:
            pieces += [("h", 2, 1, depth - d + 1, d - 1)]
    else:
        if d > 1:
            pieces += [("h", 0, 2, depth - d, d - 1)]
        if d > 2:
            pieces += [("h", 2, 1, depth - d + 1, d - 2)]
    if mats:
        pieces += [("m", 0, 1, depth - mats, mats)]
    return pieces


def size_of(pieces):
    return sum(p[2] * p[4] for p in pieces)


def message_size(d, mats, depth, first):
    return max(size_of(down_pieces(d, mats)), size_of(up_pieces(d, mats, depth, first)))


def spots(pieces):
    at = 0
    for name, comp, comps, plane, planes in pieces:
        for c in range(comp, comp + comps):
            yield name, c, plane, planes, at
            at += planes


def start_all(pairs, sem):
    copies = [pltpu.make_async_copy(a, b, sem.at[k]) for k, (a, b) in enumerate(pairs)]
    for copy in copies:
        copy.start()
    return copies


def first_pack_kernel(d, mats, depth, e_ref, h_ref, m_ref, far_ref, near_ref, m_in, sem):
    even = lax.rem(lax.axis_index("slab"), 2) == 0

    def pack(down_ref, up_ref):
        sides = (
            (down_pieces(d, mats), down_ref),
            (up_pieces(d, mats, depth, True), up_ref),
        )
        moves, mats_at = [], []
        for k, (pieces, out) in enumerate(sides):
            for name, c, plane, planes, at in spots(pieces):
                if name == "m":
                    moves.append((m_ref.at[pl.ds(plane, planes)], m_in.at[k]))
                    mats_at.append((k, out, at))
                else:
                    source = e_ref if name == "e" else h_ref
                    moves.append((source.at[c, pl.ds(plane, planes)], out.at[pl.ds(at, planes)]))
        for copy in start_all(moves, sem):
            copy.wait()
        for k, out, at in mats_at:
            out[pl.ds(at, mats)] = m_in[k].astype(jnp.float32)

    @pl.when(even)
    def _():
        pack(far_ref, near_ref)

    @pl.when(jnp.logical_not(even))
    def _():
        pack(near_ref, far_ref)


class Yee:
    def __init__(self, e, h, coefs, height, width, first_plane, below):
        self.e, self.h, self.coefs = e, h, coefs
        self.first_plane, self.width = first_plane, width
        self.own = pl.ds(PAD, height)
        self.next_row, self.last_row = pl.ds(PAD + 1, height), pl.ds(PAD - 1, height)
        lane = lax.broadcasted_iota(jnp.int32, (height, width), 1)
        self.lane_last, self.lane_first = lane == width - 1, lane == 0
        self.ghost_factor = None if below is None else COURANT * below.astype(jnp.float32)
        planes = e.shape[1]
        e[:, :, pl.ds(PAD + height, PAD)] = jnp.zeros((3, planes, PAD, width), jnp.float32)
        h[:, :, pl.ds(0, PAD)] = jnp.zeros((3, planes, PAD, width), jnp.float32)

    def fore_x(self, v):
        return jnp.where(self.lane_last, 0.0, pltpu.roll(v, self.width - 1, 1)) - v

    def back_x(self, v):
        return v - jnp.where(self.lane_first, 0.0, pltpu.roll(v, 1, 1))

    def step_h(self, z, ghost=False):
        e, h, own, up = self.e, self.h, self.own, self.next_row
        at = self.first_plane + z
        factor = self.ghost_factor if ghost else COURANT
        ex, ey, ez = e[0, at, own], e[1, at, own], e[2, at, own]
        h[0, at, own] = h[0, at, own] - factor * ((e[2, at, up] - ez) - (e[1, at + 1, own] - ey))
        h[1, at, own] = h[1, at, own] - factor * ((e[0, at + 1, own] - ex) - self.fore_x(ez))
        h[2, at, own] = h[2, at, own] - factor * (self.fore_x(ey) - (e[0, at, up] - ex))

    def step_e(self, z):
        e, h, own, down = self.e, self.h, self.own, self.last_row
        at = self.first_plane + z
        hx, hy, hz = h[0, at, own], h[1, at, own], h[2, at, own]
        keep, drive = self.coefs[0, at], self.coefs[1, at]
        e[0, at, own] = keep * e[0, at, own] + drive * (
            (hz - h[2, at, down]) - (hy - h[1, at - 1, own])
        )
        e[1, at, own] = keep * e[1, at, own] + drive * (
            (hx - h[0, at - 1, own]) - self.back_x(hz)
        )
        e[2, at, own] = keep * e[2, at, own] + drive * (self.back_x(hy) - (hx - h[0, at, down]))


def material_tables(tables, width):
    loss = [jnp.full((1, width), tables[1, k], jnp.float32) for k in range(tables.shape[1])]
    permit = [jnp.full((1, width), tables[0, k], jnp.float32) for k in range(tables.shape[1])]
    keeps = [(1.0 - x) / (1.0 + x) for x in loss]
    drives = [COURANT / (p * (1.0 + x)) for p, x in zip(permit, loss)]
    return keeps, drives


def look_up(values, which):
    total = jnp.broadcast_to(values[0], which.shape)
    for k in range(1, len(values)):
        total = jnp.where(which == k, values[k], total)
    return total


def monitor_info(info, m, monitors):
    return info[4 + m], info[4 + monitors + m], info[4 + 2 * monitors + m]


def take_sample(e, c, spot, start, extent, rows):
    height, width = e.shape[2] - 2 * PAD, e.shape[3]
    plane = pltpu.roll(e[c, spot, pl.ds(PAD, height)], height - start, 0)[:rows]
    return jnp.where(lax.broadcasted_iota(jnp.int32, (rows, width), 0) < extent, plane, 0.0)


def inner_kernel(d, first, depth, monitors, rows, info, *refs):
    if first:
        tables, e_in, h_in, m_in, *refs = refs
    else:
        e_in, h_in, coefs_in, *refs = refs
    e_out, h_out, mine_out, other_out, edge_out, *refs = refs
    if first:
        coefs_out, e, h, coefs, m_buf, sem = refs
    else:
        e, h, coefs, sem = refs
    height, width = e_in.shape[2:]
    g = 1
    own, inside = pl.ds(g, depth), pl.ds(PAD, height)
    fields = ((e_in, e), (h_in, h))
    moves = [(x_in.at[c], x.at[c, own, inside]) for x_in, x in fields for c in range(3)]
    if first:
        moves.append((m_in, m_buf))
    else:
        moves += [(coefs_in.at[k], coefs.at[k, own]) for k in range(2)]
    copies = start_all(moves, sem)
    yee = Yee(e, h, coefs, height, width, g, None)
    if first:
        copies.pop().wait()
        keeps, drives = material_tables(tables, width)

        def fill(z, _):
            which = m_buf[z]
            coefs[0, g + z] = look_up(keeps, which)
            coefs[1, g + z] = look_up(drives, which)
            return 0

        lax.fori_loop(0, depth, fill, 0)
    for copy in copies:
        copy.wait()

    mine, other = info[0], 1 - info[0]
    group = 4
    for s in range(1, d + 1):
        low, high = s, depth - s
        yee.step_h(low - 1)

        def chunk(base, planes):
            for u in range(planes):
                yee.step_h(base + u)
            for u in range(planes):
                yee.step_e(base + u)

        whole = (high - low) // group

        def body(k, _):
            chunk(low + group * k, group)
            return 0

        lax.fori_loop(0, whole, body, 0)
        if low + group * whole < high:
            chunk(low + group * whole, high - low - group * whole)
        for m in range(monitors):
            offset, start, extent = monitor_info(info, m, monitors)
            held = jnp.logical_and(offset >= low, offset < high)
            taken = jnp.where(held, extent, 0)
            spot = g + jnp.clip(offset, 0, depth - 1)
            mine_out[m, s - 1] = take_sample(e, mine, spot, start, taken, rows)
            other_out[m, s - 1] = take_sample(e, other, spot, start, taken, rows)

    moves = []
    for k, (x, x_out) in enumerate(((e, e_out), (h, h_out))):
        moves += [(x.at[c, own, inside], x_out.at[c]) for c in range(3)]
    copies = start_all(moves, sem)
    for k, x in enumerate((e, h)):
        for c in range(3):
            edge_out[k, c, pl.ds(0, d)] = x[c, pl.ds(g, d), inside]
            edge_out[k, c, pl.ds(d, d + 1)] = x[c, pl.ds(g + depth - 1 - d, d + 1), inside]
    if first:
        for k in range(2):
            coefs_out[k] = coefs[k, own]
    for copy in copies:
        copy.wait()


def edge_kernel(d, nxt, first, depth, monitors, rows, info, *refs):
    edge_in, coefs_in, mine_in, other_in, far_in, near_in, *refs = refs
    mats = GHOST - 1
    if first:
        tables, *refs = refs
    else:
        ghosts_in, below_in, _, *refs = refs
    if nxt:
        _, _, e_out, h_out, mine_out, other_out, below_out, far_out, near_out, *refs = refs
        if first:
            ghosts_out, *refs = refs
    else:
        fresh_out, mine_out, other_out, _, *refs = refs
    e, h, coefs, sem = refs
    height, width = edge_in.shape[3:]
    g = GHOST
    inside = pl.ds(PAD, height)
    even = info[0] == 0
    below, above = info[1], info[2]

    yee = Yee(e, h, coefs, height, width, g, below)
    for k, x in enumerate((e, h)):
        for source, planes, at in ((0, d, 0), (d, d + 1, depth - 1 - d)):
            for c in range(3):
                part = edge_in[k, c, pl.ds(source, planes)]
                x[c, pl.ds(g + at, planes), inside] = part
    for plane in (0, depth - d):
        for k in range(2):
            coefs[k, pl.ds(g + plane, d)] = coefs_in[k, pl.ds(plane, d)]
    if not first:
        h[:, g - 1, inside] = below_in[...]

    sides = (
        (-depth, up_pieces(d, mats if first else 0, depth, first)),
        (depth, down_pieces(d, mats if first else 0)),
    )

    def unpack(below_ref, above_ref):
        for (shift, pieces), source in zip(sides, (below_ref, above_ref)):
            for name, c, plane, planes, at in spots(pieces):
                where = pl.ds(g + plane + shift, planes)
                value = source[pl.ds(at * height, planes * height)]
                value = value.reshape(planes, height, width)
                if name == "e":
                    e[c, where, inside] = value
                elif name == "h":
                    h[c, where, inside] = value
                else:
                    coefs[0, where] = value

    @pl.when(even)
    def _():
        unpack(far_in, near_in)

    @pl.when(jnp.logical_not(even))
    def _():
        unpack(near_in, far_in)

    ghost_planes = list(range(g - mats, g)) + list(range(g + depth, g + depth + mats))
    if first:
        keeps, drives = material_tables(tables, width)
        for at in ghost_planes:
            alive = (below if at < g else above).astype(jnp.float32)
            which = coefs[0, at].astype(jnp.int32)
            coefs[0, at] = look_up(keeps, which) * alive
            coefs[1, at] = look_up(drives, which) * alive
        if nxt:
            for k, at in enumerate(ghost_planes):
                ghosts_out[:, k] = coefs[:, at]
    else:
        for k, at in enumerate(ghost_planes):
            coefs[:, at] = ghosts_in[:, k]

    mine, other = info[0], 1 - info[0]
    for s in range(1, d + 1):
        lower = list(range(s - d, s))
        upper = list(range(depth - s, depth + d - s))
        for z in lower:
            yee.step_h(z - 1, z - 1 < 0)
        for z in upper:
            yee.step_h(z)
        for z in lower + upper:
            yee.step_e(z)
        for m in range(monitors):
            offset, start, extent = monitor_info(info, m, monitors)
            held = jnp.logical_or(
                jnp.logical_and(offset >= 0, offset < s),
                jnp.logical_and(offset >= depth - s, offset < depth),
            )
            spot = g + jnp.clip(offset, 0, depth - 1)
            mine_out[m, s - 1] = jnp.where(
                held, take_sample(e, mine, spot, start, extent, rows), mine_in[m, s - 1]
            )
            fresh = jnp.where(
                held, take_sample(e, other, spot, start, extent, rows), other_in[m, s - 1]
            )
            other_out[m, s - 1] = fresh

    copies = []
    if nxt:
        moves = []
        for x, x_out in ((e, e_out), (h, h_out)):
            for plane in (0, depth - d):
                source = x.at[:, pl.ds(g + plane, d), inside]
                moves.append((source, x_out.at[:, pl.ds(plane, d)]))
        copies = start_all(moves, sem)
    else:
        for k, x in enumerate((e, h)):
            for j, plane in enumerate((0, depth - d)):
                for c in range(3):
                    part = x[c, pl.ds(g + plane, d), inside]
                    fresh_out[k, c, pl.ds(j * d, d)] = part
    if nxt:
        below_out[...] = h[:, g - 1, inside]

        def pack(down_ref, up_ref):
            for pieces, out in (
                (down_pieces(nxt, 0), down_ref),
                (up_pieces(nxt, 0, depth, False), up_ref),
            ):
                for name, c, plane, planes, at in spots(pieces):
                    source = e if name == "e" else h
                    value = source[c, pl.ds(g + plane, planes), inside]
                    out[pl.ds(at * height, planes * height)] = value.reshape(-1, width)

        @pl.when(even)
        def _():
            pack(far_out, near_out)

        @pl.when(jnp.logical_not(even))
        def _():
            pack(near_out, far_out)

    for copy in copies:
        copy.wait()


def spectrum_kernel(side, chunks, monitors, freqs, info, table, *refs):
    samples, (blocks, sem) = refs[: len(chunks)], refs[-2:]
    if side == 0:
        fresh, _, _, out, *state = refs[len(chunks) : -2]
        edge = fresh.shape[2] // 2
        moves = []
        for k, x_out in enumerate(state):
            for j, plane in enumerate((0, x_out.shape[1] - edge)):
                moves.append(
                    (fresh.at[k, :, pl.ds(j * edge, edge)], x_out.at[:, pl.ds(plane, edge)])
                )
        copies = start_all(moves, sem)
    else:
        out = refs[-3]
        copies = []
    rows, width = samples[0].shape[2:]
    steps = sum(chunks)
    c = info[0] if side == 0 else 1 - info[0]

    def copy(f):
        return pltpu.make_async_copy(blocks.at[f], out.at[f, :, :, c], sem.at[4 + f])

    def body(f, _):
        for m in range(monitors):
            start = monitor_info(info, m, monitors)[1]
            at = jnp.bitwise_xor(m, info[3])
            planes = [chunk[at, t] for chunk, d in zip(samples, chunks) for t in range(d)]
            for part in range(2):
                total = planes[0] * table[f, part * steps]
                for t in range(1, steps):
                    total = total + planes[t] * table[f, part * steps + t]
                blocks[f, part, m, pl.ds(0, (blocks.shape[3] - rows))] = jnp.zeros(((blocks.shape[3] - rows), width), jnp.float32)
                blocks[f, part, m, pl.ds(rows, (blocks.shape[3] - rows))] = jnp.zeros(((blocks.shape[3] - rows), width), jnp.float32)
                blocks[f, part, m, pl.ds(start, rows)] = total
        copy(f).start()
        return 0

    lax.fori_loop(0, freqs, body, 0)
    for f in range(freqs):
        copy(f).wait()
    for move in copies:
        move.wait()


class Sharing:
    def __init__(self, slabs, rows_when):
        self.slabs, self.rows_when = slabs, rows_when
        me = lax.axis_index("slab")
        self.quarter = 2 * (me // 4 % 2) + me // 8 % 2
        self.half = me // 2 % 2
        self.others = [2**k for k in range(1, slabs.bit_length() - 1)]
        self.others = [k for k in self.others if k not in ((4, 8) if not rows_when else (2, 4, 8))]

    def swap(self, block, stride):
        return lax.ppermute(block, "slab", [(i, i ^ stride) for i in range(self.slabs)])

    def halve(self, total, axis):
        sent = lax.dynamic_index_in_dim(total, 1 - self.half, axis, keepdims=False)
        kept = lax.dynamic_index_in_dim(total, self.half, axis, keepdims=False)
        return kept + self.swap(sent, 2)

    def scatter(self, total):
        if self.rows_when:
            total = total.reshape(total.shape[0], 2, -1, total.shape[-1])
        if self.rows_when == "before":
            total = self.halve(total, 1)
        pieces = [
            lax.dynamic_index_in_dim(total, self.quarter ^ x, 0, keepdims=False)
            for x in range(4)
        ]
        part = pieces[0]
        for x, stride in ((1, 8), (2, 4), (3, 12)):
            part = part + self.swap(pieces[x], stride)
        if self.rows_when == "after":
            part = self.halve(part, 0)
        for stride in self.others:
            part = part + self.swap(part, stride)
        return part

    def gather(self, part, shape):
        total = jnp.stack([part] + [self.swap(part, stride) for stride in (8, 4, 12)])
        if self.rows_when:
            theirs = self.swap(total, 2)
            first = self.half == 0
            total = jnp.stack(
                [jnp.where(first, total, theirs), jnp.where(first, theirs, total)], 1
            )
        return total.reshape(shape)


def per_device(
    slabs, e_start, h_start, material, mat_permit, mat_loss, monitor_z, monitor_span, freq_bins
):
    depth, height, width = e_start.shape[1:]
    monitors = monitor_z.shape[0]
    freqs = freq_bins.shape[0]
    rows = 3 * height // 4
    mats = GHOST - 1
    me = lax.axis_index("slab")
    info = jnp.concatenate(
        [
            jnp.stack(
                [
                    me % 2,
                    (me > 0).astype(jnp.int32),
                    (me < slabs - 1).astype(jnp.int32),
                    2 * (me // 4 % 2) + me // 8 % 2,
                ]
            ),
            monitor_z - me * depth,
            monitor_span[:, 0],
            monitor_span[:, 1] - monitor_span[:, 0],
        ]
    ).astype(jnp.int32)
    tables = jnp.stack([mat_permit, mat_loss])
    moments = jnp.arange(1, STEPS + 1, dtype=jnp.int32)
    phase_turns = freq_bins[:, None] * moments[None, :] % PERIOD
    angles = phase_turns.astype(jnp.float32) * jnp.float32(2.0 * math.pi / PERIOD)
    phase_table = jnp.concatenate([jnp.cos(angles), -jnp.sin(angles)], 1)

    far_pairs = []
    for i in range(1, slabs - 1, 2):
        far_pairs += [(i, i + 1), (i + 1, i)]
    near_pairs = [(i, i ^ 1) for i in range(slabs)]

    def near_swap(block):
        return lax.ppermute(block, "slab", near_pairs)

    def f32(*shape):
        return jax.ShapeDtypeStruct(shape, jnp.float32)

    def vmem(*shape):
        return pltpu.VMEM(shape, jnp.float32)

    def in_hbm(*arrays):
        return [pltpu.with_memory_space_constraint(x, pltpu.HBM) for x in arrays]

    def in_vmem(*arrays):
        return [pltpu.with_memory_space_constraint(x, pltpu.VMEM) for x in arrays]

    def scratch(ghosts):
        planes = depth + 2 * ghosts
        padded = (3, planes, height + 2 * PAD, width)
        return [pltpu.VMEM(padded, jnp.float32)] * 2 + [
            pltpu.VMEM((2, planes, height, width), jnp.float32)
        ]

    d = ROUNDS[0]
    size = message_size(d, mats, depth, True)
    copies = sum(1 for _ in spots(down_pieces(d, mats))) + sum(
        1 for _ in spots(up_pieces(d, mats, depth, True))
    )
    with jax.named_scope("first_pack"):
        far, near = pl.pallas_call(
            functools.partial(first_pack_kernel, d, mats, depth),
            out_shape=[vmem(size, height, width)] * 2,
            in_specs=[HBM] * 3,
            out_specs=[VMEM] * 2,
            scratch_shapes=[
                pltpu.VMEM((2, mats, height, width), jnp.int32),
                pltpu.SemaphoreType.DMA((copies,)),
            ],
            compiler_params=params(),
            cost_estimate=cost(2),
        )(*in_hbm(e_start, h_start, material))
    far, near = far.reshape(-1, width), near.reshape(-1, width)

    state = [f32(*e_start.shape), f32(*h_start.shape)]
    e, h = e_start, h_start
    coefs = ghosts = below = fresh = None
    mine = None
    for k, d in enumerate(ROUNDS):
        first = k == 0
        nxt = ROUNDS[k + 1] if k + 1 < len(ROUNDS) else 0
        far = lax.ppermute(far, "slab", far_pairs)
        near = near_swap(near)
        if not first:
            before = mine + near_swap(other)
        samples = [vmem(monitors, d, rows, width)] * 2
        edge = vmem(2, 3, 2 * d + 1, height, width)
        with jax.named_scope(f"inner{k}"):
            kernel = functools.partial(inner_kernel, d, first, depth, monitors, rows)
            if first:
                e, h, mine, other, edge, coefs = pl.pallas_call(
                    kernel,
                    out_shape=state + samples + [edge, vmem(2, depth, height, width)],
                    in_specs=[SMEM, SMEM, HBM, HBM, HBM],
                    out_specs=[HBM] * 2 + [VMEM] * 4,
                    scratch_shapes=scratch(1)
                    + [
                        pltpu.VMEM((depth, height, width), jnp.int32),
                        pltpu.SemaphoreType.DMA((12,)),
                    ],
                    compiler_params=params(),
                    cost_estimate=cost(5),
                )(info, tables, *in_hbm(e, h, material))
            else:
                e, h, mine, other, edge = pl.pallas_call(
                    kernel,
                    out_shape=state + samples + [edge],
                    in_specs=[SMEM, HBM, HBM, ANY],
                    out_specs=[HBM] * 2 + [VMEM] * 3,
                    input_output_aliases={1: 0, 2: 1},
                    scratch_shapes=scratch(1) + [pltpu.SemaphoreType.DMA((12,))],
                    compiler_params=params(),
                    cost_estimate=cost(5),
                )(info, *in_hbm(e, h), *in_vmem(coefs))
        operands = [info, *in_vmem(edge, coefs, mine, other)]
        operands += (in_hbm(far) if first else in_vmem(far)) + in_vmem(near)
        specs = [SMEM] + [VMEM] * 6
        if first:
            operands += [tables]
            specs += [SMEM]
        else:
            operands += in_vmem(ghosts, below, before)
            specs += [VMEM, VMEM, ANY]
        outs = [vmem(2, 3, 2 * d, height, width)] + samples
        kinds = [VMEM] * 3
        aliases = {}
        if not first:
            aliases = {len(operands) - 1: 3}
            outs += [vmem(*before.shape)]
            kinds += [ANY]
        if nxt:
            outs = state + samples
            kinds = [HBM] * 2 + [VMEM] * 2
            aliases = {len(operands): 0, len(operands) + 1: 1}
            operands += [e, h]
            specs += [HBM] * 2
            size = message_size(nxt, 0, depth, False) * height
            outs += [vmem(3, height, width), vmem(size, width), vmem(size, width)]
            kinds += [VMEM]
            if first:
                outs += [vmem(2, 2 * mats, height, width)]
        with jax.named_scope(f"edge{k}"):
            results = pl.pallas_call(
                functools.partial(edge_kernel, d, nxt, first, depth, monitors, rows),
                out_shape=outs,
                in_specs=specs,
                out_specs=kinds + [VMEM] * (len(outs) - len(kinds)),
                input_output_aliases=aliases,
                scratch_shapes=scratch(GHOST) + [pltpu.SemaphoreType.DMA((8,))],
                compiler_params=params(),
                cost_estimate=cost(4),
            )(*operands)
        if nxt:
            e, h, mine, other, below, far, near = results[:7]
            if first:
                ghosts = results[7]
        else:
            fresh, mine, other, before = results
            early = Sharing(slabs, ROWS_WHEN[k - 1])
            part = early.scatter(before)
    late = Sharing(slabs, ROWS_WHEN[-1])
    total = mine + near_swap(other)
    sums = []
    for sharing, block in ((early, part), (late, late.scatter(total))):
        sums.append(sharing.gather(block, total.shape))
    spectrum = []
    for side, chunks in enumerate((sums, [near_swap(block) for block in sums])):
        operands = [info, phase_table, *in_vmem(*chunks)]
        if side == 0:
            operands += in_vmem(fresh) + in_hbm(e, h)
        else:
            operands += in_hbm(*spectrum)
        last = len(operands)
        with jax.named_scope(f"spectrum{side}"):
            results = pl.pallas_call(
                functools.partial(spectrum_kernel, side, ROUNDS, monitors, freqs),
                out_shape=[f32(freqs, 2, monitors, 2, height, width)] + state * (1 - side),
                in_specs=[SMEM, SMEM]
                + [VMEM] * (len(chunks) + 1 - side)
                + [HBM] * (2 - side),
                out_specs=[HBM] * (3 - 2 * side),
                input_output_aliases={last - 1: 0} if side else {last - 2: 1, last - 1: 2},
                scratch_shapes=[
                    pltpu.VMEM((freqs, 2, monitors, height, width), jnp.float32),
                    pltpu.SemaphoreType.DMA((4 + freqs,)),
                ],
                compiler_params=params(),
                cost_estimate=cost(2),
            )(*operands)
        spectrum = results[:1]
        if side == 0:
            e, h = results[1:]
    (spectrum,) = spectrum
    return e, h, spectrum


def solution(mesh):
    slabs = mesh.shape["slab"]
    in_specs = (
        P(None, ("design", "slab"), None, None),
        P(None, ("design", "slab"), None, None),
        P(("design", "slab"), None, None),
        P(),
        P(),
        P(),
        P(),
        P("slab"),
    )
    out_specs = (
        P(None, ("design", "slab"), None, None),
        P(None, ("design", "slab"), None, None),
        P(("design", "slab"), None, None, None, None, None),
    )
    return jax.shard_map(
        functools.partial(per_device, slabs),
        mesh=mesh,
        in_specs=in_specs,
        out_specs=out_specs,
        check_vma=False,
    )
```
